32 devices in a mesh: dp: 4 (over x, core), expert: 8 (over z, y).
Axes of the slice: x: 2, y: 2, z: 4, core: 2. Of those that a mesh axis runs over, the one named last changes fastest.
Arguments:
- tokens: bfloat16 [32768, 768], P(('dp', 'expert')), may hold values from -6 to 6
- segment_ids: int32 [32, 1024], P(('dp', 'expert')), may hold values from 0 to 3, never falling along the last dimension, each value on 1 to 512 neighbouring positions
- routes: int32 [32768, 1], P(('dp', 'expert')), may hold values from 0 to 7; in each aligned block of 1024 rows (0 to 1023, 1024 to 2047, ...) at most 256 rows name the same one
- norm1_gain: float32 [768], replicated, may hold values from 0.5 to 1.5
- norm1_bias: float32 [768], replicated, may hold values from -1 to 1
- query_weight: bfloat16 [768, 768], replicated, may hold values from -0.21875 to 0.21875
- w_key: bfloat16 [768, 768], replicated, may hold values from -0.21875 to 0.21875
- w_value: bfloat16 [768, 768], replicated, may hold values from -0.21875 to 0.21875
- w_output: bfloat16 [768, 768], replicated, may hold values from -1.75 to 1.75
- norm2_gain: float32 [768], replicated, may hold values from 0.5 to 1.5
- norm2_bias: float32 [768], replicated, may hold values from -1 to 1
- router_proj: float32 [768, 16], replicated, may hold values from -0.0546875 to 0.0546875
- expert_embed: float32 [8, 16], replicated, may hold values from -1.5 to 1.5
- expert_in: bfloat16 [8, 768, 3072], P('expert'), may hold values from -0.21875 to 0.21875
- expert_out: bfloat16 [8, 3072, 768], P('expert'), may hold values from -1.25 to 1.25
- cotangent: bfloat16 [32768, 768], P(('dp', 'expert')), may hold values from -6 to 6
Outputs:
- output: bfloat16 [32768, 768], P(('dp', 'expert'))
- grad_input: float32 [32768, 768], P(('dp', 'expert'))
- grad_norm1_gain: float32 [768], replicated
- grad_norm1_bias: float32 [768], replicated
- grad_w_query: float32 [768, 768], replicated
- grad_w_key: float32 [768, 768], replicated
- grad_w_value: float32 [768, 768], replicated
- grad_w_output: float32 [768, 768], replicated
- grad_norm2_gain: float32 [768], replicated
- grad_norm2_bias: float32 [768], replicated
- grad_router_proj: float32 [768, 16], replicated
- grad_expert_embed: float32 [8, 16], replicated
- grad_expert_in: float32 [8, 768, 3072], P('expert', None, 'dp')
- grad_expert_out: float32 [8, 3072, 768], P('expert', 'dp')
The draws below stay inside these ranges and needn't reach their ends.
Inputs may be any that keep to these rules, and one draw needn't show every extreme that they name: `routes`: among the 1024 tokens of one device no expert is named more than 256 times, and in every draw some expert is named exactly 256 times by one device's tokens. `segment_ids`: within each sequence the ids never fall; each document has 1 to 512 tokens, and one has exactly 512.
All inputs are finite; a program needn't handle non-finite values.
Results may differ from the reference program's by a relative error of at most 0.02.
The reference program's roundings to bfloat16 on the way count: a program that leaves them out, or rounds other values in their place, can miss the bound.
Values may be sent and summed in bfloat16 or wider, within the bound.
A program may use at most 256 MiB of HBM per device.

```python
import math
import jax
import jax.numpy as jnp
import numpy as np
from jax import lax

D = 768
HEADS = 12
HEAD_DIM = 64
FF = 3072
ROUTER = 16
SEQ = 1024
DOCS = 4
EXPERTS = 8
TOK_DEV = 1024
CAP = 256
SEQS = 32
TOKENS = 32768
DEVICES = 32


def block_scale(stream_key, shape, cuts, low, high):
    level = 1.0
    for axis_at, blocks in cuts:
        steps = jax.random.uniform(jax.random.fold_in(jax.random.fold_in(stream_key, 6), axis_at), (blocks,), jnp.float32, low / len(cuts), high / len(cuts))
        level = level * jnp.repeat(jnp.exp(steps), shape[axis_at] // blocks).reshape((-1,) + (1,) * (len(shape) - 1 - axis_at))
    return level


def split_up(count, total, bound, slope):
    weights = [(1 << 20) // math.isqrt(grade ** slope) + 1 for grade in range(2, count + 1)]
    rest, counts = total - bound - (count - 1), [1] * (count - 1)
    while rest > 0:
        candidates = [i for i in range(count - 1) if counts[i] < bound]
        mass, remaining = sum([weights[i] for i in candidates]), rest
        for i in candidates:
            addition = min(bound - counts[i], max(1, remaining * weights[i] // mass), rest)
            counts[i] = counts[i] + addition
            rest = rest - addition
    return np.array([bound] + counts)


def uneven_parts(rng, count, total, most, skew):
    if count == 2:
        one = jax.random.randint(rng, (), max(1, total - most), min(most, total - 1) + 1)
        return jnp.stack([one, total - one])
    tallies = jnp.asarray(split_up(count, total, most, skew), jnp.int32)
    couples = (count - 1) // 2
    donor, sink = tallies[1:1 + 2 * couples:2], tallies[2:2 + 2 * couples:2]
    margin = jnp.minimum(donor - 1, most - sink)
    moved = jax.random.randint(jax.random.fold_in(rng, 1), (couples,), 0, 1 << 20) % (margin + 1)
    tallies = tallies.at[1:1 + 2 * couples:2].set(donor - moved).at[2:2 + 2 * couples:2].set(sink + moved)
    return tallies[jax.random.permutation(jax.random.fold_in(rng, 2), count)]


def shared_out(own_key, own, number, rows, count, top, limit, slope):
    sequence = jax.random.permutation(own_key, count)
    packed, usual = load_shares(count, rows * top, limit, slope, True), load_shares(count, rows * top, limit, slope, False)
    places = jnp.arange(count)

    def named(sizes, turn):
        used = int((sizes > 0).sum())
        fixed = max(1, used // 4)
        shifted = fixed + (places - fixed + turn * (used - fixed)) % max(1, count - fixed)
        return jnp.zeros((count,), jnp.int32).at[sequence[jnp.where(places < fixed, places, shifted)]].set(jnp.asarray(sizes, jnp.int32))

    sizes = jnp.where(number % 4 == 0, named(packed, number // 4), named(usual, number - number // 4 - 1))
    mixed = jax.random.permutation(jax.random.fold_in(own, 3), count)
    source_of, receiver = mixed[0:count // 2 * 2:2], mixed[1:count // 2 * 2:2]
    slack = jnp.minimum(sizes[source_of] - 1, limit - sizes[receiver]) // 2
    slack = jnp.where((source_of == sequence[0]) | (receiver == sequence[0]) | (sizes[receiver] == 0), 0, jnp.maximum(slack, 0))
    shifted = jax.random.randint(jax.random.fold_in(own, 4), (count // 2,), 0, 1 << 20) % (slack + 1)
    sizes = sizes.at[source_of].add(-shifted).at[receiver].add(shifted)
    members = jnp.searchsorted(jnp.cumsum(sizes), jnp.arange(rows * top), side="right").astype(jnp.int32)
    grid = members.reshape(top, rows).T
    grid = grid[jax.random.permutation(jax.random.fold_in(own, 1), rows)]
    turn = jax.random.randint(jax.random.fold_in(own, 2), (rows, 1), 0, top)
    return jnp.take_along_axis(grid, (jnp.arange(top)[None, :] + turn) % top, axis=1)


def load_shares(count, total, limit, skew, full):
    portions = [(1 << 20) // math.isqrt(grade ** skew) + 1 for grade in range(1, count + 1)]
    largest = limit if full else min(limit, max(-(-total // count), total * portions[0] // sum(portions)))
    least = 1 if total - largest >= count - 1 else 0
    counts, spare = [largest] + [least] * (count - 1), total - largest - least * (count - 1)
    while spare > 0:
        candidates = [i for i in range(1, count) if counts[i] < largest] or [i for i in range(1, count) if counts[i] < limit]
        whole, budget = sum([portions[i] for i in candidates]), spare
        for i in candidates:
            extra = min(limit - counts[i], max(1, budget * portions[i] // whole), spare)
            counts[i] = counts[i] + extra
            spare = spare - extra
    return np.array(counts)


def gaussian(stream_key, dims, scale, most, split=(), held_as=jnp.bfloat16):
    loudness = block_scale(stream_key, dims, split, -0.22, 0.18) if split else 1.0
    array = jax.random.normal(stream_key, dims, jnp.float32) * scale * loudness
    return jnp.minimum(jnp.maximum(array, -most), most).astype(held_as)


def setup_inputs(seed: int = 0) -> dict:
    splits = jax.random.split(jax.random.key(seed), 17)
    tokens = gaussian(splits[0], (TOKENS, D), 1.0, 6.0, ((0, 32),))
    segment_ids = jax.vmap(lambda own: jnp.searchsorted(jnp.cumsum(uneven_parts(own, DOCS, SEQ, SEQ // 2, 1)), jnp.arange(SEQ), side="right"))(jax.random.split(splits[1], SEQS)).reshape((SEQS, SEQ)).astype(jnp.int32)
    routes_keys = jax.random.split(jax.random.fold_in(splits[2], 1), TOKENS // TOK_DEV)
    routes_turns = jax.random.permutation(jax.random.fold_in(splits[2], 3), TOKENS // TOK_DEV)
    routes = jax.vmap(lambda own, number: shared_out(jax.random.fold_in(splits[2], 2), own, number, TOK_DEV, EXPERTS, 1, CAP, 2))(routes_keys, routes_turns).reshape((TOKENS, 1))
    norm1_gain = jnp.clip(1.0 + 0.1 * jax.random.normal(splits[3], (D,), jnp.float32), 0.5, 1.5)
    norm1_bias = gaussian(splits[4], (D,), 0.2, 1.0, (), jnp.float32)
    query_weight = gaussian(splits[5], (D, D), D ** -0.5, 0.21875)
    w_key = gaussian(splits[6], (D, D), D ** -0.5, 0.21875)
    w_value = gaussian(splits[7], (D, D), D ** -0.5, 0.21875)
    w_output = gaussian(splits[8], (D, D), (max(1, D // 64)) ** -0.5, 1.75)
    norm2_gain = jnp.clip(1.0 + 0.1 * jax.random.normal(splits[9], (D,), jnp.float32), 0.5, 1.5)
    norm2_bias = gaussian(splits[10], (D,), 0.2, 1.0, (), jnp.float32)
    router_proj = gaussian(splits[11], (D, ROUTER), (ROUTER * D) ** -0.5, 0.0546875, (), jnp.float32)
    expert_embed = gaussian(splits[12], (EXPERTS, ROUTER), 0.25, 1.5, (), jnp.float32)
    expert_in = gaussian(splits[13], (EXPERTS, D, FF), D ** -0.5, 0.21875, ((0, 8),))
    expert_out = gaussian(splits[14], (EXPERTS, FF, D), (max(1, FF // (2 * EXPERTS * EXPERTS))) ** -0.5, 1.25, ((0, 8),))
    cotangent = gaussian(splits[15], (TOKENS, D), 1.0, 6.0, ((0, 32),))
    return dict(tokens=tokens, segment_ids=segment_ids, routes=routes, norm1_gain=norm1_gain, norm1_bias=norm1_bias, query_weight=query_weight, w_key=w_key, w_value=w_value, w_output=w_output, norm2_gain=norm2_gain, norm2_bias=norm2_bias, router_proj=router_proj, expert_embed=expert_embed, expert_in=expert_in, expert_out=expert_out, cotangent=cotangent)


normalizer_sharpness = 0.25
exact_arithmetic_mode = lax.Precision.HIGHEST

@jax.custom_vjp
def low(v):
    return lax.optimization_barrier(v.astype(jnp.bfloat16)).astype(jnp.float32)

@jax.custom_vjp
def low_back(v):
    return v

def low_keep(v):
    return (low(v), None)

def low_pass(kept, grad):
    return (grad,)

def back_keep(v):
    return (v, None)

def reverse_narrow_cast(kept, grad):
    return (low(grad),)
low.defvjp(low_keep, low_pass)
low_back.defvjp(back_keep, reverse_narrow_cast)

def layer_norm(values, gain, shift):
    average = lax.optimization_barrier(jnp.mean(values, -1, keepdims=True))
    centred = values - average
    spread = lax.optimization_barrier(jnp.mean(centred * centred, -1, keepdims=True))
    return centred * lax.rsqrt(spread + 1e-05) * gain + shift

def router_gate(normed, router_proj, expert_embed, chosen):
    narrowed_feature_count = jnp.dot(normed, router_proj, precision=exact_arithmetic_mode)
    narrowed_feature_count = narrowed_feature_count * lax.rsqrt(jnp.maximum(lax.optimization_barrier(jnp.sum(narrowed_feature_count * narrowed_feature_count, -1, keepdims=True)), 1.0))
    index_mapping_array = expert_embed * lax.rsqrt(jnp.maximum(lax.optimization_barrier(jnp.sum(expert_embed * expert_embed, -1, keepdims=True)), 1.0))
    gating_raw_scores = jnp.dot(narrowed_feature_count, index_mapping_array.T, precision=exact_arithmetic_mode) / normalizer_sharpness
    router_probs = jax.nn.softmax(gating_raw_scores, axis=-1)
    return lax.optimization_barrier(jnp.sum(router_probs * chosen, -1))

def attend(queries, keys_seq, values_seq, seg_ids):
    scores = jnp.einsum('qhd,khd->hqk', queries, keys_seq, precision=exact_arithmetic_mode) * queries.shape[-1] ** (-0.5)
    scores = low_back(scores)
    same_doc = seg_ids[:, None] == seg_ids[None, :]
    scores = jnp.where(same_doc[None], scores, -1e+30)
    probs = low(jax.nn.softmax(scores, axis=-1))
    return jnp.einsum('hqk,khd->qhd', probs, values_seq, precision=exact_arithmetic_mode)

def reference(tokens, segment_ids, routes, norm1_gain, norm1_bias, query_weight, w_key, w_value, w_output, norm2_gain, norm2_bias, router_proj, expert_embed, expert_in, expert_out, cotangent):
    seqs_all = segment_ids.shape[0]
    seq_len = segment_ids.shape[1]
    token_total = tokens.shape[0]
    route = routes[:, 0]
    expert_ids = jnp.arange(EXPERTS, dtype=jnp.int32)
    hits = (route.reshape(DEVICES, TOK_DEV)[:, :, None] == expert_ids[None, None, :]).astype(jnp.int32)
    slot_rank = lax.optimization_barrier(jnp.sum((jnp.cumsum(hits, 1) - hits) * hits, 2)).reshape(-1).astype(jnp.int32)
    device_of = (jnp.arange(token_total, dtype=jnp.int32) // TOK_DEV).astype(jnp.int32)
    slot_of = (device_of * CAP + slot_rank).astype(jnp.int32)
    slot_token = jnp.full((EXPERTS, DEVICES * CAP), -1, jnp.int32).at[route, slot_of].set(jnp.arange(token_total, dtype=jnp.int32))
    chosen = (route[:, None] == expert_ids[None, :]).astype(jnp.float32)
    group = math.gcd(seqs_all, max(1, 4096 // seq_len))
    seg_groups = segment_ids.reshape(seqs_all // group, group, seq_len)

    def forward(xf, gain1, shift1, wq, wk, wv, wo, gain2, shift2, rproj, embed, w_in, w_out):
        normed1 = low(layer_norm(xf, gain1, shift1))

        def project(weight):
            made = low_back(low(jnp.dot(normed1, weight, precision=exact_arithmetic_mode)))
            return made.reshape(seqs_all // group, group, seq_len, HEADS, HEAD_DIM)
        query_groups, key_groups, value_groups = (project(wq), project(wk), project(wv))

        def attend_step(running, stacked):
            return (running, jax.vmap(attend)(*stacked))
        _, mixed = lax.scan(jax.checkpoint(attend_step), jnp.zeros((), jnp.float32), (query_groups, key_groups, value_groups, seg_groups))
        mixed = low_back(low(mixed.reshape(token_total, HEADS * HEAD_DIM)))
        hidden = xf + low_back(jnp.dot(mixed, wo, precision=exact_arithmetic_mode))
        normed2 = layer_norm(hidden, gain2, shift2)
        gate = router_gate(normed2, rproj, embed, chosen)
        normed_low = low_back(low(normed2))

        def expert_step(running, stacked):
            weight_in, weight_out, token_ids = stacked
            filled = token_ids >= 0
            expert_rows = jnp.where(filled[:, None], normed_low[jnp.maximum(token_ids, 0)], 0.0)
            pre = low_back(jnp.dot(expert_rows, weight_in, precision=exact_arithmetic_mode))
            active_mask = low(jax.nn.gelu(pre, approximate=False))
            produced = low_back(low(jnp.dot(active_mask, weight_out, precision=exact_arithmetic_mode)))
            return (running, produced)
        _, produced_all = lax.scan(jax.checkpoint(expert_step), jnp.zeros((), jnp.float32), (w_in, w_out, slot_token))
        produced = produced_all[route, slot_of]
        return hidden + gate[:, None] * produced
    primals = (tokens.astype(jnp.float32), norm1_gain, norm1_bias, query_weight.astype(jnp.float32), w_key.astype(jnp.float32), w_value.astype(jnp.float32), w_output.astype(jnp.float32), norm2_gain, norm2_bias, router_proj, expert_embed, expert_in.astype(jnp.float32), expert_out.astype(jnp.float32))
    result, pullback = jax.vjp(forward, *primals)
    grads = pullback(cotangent.astype(jnp.float32))
    return (result.astype(jnp.bfloat16), grads[0], grads[1], grads[2], grads[3], grads[4], grads[5], grads[6], grads[7], grads[8], grads[9], grads[10], grads[11], grads[12])
```

```python
import functools

import jax
import jax.numpy as jnp
from jax import lax
from jax.experimental import pallas as pl
from jax.experimental.pallas import tpu as pltpu
from jax.sharding import PartitionSpec as P

HEAD_DIM = 64
PAIR = 2 * HEAD_DIM
SHARPNESS = 0.25
EXACT = lax.Precision.HIGHEST
BF16 = jnp.bfloat16
F32 = jnp.float32
FAR = -1e30
MIB = 1 << 20


def mm(left, right):
    return jnp.dot(left, right, preferred_element_type=F32)


def mm_rows(left, right, precision=None):
    return lax.dot_general(
        left, right, (((0,), (0,)), ((), ())), precision=precision, preferred_element_type=F32
    )


def mm_cols(left, right, precision=None):
    return lax.dot_general(
        left, right, (((1,), (1,)), ((), ())), precision=precision, preferred_element_type=F32
    )


def iota(shape, axis):
    return lax.broadcasted_iota(jnp.int32, shape, axis)


def one_hot(condition):
    return jnp.where(condition, 1.0, 0.0).astype(BF16)


def params(limit=56):
    return pltpu.CompilerParams(vmem_limit_bytes=limit * MIB)


def cost(flops, moved, trans=0):
    return pl.CostEstimate(flops=int(flops), bytes_accessed=int(moved), transcendentals=int(trans))


def spec_all(shape):
    zeros = (0,) * len(shape)
    return pl.BlockSpec(shape, lambda *ids: zeros)


def slot_row_of(route_row, experts, cap):
    tokens = route_row.shape[1]
    padded = max(8, experts)
    hits = one_hot(iota((padded, tokens), 0) == route_row)
    earlier = one_hot(iota((tokens, tokens), 0) < iota((tokens, tokens), 1))
    ranks = mm(hits, earlier)
    rank = jnp.sum(ranks * hits.astype(F32), 0, keepdims=True)
    return route_row * cap + rank.astype(jnp.int32)


def slot_col_of(route_col, experts, cap):
    tokens = route_col.shape[0]
    hits = one_hot(iota((tokens, 128), 1) == route_col)
    earlier = one_hot(iota((tokens, tokens), 1) < iota((tokens, tokens), 0))
    ranks = mm(earlier, hits)
    rank = jnp.sum(ranks * hits.astype(F32), 1, keepdims=True)
    return route_col * cap + rank.astype(jnp.int32)


def as_row(col):
    rows = col.shape[0]
    eye = iota((rows, rows), 0) == iota((rows, rows), 1)
    return jnp.sum(jnp.where(eye, col, 0.0), 0, keepdims=True)


def as_col(row):
    rows = row.shape[1]
    eye = iota((rows, rows), 0) == iota((rows, rows), 1)
    return jnp.sum(jnp.where(eye, row, 0.0), 1, keepdims=True)


def gather_kernel(experts, cap, route_ref, x_ref, out_ref, slot_ref):
    step = pl.program_id(0)

    @pl.when(step == 0)
    def _():
        slot = slot_row_of(route_ref[...], experts, cap)
        slot_ref[...] = jnp.broadcast_to(slot, slot_ref.shape)

    rows = out_ref.shape[0]
    tokens = x_ref.shape[0]
    pick = one_hot(iota((rows, tokens), 0) + step * rows == slot_ref[0:1, :])
    out_ref[...] = mm(pick, x_ref[...]).astype(BF16)


def gather_slots(route_row, x, experts, cap):
    tokens, width = x.shape
    slots = experts * cap
    rows = 256
    return pl.pallas_call(
        functools.partial(gather_kernel, experts, cap),
        grid=(slots // rows,),
        in_specs=[spec_all((1, tokens)), spec_all((tokens, width))],
        out_specs=pl.BlockSpec((rows, width), lambda i: (i, 0)),
        out_shape=jax.ShapeDtypeStruct((slots, width), BF16),
        scratch_shapes=[pltpu.VMEM((8, tokens), jnp.int32)],
        compiler_params=params(32),
        cost_estimate=cost(2 * slots * tokens * width, 2 * width * (tokens + slots)),
        name="gather_slots",
    )(route_row, x)


def norm_parts(values):
    average = jnp.mean(values, -1, keepdims=True)
    centred = values - average
    spread = jnp.mean(centred * centred, -1, keepdims=True)
    scale = lax.rsqrt(spread + 1e-05)
    return centred * scale, scale


def norm_back(grad, gain, unit, scale):
    grad_unit = grad * gain
    inner = jnp.mean(grad_unit * unit, -1, keepdims=True)
    return scale * (grad_unit - jnp.mean(grad_unit, -1, keepdims=True) - unit * inner)


def qkv_kernel(x_ref, gain_ref, bias_ref, wq_ref, wk_ref, wv_ref, q_ref, k_ref, v_ref):
    unit, _ = norm_parts(x_ref[...].astype(F32))
    normed = (unit * gain_ref[...] + bias_ref[...]).astype(BF16)
    for w_ref, o_ref in ((wq_ref, q_ref), (wk_ref, k_ref), (wv_ref, v_ref)):
        o_ref[...] = mm(normed, w_ref[...]).astype(BF16)


def qkv(x, gain, bias, wq, wk, wv):
    tokens, width = x.shape
    rows = 256
    block = pl.BlockSpec((rows, width), lambda i: (i, 0))
    made = jax.ShapeDtypeStruct((tokens, width), BF16)
    return pl.pallas_call(
        qkv_kernel,
        grid=(tokens // rows,),
        in_specs=[block, spec_all((1, width)), spec_all((1, width))]
        + [spec_all((width, width))] * 3,
        out_specs=[block] * 3,
        out_shape=[made] * 3,
        compiler_params=params(32),
        cost_estimate=cost(6 * tokens * width * width, 2 * (4 * tokens * width + 3 * width * width)),
        name="qkv",
    )(x, gain, bias, wq, wk, wv)


def key_window(block, rows, tokens, longest):
    first = max(0, (block * rows - longest + 1) // 128 * 128)
    last = min(tokens, -(-(block * rows + rows - 1 + longest) // 128) * 128)
    return first, last


def attention_kernel(rows, longest, q_ref, k_ref, v_ref, seg_ref, mixed_ref, prob_ref):
    tokens = q_ref.shape[0]
    lane = iota((tokens, PAIR), 1)
    own = (lane < HEAD_DIM, lane >= HEAD_DIM)
    seg = seg_ref[...]
    queries = q_ref[...] * jnp.asarray(HEAD_DIM**-0.5, BF16)
    keys = k_ref[...]
    for h in range(2):
        other = (1 - h) * HEAD_DIM
        q_tag = jnp.where(lane - other == seg, 1.0, 0.0).astype(BF16)
        k_tag = jnp.where(lane - other == seg, 0.0, FAR)
        k_tag = jnp.where((lane >= other) & (lane < other + 8), k_tag, 0.0).astype(BF16)
        q_h = jnp.where(own[h], queries, q_tag)
        k_h = jnp.where(own[h], keys, k_tag)
        for block in range(tokens // rows):
            first, last = key_window(block, rows, tokens, longest)
            mine = slice(block * rows, (block + 1) * rows)
            scores = mm_cols(k_h[first:last], q_h[mine])
            largest = jnp.max(scores, 0, keepdims=True)
            weights = jnp.exp(scores - largest)
            total = jnp.sum(weights, 0, keepdims=True)
            probs = (weights * (1.0 / total)).astype(BF16)
            prob_ref[h, first:last, mine] = probs
            out = mm_rows(probs, v_ref[first:last, :]).astype(BF16)
            if h == 0:
                mixed_ref[mine, :] = out
            else:
                mixed_ref[mine, :] = jnp.where(own[1][mine], out, mixed_ref[mine, :])


def attention(q, k, v, seg_col, longest):
    tokens, width = q.shape
    pairs = width // PAIR
    rows = 256
    block = pl.BlockSpec((tokens, PAIR), lambda p: (0, p))
    return pl.pallas_call(
        functools.partial(attention_kernel, rows, longest),
        grid=(pairs,),
        in_specs=[block, block, block, spec_all((tokens, 1))],
        out_specs=[block, pl.BlockSpec((2, tokens, tokens), lambda p: (p, 0, 0))],
        out_shape=[
            jax.ShapeDtypeStruct((tokens, width), BF16),
            jax.ShapeDtypeStruct((2 * pairs, tokens, tokens), BF16),
        ],
        compiler_params=params(),
        cost_estimate=cost(
            4 * 2 * pairs * tokens * tokens * 256, 4 * pairs * tokens * tokens, tokens * tokens
        ),
        name="attention",
    )(q, k, v, seg_col)


def attention_back_kernel(
    rows, longest, q_ref, k_ref, v_ref, do_ref, prob_ref, delta_ref,
    dq_ref, dk_ref, dv_ref, dk_sum, dv_sum,
):
    tokens = q_ref.shape[0]
    lane = iota((tokens, PAIR), 1)
    own = (lane < HEAD_DIM, lane >= HEAD_DIM)
    zero = jnp.zeros((), BF16)
    scale = HEAD_DIM**-0.5
    dk_sum[...] = jnp.zeros_like(dk_sum)
    dv_sum[...] = jnp.zeros_like(dv_sum)
    for block in range(tokens // rows):
        first, last = key_window(block, rows, tokens, longest)
        mine = slice(block * rows, (block + 1) * rows)
        values = v_ref[first:last, :]
        dq = jnp.zeros((rows, PAIR), F32)
        dk = jnp.zeros((last - first, PAIR), F32)
        dv = jnp.zeros((last - first, PAIR), F32)
        for h in range(2):
            do_h = jnp.where(own[h][mine], do_ref[mine, :], zero)
            q_h = jnp.where(own[h][mine], q_ref[mine, :], zero)
            k_h = jnp.where(own[h][first:last], k_ref[first:last, :], zero)
            probs = prob_ref[h, first:last, mine]
            grad_probs = mm_cols(values, do_h)
            grad_scores = (
                probs.astype(F32) * (grad_probs - delta_ref[0, h : h + 1, mine])
            ).astype(BF16)
            dq = dq + mm_rows(grad_scores, k_h)
            dk = dk + mm(grad_scores, q_h)
            dv = dv + mm(probs, do_h)
        dq_ref[mine, :] = (dq * scale).astype(BF16)
        dk_sum[first:last, :] += dk
        dv_sum[first:last, :] += dv
    dk_ref[...] = (dk_sum[...] * scale).astype(BF16)
    dv_ref[...] = dv_sum[...].astype(BF16)


def attention_back(q, k, v, grad_mixed, probs, delta, longest):
    tokens, width = q.shape
    pairs = width // PAIR
    rows = 256
    block = pl.BlockSpec((tokens, PAIR), lambda p: (0, p))
    made = jax.ShapeDtypeStruct((tokens, width), BF16)
    return pl.pallas_call(
        functools.partial(attention_back_kernel, rows, longest),
        grid=(pairs,),
        in_specs=[block] * 4
        + [
            pl.BlockSpec((2, tokens, tokens), lambda p: (p, 0, 0)),
            pl.BlockSpec((1, 8, tokens), lambda p: (p, 0, 0)),
        ],
        out_specs=[block] * 3,
        out_shape=[made] * 3,
        scratch_shapes=[pltpu.VMEM((tokens, PAIR), F32)] * 2,
        compiler_params=params(),
        cost_estimate=cost(8 * 2 * pairs * tokens * tokens * 256, 4 * pairs * tokens * tokens),
        name="attention_back",
    )(q, k, v, grad_mixed, probs, delta)


def router_parts(normed, proj, embed, route, experts):
    low = jnp.dot(normed, proj, precision=EXACT, preferred_element_type=F32)
    low_squares = jnp.sum(low * low, -1, keepdims=True)
    low_scale = lax.rsqrt(jnp.maximum(low_squares, 1.0))
    low_unit = low * low_scale
    squares = jnp.sum(embed * embed, -1, keepdims=True)
    table_scale = lax.rsqrt(jnp.maximum(squares, 1.0))
    table = embed * table_scale
    logits = mm_cols(low_unit, table, EXACT) / SHARPNESS
    lane = iota(logits.shape, 1)
    logits = jnp.where(lane < experts, logits, FAR)
    weights = jnp.exp(logits - jnp.max(logits, -1, keepdims=True))
    probs = weights / jnp.sum(weights, -1, keepdims=True)
    chosen = jnp.where(lane == route, 1.0, 0.0)
    gate = jnp.sum(probs * chosen, -1, keepdims=True)
    return gate, probs, chosen, low, low_squares, low_scale, low_unit, squares, table_scale, table


def clipped_back(grad_unit, raw, scale, squares):
    share = jnp.where(squares > 1.0, 1.0, jnp.where(squares == 1.0, 0.5, 0.0))
    inner = jnp.sum(grad_unit * raw, -1, keepdims=True)
    return scale * grad_unit - share * scale * scale * scale * inner * raw


def middle_kernel(
    experts, cap, mixed_ref, x_ref, wo_ref, gain_ref, bias_ref, proj_ref, embed_ref,
    route_ref, route_row_ref, hidden_ref, gate_ref, slots_ref, gates_ref, kept,
):
    tokens, width = x_ref.shape
    rows = 256

    def row_block(i, carry):
        at = pl.ds(pl.multiple_of(i * rows, rows), rows)
        hidden = x_ref[at, :].astype(F32) + mm(mixed_ref[at, :], wo_ref[...])
        hidden_ref[at, :] = hidden
        unit, _ = norm_parts(hidden)
        normed = unit * gain_ref[...] + bias_ref[...]
        gate = router_parts(normed, proj_ref[...], embed_ref[...], route_ref[at, :], experts)[0]
        gate_ref[at, :] = jnp.broadcast_to(gate, (rows, 128))
        high = gate.astype(BF16).astype(F32)
        mid = (gate - high).astype(BF16).astype(F32)
        rest = gate - high - mid
        lane = iota((rows, 128), 1)
        split = jnp.where(lane == 0, high, jnp.where(lane == 1, mid, jnp.where(lane == 2, rest, 0.0)))
        kept[at, 0:width] = normed.astype(BF16)
        kept[at, width : width + 128] = split.astype(BF16)
        return carry

    lax.fori_loop(0, tokens // rows, row_block, 0)
    slot = slot_row_of(route_row_ref[...], experts, cap)

    def slot_block(i, carry):
        at = pl.ds(pl.multiple_of(i * rows, rows), rows)
        pick = one_hot(iota((rows, tokens), 0) + i * rows == slot)
        got = mm(pick, kept[...])
        slots_ref[at, :] = got[:, 0:width].astype(BF16)
        gates_ref[pl.ds(i, 1), :, :] = jnp.broadcast_to(
            as_row(jnp.sum(got[:, width : width + 128], 1, keepdims=True)), (8, rows)
        )[None]
        return carry

    lax.fori_loop(0, experts * cap // rows, slot_block, 0)


def middle(mixed, x, wo, gain, bias, proj, embed, route, route_row, experts, cap):
    tokens, width = x.shape
    slots = experts * cap
    args = (mixed, x, wo, gain, bias, proj, embed, route, route_row)
    return pl.pallas_call(
        functools.partial(middle_kernel, experts, cap),
        out_shape=[
            jax.ShapeDtypeStruct((tokens, width), F32),
            jax.ShapeDtypeStruct((tokens, 128), F32),
            jax.ShapeDtypeStruct((slots, width), BF16),
            jax.ShapeDtypeStruct((slots // 256, 8, 256), F32),
        ],
        scratch_shapes=[pltpu.VMEM((tokens, width + 128), BF16)],
        compiler_params=params(),
        cost_estimate=cost(2 * tokens * width * (width + slots), 16 * tokens * width),
        name="middle",
    )(*args)


def gelu_parts(pre):
    size = jnp.abs(pre)
    t = pl.reciprocal(1.0 + 0.23164189298 * size, approx=False)
    bell = jnp.exp(-0.5 * pre * pre)
    tail = t * (
        0.127414796
        + t * (-0.142248368 + t * (0.7107068705 + t * (-0.7265760135 + t * 0.5307027145)))
    )
    tail = tail * bell
    phi_sum = jnp.where(pre >= 0, 1.0 - tail, tail)
    return phi_sum, pre * bell * 0.3989422804014327


def expert_kernel(
    x_ref, up_ref, gate_ref, w_in_ref, w_out_ref,
    made_ref, back_ref, gate_grad_ref, active_ref, grad_pre_ref, scaled_ref,
):
    hidden = w_in_ref.shape[1]
    step = 512
    gate = as_col(gate_ref[0, 0:1, :])
    up = up_ref[...].astype(F32)
    scaled = (up * gate).astype(BF16)
    scaled_ref[...] = scaled
    x = x_ref[...]
    for at in range(0, hidden, step):
        part = slice(at, at + step)
        pre = mm(x, w_in_ref[:, part])
        grad_active = mm_cols(scaled, w_out_ref[part, :])
        phi_sum, slope = gelu_parts(pre)
        active_ref[:, part] = (pre * phi_sum).astype(BF16)
        grad_pre_ref[:, part] = (grad_active * (phi_sum + slope)).astype(BF16)
    made = mm(active_ref[...], w_out_ref[...]).astype(BF16)
    made_ref[...] = made
    gate_grad = jnp.sum(up * made.astype(F32), 1, keepdims=True)
    gate_grad_ref[...] = jnp.broadcast_to(as_row(gate_grad), (8, x.shape[0]))[None]
    back_ref[...] = mm_cols(grad_pre_ref[...], w_in_ref[...]).astype(BF16)


def expert(x, up, gates, w_in, w_out):
    slots, width = x.shape
    hidden = w_in.shape[1]
    rows = 256
    block = pl.BlockSpec((rows, width), lambda i: (i, 0))
    wide = pl.BlockSpec((rows, hidden), lambda i: (i, 0))
    line = pl.BlockSpec((1, 8, rows), lambda i: (i, 0, 0))
    made = jax.ShapeDtypeStruct((slots, width), BF16)
    made_wide = jax.ShapeDtypeStruct((slots, hidden), BF16)
    return pl.pallas_call(
        expert_kernel,
        grid=(slots // rows,),
        in_specs=[block, block, line, spec_all((width, hidden)), spec_all((hidden, width))],
        out_specs=[block, block, line, wide, wide, block],
        out_shape=[
            made,
            made,
            jax.ShapeDtypeStruct((slots // rows, 8, rows), F32),
            made_wide,
            made_wide,
            made,
        ],
        compiler_params=params(),
        cost_estimate=cost(8 * slots * width * hidden, 4 * slots * hidden),
        name="expert",
    )(x, up, gates, w_in, w_out)


def expert_grads_kernel(x_ref, scaled_ref, active_ref, grad_pre_ref, din_ref, dout_ref):
    din_ref[...] = mm_rows(x_ref[...], grad_pre_ref[...]).astype(BF16)
    dout_ref[...] = mm_rows(active_ref[...], scaled_ref[...]).astype(BF16)


def expert_grads(x, scaled, active, grad_pre):
    slots, width = x.shape
    hidden = active.shape[1]
    step = 512
    tall = pl.BlockSpec((slots, step), lambda i: (0, i))
    return pl.pallas_call(
        expert_grads_kernel,
        grid=(hidden // step,),
        in_specs=[spec_all((slots, width)), spec_all((slots, width)), tall, tall],
        out_specs=[
            pl.BlockSpec((width, step), lambda i: (0, i)),
            pl.BlockSpec((step, width), lambda i: (i, 0)),
        ],
        out_shape=[
            jax.ShapeDtypeStruct((width, hidden), BF16),
            jax.ShapeDtypeStruct((hidden, width), BF16),
        ],
        compiler_params=params(),
        cost_estimate=cost(4 * slots * width * hidden, 4 * slots * hidden + 4 * width * hidden),
        name="expert_grads",
    )(x, scaled, active, grad_pre)


def middle_back_kernel(
    experts, cap, back_ref, gate_grads_ref, hidden_ref, cot_ref, mixed_ref, wo_ref,
    gain_ref, bias_ref, proj_ref, embed_ref, route_ref,
    grad_hidden_ref, grad_mixed_ref, delta_ref, dwo_ref, small_ref, dproj_ref, dembed_ref,
    slot_ref, low_ref,
):
    tokens, width = hidden_ref.shape
    slots = back_ref.shape[0]
    rows = 256
    slot_ref[...] = jnp.broadcast_to(slot_col_of(route_ref[...], experts, cap), slot_ref.shape)
    small_ref[...] = jnp.zeros_like(small_ref)
    dproj_ref[...] = jnp.zeros_like(dproj_ref)
    dembed_ref[...] = jnp.zeros_like(dembed_ref)
    heads = width // HEAD_DIM
    pairs = heads // 2
    head_of = iota((8 * pairs, width), 1) // HEAD_DIM
    line = iota((8 * pairs, width), 0)
    head_lines = jnp.where(head_of == line // 8 * 2 + line % 8, 1.0, 0.0)
    head_lines = jnp.where(line % 8 < 2, head_lines, 0.0)

    def row_block(i, carry):
        at = pl.ds(pl.multiple_of(i * rows, rows), rows)
        place = slot_ref[at, 0:1]
        pick = iota((rows, slots), 1) == place
        grad = mm(one_hot(pick), back_ref[...])
        gate_grad = jnp.zeros((rows, 1), F32)
        for e in range(slots // rows):
            gate_grad = gate_grad + jnp.sum(
                jnp.where(pick[:, e * rows : (e + 1) * rows], gate_grads_ref[e, 0:1, :], 0.0),
                1,
                keepdims=True,
            )
        unit, scale = norm_parts(hidden_ref[at, :])
        normed = unit * gain_ref[...] + bias_ref[...]
        proj = proj_ref[...]
        embed = embed_ref[...]
        gate, probs, chosen, low, low_squares, low_scale, low_unit, _, _, table = router_parts(
            normed, proj, embed, route_ref[at, :], experts
        )
        grad_logits = gate_grad * gate * (chosen - probs) / SHARPNESS
        grad_unit = jnp.dot(grad_logits, table, precision=EXACT, preferred_element_type=F32)
        dembed_ref[...] += mm_rows(grad_logits, low_unit, EXACT)
        grad_low = clipped_back(grad_unit, low, low_scale, low_squares)
        dproj_ref[...] += mm_rows(normed, grad_low, EXACT)
        grad = grad + mm_cols(grad_low, proj, EXACT)
        small_ref[0:1, :] += jnp.sum(grad * unit, 0, keepdims=True)
        small_ref[1:2, :] += jnp.sum(grad, 0, keepdims=True)
        grad_hidden = cot_ref[at, :].astype(F32) + norm_back(grad, gain_ref[...], unit, scale)
        grad_hidden_ref[at, :] = grad_hidden
        low_grad = grad_hidden.astype(BF16)
        low_ref[at, :] = low_grad
        grad_mixed = mm_cols(low_grad, wo_ref[...]).astype(BF16)
        grad_mixed_ref[at, :] = grad_mixed
        products = grad_mixed.astype(F32) * mixed_ref[at, :].astype(F32)
        lines = mm_cols(head_lines, products, EXACT)
        for p in range(pairs):
            delta_ref[p, :, at] = lines[8 * p : 8 * p + 8, :]
        return carry

    lax.fori_loop(0, tokens // rows, row_block, 0)
    embed = embed_ref[...]
    squares = jnp.sum(embed * embed, -1, keepdims=True)
    table_scale = lax.rsqrt(jnp.maximum(squares, 1.0))
    dembed_ref[...] = clipped_back(dembed_ref[...], embed, table_scale, squares)
    dwo_ref[...] = mm_rows(mixed_ref[...], low_ref[...])


def middle_back(
    back, gate_grads, hidden, cot, mixed, wo, gain, bias, proj, embed, route, experts, cap
):
    tokens, width = hidden.shape
    slots = back.shape[0]
    args = (back, gate_grads, hidden, cot, mixed, wo, gain, bias, proj, embed, route)
    return pl.pallas_call(
        functools.partial(middle_back_kernel, experts, cap),
        out_shape=[
            jax.ShapeDtypeStruct((tokens, width), F32),
            jax.ShapeDtypeStruct((tokens, width), BF16),
            jax.ShapeDtypeStruct((width // PAIR, 8, tokens), F32),
            jax.ShapeDtypeStruct((width, width), F32),
            jax.ShapeDtypeStruct((8, width), F32),
            jax.ShapeDtypeStruct(proj.shape, F32),
            jax.ShapeDtypeStruct(embed.shape, F32),
        ],
        scratch_shapes=[pltpu.VMEM((tokens, 128), jnp.int32), pltpu.VMEM((tokens, width), BF16)],
        compiler_params=params(),
        cost_estimate=cost(2 * tokens * width * (2 * width + slots), 20 * tokens * width),
        name="middle_back",
    )(*args)


def qkv_back_kernel(
    x_ref, gain_ref, bias_ref, grad_hidden_ref, dq_ref, dk_ref, dv_ref, wq_ref, wk_ref, wv_ref,
    grad_ref, dwq_ref, dwk_ref, dwv_ref, small_ref, low_ref,
):
    tokens, width = x_ref.shape
    rows = 256
    small_ref[...] = jnp.zeros_like(small_ref)

    def row_block(i, carry):
        at = pl.ds(pl.multiple_of(i * rows, rows), rows)
        unit, scale = norm_parts(x_ref[at, :].astype(F32))
        low_ref[at, :] = (unit * gain_ref[...] + bias_ref[...]).astype(BF16)
        grad = (
            mm_cols(dq_ref[at, :], wq_ref[...])
            + mm_cols(dk_ref[at, :], wk_ref[...])
            + mm_cols(dv_ref[at, :], wv_ref[...])
        )
        small_ref[0:1, :] += jnp.sum(grad * unit, 0, keepdims=True)
        small_ref[1:2, :] += jnp.sum(grad, 0, keepdims=True)
        grad_ref[at, :] = grad_hidden_ref[at, :] + norm_back(grad, gain_ref[...], unit, scale)
        return carry

    lax.fori_loop(0, tokens // rows, row_block, 0)
    low = low_ref[...]
    dwq_ref[...] = mm_rows(low, dq_ref[...])
    dwk_ref[...] = mm_rows(low, dk_ref[...])
    dwv_ref[...] = mm_rows(low, dv_ref[...])


def qkv_back(x, gain, bias, grad_hidden, dq, dk, dv, wq, wk, wv):
    tokens, width = x.shape
    square = jax.ShapeDtypeStruct((width, width), F32)
    return pl.pallas_call(
        qkv_back_kernel,
        out_shape=[
            jax.ShapeDtypeStruct((tokens, width), F32),
            square,
            square,
            square,
            jax.ShapeDtypeStruct((8, width), F32),
        ],
        scratch_shapes=[pltpu.VMEM((tokens, width), BF16)],
        compiler_params=params(),
        cost_estimate=cost(12 * tokens * width * width, 20 * tokens * width),
        name="qkv_back",
    )(x, gain, bias, grad_hidden, dq, dk, dv, wq, wk, wv)


def output_kernel(experts, cap, made_ref, hidden_ref, gate_ref, route_ref, out_ref, slot_ref):
    tokens, width = hidden_ref.shape
    slots = made_ref.shape[0]
    rows = 256
    slot_ref[...] = jnp.broadcast_to(slot_col_of(route_ref[...], experts, cap), slot_ref.shape)

    def row_block(i, carry):
        at = pl.ds(pl.multiple_of(i * rows, rows), rows)
        pick = one_hot(iota((rows, slots), 1) == slot_ref[at, 0:1])
        produced = mm(pick, made_ref[...])
        out_ref[at, :] = (hidden_ref[at, :] + gate_ref[at, 0:1] * produced).astype(BF16)
        return carry

    lax.fori_loop(0, tokens // rows, row_block, 0)


def layer_output(made, hidden, gate, route, experts, cap):
    tokens, width = hidden.shape
    return pl.pallas_call(
        functools.partial(output_kernel, experts, cap),
        out_shape=jax.ShapeDtypeStruct((tokens, width), BF16),
        scratch_shapes=[pltpu.VMEM((tokens, 128), jnp.int32)],
        compiler_params=params(),
        cost_estimate=cost(2 * tokens * width * made.shape[0], 10 * tokens * width),
        name="layer_output",
    )(made, hidden, gate, route)


def exchange(array, experts):
    split = array.reshape(experts, array.shape[0] // experts, *array.shape[1:])
    return lax.all_to_all(split, "expert", split_axis=0, concat_axis=0, tiled=True).reshape(
        array.shape
    )


def lines_out(lines, experts, cap):
    return lines[:, 0, :].reshape(experts, cap)


def lines_in(rows):
    flat = rows.reshape(-1, 1, 256)
    return jnp.broadcast_to(flat, (flat.shape[0], 8, 256))


def on_device(
    tokens,
    segment_ids,
    routes,
    norm1_gain,
    norm1_bias,
    query_weight,
    w_key,
    w_value,
    w_output,
    norm2_gain,
    norm2_bias,
    router_proj,
    expert_embed,
    expert_in,
    expert_out,
    cotangent,
):
    count, width = tokens.shape
    experts = lax.axis_size("expert")
    cap = 2 * count // experts
    longest = segment_ids.shape[1] // 2
    route_row = routes.reshape(1, count)
    seg_col = segment_ids.reshape(count, 1)
    gain1, bias1 = norm1_gain[None], norm1_bias[None]
    gain2, bias2 = norm2_gain[None], norm2_bias[None]
    space = router_proj.shape[1]
    proj = jnp.pad(router_proj, ((0, 0), (0, 128 - space)))
    embed = jnp.pad(expert_embed, ((0, 128 - experts), (0, 128 - space)))

    up_slots = gather_slots(route_row, cotangent, experts, cap)
    up_here = exchange(up_slots, experts)
    q, k, v = qkv(tokens, gain1, bias1, query_weight, w_key, w_value)
    mixed, probs = attention(q, k, v, seg_col, longest)
    hidden, gate, slots, gates = middle(
        mixed, tokens, w_output, gain2, bias2, proj, embed, routes, route_row, experts, cap
    )
    x_here = exchange(slots, experts)
    gates_here = lines_in(exchange(lines_out(gates, experts, cap), experts))
    made, back, gate_grads, active, grad_pre, scaled = expert(
        x_here, up_here, gates_here, expert_in[0], expert_out[0]
    )
    back_home = exchange(back, experts)
    gate_grads_home = lines_in(exchange(lines_out(gate_grads, experts, cap), experts))
    grad_in, grad_out = expert_grads(x_here, scaled, active, grad_pre)
    made_home = exchange(made, experts)
    grad_in = lax.psum_scatter(grad_in[None], "dp", scatter_dimension=2, tiled=True)
    grad_out = lax.psum_scatter(grad_out[None], "dp", scatter_dimension=1, tiled=True)
    grad_hidden, grad_mixed, delta, dwo, small2, dproj, dembed = middle_back(
        back_home, gate_grads_home, hidden, cotangent, mixed, w_output, gain2, bias2,
        proj, embed, routes, experts, cap,
    )
    dq, dk, dv = attention_back(q, k, v, grad_mixed, probs, delta, longest)
    grad_input, dwq, dwk, dwv, small1 = qkv_back(
        tokens, gain1, bias1, grad_hidden, dq, dk, dv, query_weight, w_key, w_value
    )
    output = layer_output(made_home, hidden, gate, routes, experts, cap)
    summed = lax.psum(
        (
            small1[0],
            small1[1],
            dwq,
            dwk,
            dwv,
            dwo,
            small2[0],
            small2[1],
            dproj[:, :space],
            dembed[:experts, :space],
        ),
        ("dp", "expert"),
    )
    return (output, grad_input, *summed, grad_in.astype(F32), grad_out.astype(F32))


def solution(mesh):
    split = P(("dp", "expert"), None)
    in_specs = (
        (split,) * 3 + (P(),) * 10 + (P("expert", None, None), P("expert", None, None), split)
    )
    out_specs = (
        (split, split) + (P(),) * 10 + (P("expert", None, "dp"), P("expert", "dp", None))
    )
    return jax.shard_map(
        on_device, mesh=mesh, in_specs=in_specs, out_specs=out_specs, check_vma=False
    )
```

```python
import functools

import jax
import jax.numpy as jnp
from jax import lax
from jax.experimental import pallas as pl
from jax.experimental.pallas import tpu as pltpu
from jax.sharding import PartitionSpec as P

HEAD_DIM = 64
PAIR = 2 * HEAD_DIM
SHARPNESS = 0.25
EXACT = lax.Precision.HIGHEST
BF16 = jnp.bfloat16
F32 = jnp.float32
FAR = -1e30
MIB = 1 << 20


def mm(left, right):
    return jnp.dot(left, right, preferred_element_type=F32)


def mm_rows(left, right, precision=None):
    return lax.dot_general(
        left, right, (((0,), (0,)), ((), ())), precision=precision, preferred_element_type=F32
    )


def mm_cols(left, right, precision=None):
    return lax.dot_general(
        left, right, (((1,), (1,)), ((), ())), precision=precision, preferred_element_type=F32
    )


def iota(shape, axis):
    return lax.broadcasted_iota(jnp.int32, shape, axis)


def one_hot(condition):
    return jnp.where(condition, 1.0, 0.0).astype(BF16)


def params(limit=56):
    return pltpu.CompilerParams(vmem_limit_bytes=limit * MIB)


def cost(flops, moved, trans=0):
    return pl.CostEstimate(flops=int(flops), bytes_accessed=int(moved), transcendentals=int(trans))


def spec_all(shape):
    zeros = (0,) * len(shape)
    return pl.BlockSpec(shape, lambda *ids: zeros)


def slot_row_of(route_row, experts, cap):
    tokens = route_row.shape[1]
    padded = max(8, experts)
    hits = one_hot(iota((padded, tokens), 0) == route_row)
    earlier = one_hot(iota((tokens, tokens), 0) < iota((tokens, tokens), 1))
    ranks = mm(hits, earlier)
    rank = jnp.sum(ranks * hits.astype(F32), 0, keepdims=True)
    return route_row * cap + rank.astype(jnp.int32)


def slot_col_of(route_col, experts, cap):
    tokens = route_col.shape[0]
    hits = one_hot(iota((tokens, 128), 1) == route_col)
    earlier = one_hot(iota((tokens, tokens), 1) < iota((tokens, tokens), 0))
    ranks = mm(earlier, hits)
    rank = jnp.sum(ranks * hits.astype(F32), 1, keepdims=True)
    return route_col * cap + rank.astype(jnp.int32)


def as_row(col):
    rows = col.shape[0]
    eye = iota((rows, rows), 0) == iota((rows, rows), 1)
    return jnp.sum(jnp.where(eye, col, 0.0), 0, keepdims=True)


def as_col(row):
    rows = row.shape[1]
    eye = iota((rows, rows), 0) == iota((rows, rows), 1)
    return jnp.sum(jnp.where(eye, row, 0.0), 1, keepdims=True)


def gather_kernel(experts, cap, route_ref, x_ref, *out_refs):
    slot = slot_row_of(route_ref[...], experts, cap)
    tokens = x_ref.shape[0]
    for e, out_ref in enumerate(out_refs):
        pick = one_hot(iota((cap, tokens), 0) + e * cap == slot)
        out_ref[...] = mm(pick, x_ref[...]).astype(BF16)


def gather_slots(route_row, x, experts, cap):
    tokens, width = x.shape
    slots = experts * cap
    return pl.pallas_call(
        functools.partial(gather_kernel, experts, cap),
        out_shape=[jax.ShapeDtypeStruct((cap, width), BF16)] * experts,
        compiler_params=params(32),
        cost_estimate=cost(2 * slots * tokens * width, 2 * width * (tokens + slots)),
        name="gather_slots",
    )(route_row, x)


def norm_parts(values):
    average = jnp.mean(values, -1, keepdims=True)
    centred = values - average
    spread = jnp.mean(centred * centred, -1, keepdims=True)
    scale = lax.rsqrt(spread + 1e-05)
    return centred * scale, scale


def norm_back(grad, gain, unit, scale):
    grad_unit = grad * gain
    inner = jnp.mean(grad_unit * unit, -1, keepdims=True)
    return scale * (grad_unit - jnp.mean(grad_unit, -1, keepdims=True) - unit * inner)


def qkv_kernel(x_ref, gain_ref, bias_ref, wq_ref, wk_ref, wv_ref, q_ref, k_ref, v_ref):
    unit, _ = norm_parts(x_ref[...].astype(F32))
    normed = (unit * gain_ref[...] + bias_ref[...]).astype(BF16)
    for w_ref, o_ref in ((wq_ref, q_ref), (wk_ref, k_ref), (wv_ref, v_ref)):
        o_ref[...] = mm(normed, w_ref[...]).astype(BF16)


def qkv(x, gain, bias, wq, wk, wv):
    tokens, width = x.shape
    rows = 256
    block = pl.BlockSpec((rows, width), lambda i: (i, 0))
    made = jax.ShapeDtypeStruct((tokens, width), BF16)
    return pl.pallas_call(
        qkv_kernel,
        grid=(tokens // rows,),
        in_specs=[block, spec_all((1, width)), spec_all((1, width))]
        + [spec_all((width, width))] * 3,
        out_specs=[block] * 3,
        out_shape=[made] * 3,
        compiler_params=params(32),
        cost_estimate=cost(6 * tokens * width * width, 2 * (4 * tokens * width + 3 * width * width)),
        name="qkv",
    )(x, gain, bias, wq, wk, wv)


def key_window(block, rows, tokens, longest):
    first = max(0, (block * rows - longest + 1) // 128 * 128)
    last = min(tokens, -(-(block * rows + rows - 1 + longest) // 128) * 128)
    return first, last


def attention_kernel(rows, longest, q_ref, k_ref, v_ref, seg_ref, mixed_ref, prob_ref):
    tokens = q_ref.shape[0]
    lane = iota((tokens, PAIR), 1)
    own = (lane < HEAD_DIM, lane >= HEAD_DIM)
    seg = seg_ref[...]
    queries = q_ref[...] * jnp.asarray(HEAD_DIM**-0.5, BF16)
    keys = k_ref[...]
    for h in range(2):
        other = (1 - h) * HEAD_DIM
        q_tag = jnp.where(lane - other == seg, 1.0, 0.0).astype(BF16)
        k_tag = jnp.where(lane - other == seg, 0.0, FAR)
        k_tag = jnp.where((lane >= other) & (lane < other + 8), k_tag, 0.0).astype(BF16)
        q_h = jnp.where(own[h], queries, q_tag)
        k_h = jnp.where(own[h], keys, k_tag)
        for block in range(tokens // rows):
            first, last = key_window(block, rows, tokens, longest)
            mine = slice(block * rows, (block + 1) * rows)
            scores = mm_cols(k_h[first:last], q_h[mine])
            largest = jnp.max(scores, 0, keepdims=True)
            weights = jnp.exp(scores - largest)
            total = jnp.sum(weights, 0, keepdims=True)
            probs = (weights * (1.0 / total)).astype(BF16)
            prob_ref[h, first:last, mine] = probs
            out = mm_rows(probs, v_ref[first:last, :]).astype(BF16)
            if h == 0:
                mixed_ref[mine, :] = out
            else:
                mixed_ref[mine, :] = jnp.where(own[1][mine], out, mixed_ref[mine, :])


def attention(q, k, v, seg_col, longest):
    tokens, width = q.shape
    pairs = width // PAIR
    rows = 256
    block = pl.BlockSpec((tokens, PAIR), lambda p: (0, p))
    return pl.pallas_call(
        functools.partial(attention_kernel, rows, longest),
        grid=(pairs,),
        in_specs=[block, block, block, spec_all((tokens, 1))],
        out_specs=[block, pl.BlockSpec((2, tokens, tokens), lambda p: (p, 0, 0))],
        out_shape=[
            jax.ShapeDtypeStruct((tokens, width), BF16),
            jax.ShapeDtypeStruct((2 * pairs, tokens, tokens), BF16),
        ],
        compiler_params=params(),
        cost_estimate=cost(
            4 * 2 * pairs * tokens * tokens * 256, 4 * pairs * tokens * tokens, tokens * tokens
        ),
        name="attention",
    )(q, k, v, seg_col)


def attention_back_kernel(
    rows, longest, q_ref, k_ref, v_ref, do_ref, prob_ref, delta_ref,
    dq_ref, dk_ref, dv_ref, dk_sum, dv_sum,
):
    tokens = q_ref.shape[0]
    lane = iota((tokens, PAIR), 1)
    own = (lane < HEAD_DIM, lane >= HEAD_DIM)
    zero = jnp.zeros((), BF16)
    scale = HEAD_DIM**-0.5
    dk_sum[...] = jnp.zeros_like(dk_sum)
    dv_sum[...] = jnp.zeros_like(dv_sum)
    for block in range(tokens // rows):
        first, last = key_window(block, rows, tokens, longest)
        mine = slice(block * rows, (block + 1) * rows)
        values = v_ref[first:last, :]
        dq = jnp.zeros((rows, PAIR), F32)
        dk = jnp.zeros((last - first, PAIR), F32)
        dv = jnp.zeros((last - first, PAIR), F32)
        for h in range(2):
            do_h = jnp.where(own[h][mine], do_ref[mine, :], zero)
            q_h = jnp.where(own[h][mine], q_ref[mine, :], zero)
            k_h = jnp.where(own[h][first:last], k_ref[first:last, :], zero)
            probs = prob_ref[h, first:last, mine]
            grad_probs = mm_cols(values, do_h)
            grad_scores = (
                probs.astype(F32) * (grad_probs - delta_ref[0, h : h + 1, mine])
            ).astype(BF16)
            dq = dq + mm_rows(grad_scores, k_h)
            dk = dk + mm(grad_scores, q_h)
            dv = dv + mm(probs, do_h)
        dq_ref[mine, :] = (dq * scale).astype(BF16)
        dk_sum[first:last, :] += dk
        dv_sum[first:last, :] += dv
    dk_ref[...] = (dk_sum[...] * scale).astype(BF16)
    dv_ref[...] = dv_sum[...].astype(BF16)


def attention_back(q, k, v, grad_mixed, probs, delta, longest):
    tokens, width = q.shape
    pairs = width // PAIR
    rows = 256
    block = pl.BlockSpec((tokens, PAIR), lambda p: (0, p))
    made = jax.ShapeDtypeStruct((tokens, width), BF16)
    return pl.pallas_call(
        functools.partial(attention_back_kernel, rows, longest),
        grid=(pairs,),
        in_specs=[block] * 4
        + [
            pl.BlockSpec((2, tokens, tokens), lambda p: (p, 0, 0)),
            pl.BlockSpec((1, 8, tokens), lambda p: (p, 0, 0)),
        ],
        out_specs=[block] * 3,
        out_shape=[made] * 3,
        scratch_shapes=[pltpu.VMEM((tokens, PAIR), F32)] * 2,
        compiler_params=params(),
        cost_estimate=cost(8 * 2 * pairs * tokens * tokens * 256, 4 * pairs * tokens * tokens),
        name="attention_back",
    )(q, k, v, grad_mixed, probs, delta)


def router_parts(normed, proj, embed, route, experts):
    low = jnp.dot(normed, proj, precision=EXACT, preferred_element_type=F32)
    low_squares = jnp.sum(low * low, -1, keepdims=True)
    low_scale = lax.rsqrt(jnp.maximum(low_squares, 1.0))
    low_unit = low * low_scale
    squares = jnp.sum(embed * embed, -1, keepdims=True)
    table_scale = lax.rsqrt(jnp.maximum(squares, 1.0))
    table = embed * table_scale
    logits = mm_cols(low_unit, table, EXACT) / SHARPNESS
    lane = iota(logits.shape, 1)
    logits = jnp.where(lane < experts, logits, FAR)
    weights = jnp.exp(logits - jnp.max(logits, -1, keepdims=True))
    probs = weights / jnp.sum(weights, -1, keepdims=True)
    chosen = jnp.where(lane == route, 1.0, 0.0)
    gate = jnp.sum(probs * chosen, -1, keepdims=True)
    return gate, probs, chosen, low, low_squares, low_scale, low_unit, squares, table_scale, table


def clipped_back(grad_unit, raw, scale, squares):
    share = jnp.where(squares > 1.0, 1.0, jnp.where(squares == 1.0, 0.5, 0.0))
    inner = jnp.sum(grad_unit * raw, -1, keepdims=True)
    return scale * grad_unit - share * scale * scale * scale * inner * raw


def middle_kernel(
    experts, cap, mixed_ref, x_ref, wo_ref, gain_ref, bias_ref, proj_ref, embed_ref,
    route_ref, place_row_ref, hidden_ref, gate_ref, slots_ref, gates_ref, kept,
):
    tokens, width = x_ref.shape
    rows = 256

    def row_block(i, carry):
        at = pl.ds(pl.multiple_of(i * rows, rows), rows)
        hidden = x_ref[at, :].astype(F32) + mm(mixed_ref[at, :], wo_ref[...])
        hidden_ref[at, :] = hidden
        unit, _ = norm_parts(hidden)
        normed = unit * gain_ref[...] + bias_ref[...]
        gate = router_parts(normed, proj_ref[...], embed_ref[...], route_ref[at, :], experts)[0]
        gate_ref[at, :] = jnp.broadcast_to(gate, (rows, 128))
        high = gate.astype(BF16).astype(F32)
        mid = (gate - high).astype(BF16).astype(F32)
        rest = gate - high - mid
        lane = iota((rows, 128), 1)
        split = jnp.where(lane == 0, high, jnp.where(lane == 1, mid, jnp.where(lane == 2, rest, 0.0)))
        kept[at, 0:width] = normed.astype(BF16)
        kept[at, width : width + 128] = split.astype(BF16)
        return carry

    lax.fori_loop(0, tokens // rows, row_block, 0)
    slot = slot_row_of(place_row_ref[...], experts, cap)

    def slot_block(e, carry):
        pick = one_hot(iota((cap, tokens), 0) + e * cap == slot)
        got = mm(pick, kept[...])
        slots_ref[e] = got[:, 0:width].astype(BF16)
        gates = as_row(jnp.sum(got[:, width : width + 128], 1, keepdims=True))
        gates_ref[e] = jnp.broadcast_to(gates, (8, cap))
        return carry

    lax.fori_loop(0, experts, slot_block, 0)


def middle(mixed, x, wo, gain, bias, proj, embed, route, place_row, experts, cap):
    tokens, width = x.shape
    slots = experts * cap
    args = (mixed, x, wo, gain, bias, proj, embed, route, place_row)
    return pl.pallas_call(
        functools.partial(middle_kernel, experts, cap),
        out_shape=[
            jax.ShapeDtypeStruct((tokens, width), F32),
            jax.ShapeDtypeStruct((tokens, 128), F32),
            jax.ShapeDtypeStruct((experts, cap, width), BF16),
            jax.ShapeDtypeStruct((experts, 8, cap), F32),
        ],
        scratch_shapes=[pltpu.VMEM((tokens, width + 128), BF16)],
        compiler_params=params(),
        cost_estimate=cost(2 * tokens * width * (width + slots), 16 * tokens * width),
        name="middle",
    )(*args)


def gelu_parts(pre):
    size = jnp.abs(pre)
    t = pl.reciprocal(1.0 + 0.23164189298 * size, approx=False)
    bell = jnp.exp(-0.5 * pre * pre)
    tail = t * (
        0.127414796
        + t * (-0.142248368 + t * (0.7107068705 + t * (-0.7265760135 + t * 0.5307027145)))
    )
    tail = tail * bell
    phi_sum = jnp.where(pre >= 0, 1.0 - tail, tail)
    return phi_sum, pre * bell * 0.3989422804014327


def expert_kernel(experts, x_axis, *refs):
    x_ref, gates_ref, w_in_ref, w_out_ref = refs[:4]
    up_refs = refs[4 : 4 + experts]
    back_ref, gate_grads_ref = refs[4 + experts : 6 + experts]
    rest = refs[6 + experts :]
    made_refs = rest[:experts]
    din_refs = rest[experts : experts + x_axis]
    dout_refs = rest[experts + x_axis : experts + 2 * x_axis]
    (
        x_here, up_here, gates_here, back_here, gate_grads_here, made_here,
        active, grad_pre, w_in, w_out, din_got, dout_got,
        load_sem, x_send, x_recv, g_send, g_recv, b_send, b_recv, gg_send, gg_recv,
        d_send, d_recv, store_sem,
    ) = rest[experts + 2 * x_axis :]
    cap, width = x_here.shape[1:]
    hidden = w_in.shape[1]
    me = lax.axis_index("expert")
    dp = lax.axis_index("dp")
    core = lax.rem(dp, 2)
    mesh_ids = pl.DeviceIdType.MESH

    barrier = pltpu.get_barrier_semaphore()

    def greet(s, carry):
        pl.semaphore_signal(
            barrier, inc=1, device_id={"expert": lax.rem(me + s, experts)}, device_id_type=mesh_ids
        )
        return carry

    lax.fori_loop(1, experts, greet, 0)
    pl.semaphore_signal(
        barrier, inc=1, device_id={"dp": dp + 1 - 2 * core}, device_id_type=mesh_ids
    )
    pl.semaphore_wait(barrier, experts)

    def out_copy(s):
        to = {"expert": lax.rem(me + s, experts)}
        return (
            pltpu.make_async_remote_copy(
                x_ref.at[s], x_here.at[s], x_send.at[s], x_recv.at[s], to, mesh_ids
            ),
            pltpu.make_async_remote_copy(
                gates_ref.at[s], gates_here.at[s], g_send.at[s], g_recv.at[s], to, mesh_ids
            ),
        )

    def home_copy(s):
        to = {"expert": lax.rem(me + experts - s, experts)}
        return (
            pltpu.make_async_remote_copy(
                back_here.at[s], back_ref.at[s], b_send.at[s], b_recv.at[s], to, mesh_ids
            ),
            pltpu.make_async_remote_copy(
                gate_grads_here.at[s], gate_grads_ref.at[s], gg_send.at[s], gg_recv.at[s], to, mesh_ids
            ),
        )

    def send_out(s, carry):
        for copy in out_copy(s):
            copy.start()
        return carry

    lax.fori_loop(1, experts, send_out, 0)
    loads = [
        pltpu.make_async_copy(x_ref.at[0], x_here.at[0], load_sem.at[0]),
        pltpu.make_async_copy(gates_ref.at[0], gates_here.at[0], load_sem.at[1]),
        pltpu.make_async_copy(w_in_ref, w_in, load_sem.at[2]),
        pltpu.make_async_copy(w_out_ref, w_out, load_sem.at[3]),
    ]
    for s, up_ref in enumerate(up_refs):
        loads.append(pltpu.make_async_copy(up_ref, up_here.at[s], load_sem.at[4 + s]))
    for load in loads:
        load.start()
    for load in loads:
        load.wait()

    step = 512

    def chunk(s, carry):
        @pl.when(s > 0)
        def _():
            for copy in out_copy(s):
                copy.wait_recv()

        at_rows = pl.ds(pl.multiple_of(s * cap, cap), cap)
        gate = as_col(gates_here[s][0:1, :])
        up = up_here[s].astype(F32)
        scaled = (up * gate).astype(BF16)
        x = x_here[s]
        for at in range(0, hidden, step):
            part = slice(at, at + step)
            pre = mm(x, w_in[:, part])
            grad_active = mm_cols(scaled, w_out[part, :])
            phi_sum, slope = gelu_parts(pre)
            active[at_rows, part] = (pre * phi_sum).astype(BF16)
            grad_pre[at_rows, part] = (grad_active * (phi_sum + slope)).astype(BF16)
        made = mm(active[at_rows, :], w_out[...]).astype(BF16)
        made_here[s] = made
        gate_grad = jnp.sum(up * made.astype(F32), 1, keepdims=True)
        gate_grads_here[s] = jnp.broadcast_to(as_row(gate_grad), (8, cap))
        up_here[s] = scaled
        back_here[s] = mm_cols(grad_pre[at_rows, :], w_in[...]).astype(BF16)

        @pl.when(s > 0)
        def _():
            for copy in home_copy(s):
                copy.start()

        return carry

    lax.fori_loop(0, experts, chunk, 0)
    stores = [
        pltpu.make_async_copy(back_here.at[0], back_ref.at[0], store_sem.at[0]),
        pltpu.make_async_copy(gate_grads_here.at[0], gate_grads_ref.at[0], store_sem.at[1]),
    ]
    for s, made_ref in enumerate(made_refs):
        stores.append(pltpu.make_async_copy(made_here.at[s], made_ref, store_sem.at[2 + s]))
    for store in stores:
        store.start()

    block = hidden // (2 * x_axis)
    slots = experts * cap
    other = {"dp": dp + 1 - 2 * core}
    x_all = x_here.reshape(slots, width)
    up_all = up_here.reshape(slots, width)

    def block_start(k, for_core):
        x_at = lax.rem(dp // 2 + k, x_axis)
        return pl.multiple_of((2 * x_at + for_core) * block, 128)

    def din_out(k):
        return w_in.at[:, k * block : (k + 1) * block]

    def dout_out(k):
        return w_out.at[k * block : (k + 1) * block]

    def core_copies(k):
        return (
            pltpu.make_async_remote_copy(
                din_out(k), din_got.at[k], d_send.at[k], d_recv.at[k], other, mesh_ids
            ),
            pltpu.make_async_remote_copy(
                dout_out(k),
                dout_got.at[k],
                d_send.at[x_axis + k],
                d_recv.at[x_axis + k],
                other,
                mesh_ids,
            ),
        )

    tile = 256 if block % 256 == 0 else 128

    def weight_grads(k, for_core, out, got):
        start = block_start(k, for_core)
        columns = slice(out * block, (out + 1) * block)
        for at in range(0, width, tile):
            part = slice(at, at + tile)
            value = mm_rows(x_all[:, part], grad_pre[:, pl.ds(start, block)])
            if got is not None:
                value = value + din_got[got, part, :].astype(F32)
            w_in[part, columns] = value.astype(BF16)
        for at in range(0, block, tile):
            value = mm_rows(active[:, pl.ds(pl.multiple_of(start + at, 128), tile)], up_all[...])
            if got is not None:
                value = value + dout_got[got, at : at + tile, :].astype(F32)
            w_out[out * block + at : out * block + at + tile, :] = value.astype(BF16)

    for k in range(x_axis):
        weight_grads(k, 1 - core, k, None)
        for copy in core_copies(k):
            copy.start()
    for k in range(x_axis):
        for copy in core_copies(k):
            copy.wait_recv()
        weight_grads(k, core, x_axis + k, k)
        for i, (src, ref) in enumerate(
            ((din_out(x_axis + k), din_refs[k]), (dout_out(x_axis + k), dout_refs[k]))
        ):
            store = pltpu.make_async_copy(src, ref, store_sem.at[2 + experts + 2 * k + i])
            store.start()
            stores.append(store)
    for store in stores:
        store.wait()
    for k in range(x_axis):
        for copy in core_copies(k):
            copy.wait_send()

    def finish(s, carry):
        for copy in out_copy(s):
            copy.wait_send()
        for copy in home_copy(s):
            copy.wait()
        return carry

    lax.fori_loop(1, experts, finish, 0)


def expert(x, gates, up, w_in, w_out, dp_size):
    experts, cap, width = x.shape
    hidden = w_in.shape[1]
    slots = experts * cap
    x_axis = dp_size // 2
    block = hidden // dp_size
    anywhere = pl.BlockSpec(memory_space=pl.ANY)
    rows = jax.ShapeDtypeStruct((cap, width), BF16)
    out_shape = (
        [
            jax.ShapeDtypeStruct((experts, cap, width), BF16),
            jax.ShapeDtypeStruct((experts, 8, cap), F32),
        ]
        + [rows] * experts
        + [jax.ShapeDtypeStruct((width, block), BF16)] * x_axis
        + [jax.ShapeDtypeStruct((block, width), BF16)] * x_axis
    )
    chunks = pltpu.VMEM((experts, cap, width), BF16)
    lines = pltpu.VMEM((experts, 8, cap), F32)
    sems = pltpu.SemaphoreType.DMA
    out = pl.pallas_call(
        functools.partial(expert_kernel, experts, x_axis),
        in_specs=[anywhere] * (4 + experts),
        out_specs=[anywhere] * len(out_shape),
        out_shape=out_shape,
        scratch_shapes=[
            chunks,
            chunks,
            lines,
            chunks,
            lines,
            chunks,
            pltpu.VMEM((slots, hidden), BF16),
            pltpu.VMEM((slots, hidden), BF16),
            pltpu.VMEM((width, hidden), BF16),
            pltpu.VMEM((hidden, width), BF16),
            pltpu.VMEM((x_axis, width, block), BF16),
            pltpu.VMEM((x_axis, block, width), BF16),
            sems((4 + experts,)),
        ]
        + [sems((experts,))] * 8
        + [sems((2 * x_axis,))] * 2
        + [sems((2 + experts + 2 * x_axis,))],
        compiler_params=pltpu.CompilerParams(
            vmem_limit_bytes=63 * MIB, collective_id=0, has_side_effects=True
        ),
        cost_estimate=cost(12 * slots * width * hidden, 8 * width * hidden),
        name="expert",
    )(x, gates, w_in, w_out, *up)
    back, gate_grads = out[:2]
    made = out[2 : 2 + experts]
    din = out[2 + experts : 2 + experts + x_axis]
    dout = out[2 + experts + x_axis :]
    return back, gate_grads, made, din, dout


def store_tiles(out_ref, value):
    for tile in range(out_ref.shape[0]):
        out_ref[tile] = value[:, tile * 128 : (tile + 1) * 128].astype(BF16)


def middle_back_kernel(
    experts, cap, back_ref, gate_grads_ref, hidden_ref, cot_ref, mixed_ref, wo_ref,
    gain_ref, bias_ref, proj_ref, embed_ref, route_ref, place_ref,
    grad_hidden_ref, grad_mixed_ref, delta_ref, dwo_ref, small_ref,
    slot_ref, low_ref, dproj_ref, dembed_ref,
):
    tokens, width = hidden_ref.shape
    slots = back_ref.shape[0]
    rows = 256
    slot_ref[...] = jnp.broadcast_to(slot_col_of(place_ref[...], experts, cap), slot_ref.shape)
    small_ref[...] = jnp.zeros_like(small_ref)
    dproj_ref[...] = jnp.zeros_like(dproj_ref)
    dembed_ref[...] = jnp.zeros_like(dembed_ref)
    heads = width // HEAD_DIM
    pairs = heads // 2
    head_of = iota((8 * pairs, width), 1) // HEAD_DIM
    line = iota((8 * pairs, width), 0)
    head_lines = jnp.where(head_of == line // 8 * 2 + line % 8, 1.0, 0.0)
    head_lines = jnp.where(line % 8 < 2, head_lines, 0.0)

    def row_block(i, carry):
        at = pl.ds(pl.multiple_of(i * rows, rows), rows)
        place = slot_ref[at, 0:1]
        pick = iota((rows, slots), 1) == place
        grad = mm(one_hot(pick), back_ref[...])
        gate_grad = jnp.zeros((rows, 1), F32)
        for e in range(experts):
            gate_grad = gate_grad + jnp.sum(
                jnp.where(pick[:, e * cap : (e + 1) * cap], gate_grads_ref[e, 0:1, :], 0.0),
                1,
                keepdims=True,
            )
        unit, scale = norm_parts(hidden_ref[at, :])
        normed = unit * gain_ref[...] + bias_ref[...]
        proj = proj_ref[...]
        embed = embed_ref[...]
        gate, probs, chosen, low, low_squares, low_scale, low_unit, _, _, table = router_parts(
            normed, proj, embed, route_ref[at, :], experts
        )
        grad_logits = gate_grad * gate * (chosen - probs) / SHARPNESS
        grad_unit = jnp.dot(grad_logits, table, precision=EXACT, preferred_element_type=F32)
        dembed_ref[...] += mm_rows(grad_logits, low_unit, EXACT)
        grad_low = clipped_back(grad_unit, low, low_scale, low_squares)
        dproj_ref[...] += mm_rows(grad_low, normed, EXACT)
        grad = grad + mm_cols(grad_low, proj, EXACT)
        small_ref[0:1, :] += jnp.sum(grad * unit, 0, keepdims=True)
        small_ref[1:2, :] += jnp.sum(grad, 0, keepdims=True)
        grad_hidden = cot_ref[at, :].astype(F32) + norm_back(grad, gain_ref[...], unit, scale)
        grad_hidden_ref[at, :] = grad_hidden
        low_grad = grad_hidden.astype(BF16)
        low_ref[at, :] = low_grad
        grad_mixed = mm_cols(low_grad, wo_ref[...]).astype(BF16)
        grad_mixed_ref[at, :] = grad_mixed
        products = grad_mixed.astype(F32) * mixed_ref[at, :].astype(F32)
        lines = mm_cols(head_lines, products, EXACT)
        for p in range(pairs):
            delta_ref[p, :, at] = lines[8 * p : 8 * p + 8, :]
        return carry

    lax.fori_loop(0, tokens // rows, row_block, 0)
    embed = embed_ref[...]
    squares = jnp.sum(embed * embed, -1, keepdims=True)
    table_scale = lax.rsqrt(jnp.maximum(squares, 1.0))
    dembed = clipped_back(dembed_ref[...], embed, table_scale, squares)
    lines_proj = small_ref.shape[0] - 8 - max(8, experts)
    small_ref[8 : 8 + lines_proj, :] = dproj_ref[0:lines_proj, :]
    small_ref[8 + lines_proj :, 0:128] = dembed[0 : max(8, experts), :]
    store_tiles(dwo_ref, mm_rows(mixed_ref[...], low_ref[...]))


def middle_back(
    back, gate_grads, hidden, cot, mixed, wo, gain, bias, proj, embed, route, place, space,
    experts, cap,
):
    tokens, width = hidden.shape
    slots = experts * cap
    back = back.reshape(slots, width)
    args = (back, gate_grads, hidden, cot, mixed, wo, gain, bias, proj, embed, route, place)
    return pl.pallas_call(
        functools.partial(middle_back_kernel, experts, cap),
        out_shape=[
            jax.ShapeDtypeStruct((tokens, width), F32),
            jax.ShapeDtypeStruct((tokens, width), BF16),
            jax.ShapeDtypeStruct((width // PAIR, 8, tokens), F32),
            jax.ShapeDtypeStruct((width // 128, width, 128), BF16),
            jax.ShapeDtypeStruct((8 + space + max(8, experts), width), F32),
        ],
        scratch_shapes=[
            pltpu.VMEM((tokens, 128), jnp.int32),
            pltpu.VMEM((tokens, width), BF16),
            pltpu.VMEM((128, width), F32),
            pltpu.VMEM((128, 128), F32),
        ],
        compiler_params=params(),
        cost_estimate=cost(2 * tokens * width * (2 * width + slots), 20 * tokens * width),
        name="middle_back",
    )(*args)


def qkv_back_kernel(
    x_ref, gain_ref, bias_ref, grad_hidden_ref, dq_ref, dk_ref, dv_ref, wq_ref, wk_ref, wv_ref,
    grad_ref, dwq_ref, dwk_ref, dwv_ref, small_ref, low_ref,
):
    tokens, width = x_ref.shape
    rows = 256
    small_ref[...] = jnp.zeros_like(small_ref)

    def row_block(i, carry):
        at = pl.ds(pl.multiple_of(i * rows, rows), rows)
        unit, scale = norm_parts(x_ref[at, :].astype(F32))
        low_ref[at, :] = (unit * gain_ref[...] + bias_ref[...]).astype(BF16)
        grad = (
            mm_cols(dq_ref[at, :], wq_ref[...])
            + mm_cols(dk_ref[at, :], wk_ref[...])
            + mm_cols(dv_ref[at, :], wv_ref[...])
        )
        small_ref[0:1, :] += jnp.sum(grad * unit, 0, keepdims=True)
        small_ref[1:2, :] += jnp.sum(grad, 0, keepdims=True)
        grad_ref[at, :] = grad_hidden_ref[at, :] + norm_back(grad, gain_ref[...], unit, scale)
        return carry

    lax.fori_loop(0, tokens // rows, row_block, 0)
    low = low_ref[...]
    store_tiles(dwq_ref, mm_rows(low, dq_ref[...]))
    store_tiles(dwk_ref, mm_rows(low, dk_ref[...]))
    store_tiles(dwv_ref, mm_rows(low, dv_ref[...]))


def qkv_back(x, gain, bias, grad_hidden, dq, dk, dv, wq, wk, wv):
    tokens, width = x.shape
    square = jax.ShapeDtypeStruct((width // 128, width, 128), BF16)
    return pl.pallas_call(
        qkv_back_kernel,
        out_shape=[
            jax.ShapeDtypeStruct((tokens, width), F32),
            square,
            square,
            square,
            jax.ShapeDtypeStruct((8, width), F32),
        ],
        scratch_shapes=[pltpu.VMEM((tokens, width), BF16)],
        compiler_params=params(),
        cost_estimate=cost(12 * tokens * width * width, 20 * tokens * width),
        name="qkv_back",
    )(x, gain, bias, grad_hidden, dq, dk, dv, wq, wk, wv)


def add_rows(rows, out_ref, out_at, terms):
    step = 48

    def body(i, carry):
        at = i * step
        total = None
        for ref, start in terms:
            value = ref[pl.ds(pl.multiple_of(start + at, 16), step), :].astype(F32)
            total = value if total is None else total + value
        out_ref[pl.ds(pl.multiple_of(out_at + at, 16), step), :] = total.astype(out_ref.dtype)
        return carry

    lax.fori_loop(0, rows // step, body, 0)


def reduce_kernel(x_axis, experts, n, *refs):
    grads = refs[:n]
    small_ref = refs[n]
    out_ref, small_out = refs[n + 1 : n + 3]
    (
        core_got, core_sum, plane_got, plane_sum, line_got,
        small_got, core_send, core_recv, plane_send, plane_recv, line_send, line_recv,
        line_back_send, line_back_recv, plane_back_send, plane_back_recv,
        core_back_send, core_back_recv, small_send, small_recv,
    ) = refs[n + 3 :]
    dp = lax.axis_index("dp")
    me = lax.axis_index("expert")
    core = lax.rem(dp, 2)
    x_at = dp // 2
    low = lax.rem(me, 2)
    high = me // 2
    planes, lines = 2 * x_axis, experts // 2
    mesh_ids = pl.DeviceIdType.MESH
    rows = grads[0].shape[0]
    half = rows // 2
    quarter = half // planes
    piece = quarter // lines
    plane_at = x_at * 2 + low

    other_core = {"dp": dp + 1 - 2 * core}

    def plane_peer(j):
        at = lax.rem(plane_at + j, planes)
        return at, (2 * (at // 2) + core, 2 * high + lax.rem(at, 2))

    def line_peer(j):
        at = lax.rem(high + j, lines)
        return at, {"expert": 2 * at + low}

    barrier = pltpu.get_barrier_semaphore()
    pl.semaphore_signal(barrier, inc=1, device_id=other_core, device_id_type=mesh_ids)
    for j in range(1, planes):
        pl.semaphore_signal(barrier, inc=1, device_id=plane_peer(j)[1], device_id_type=mesh_ids)
    for j in range(1, lines):
        pl.semaphore_signal(barrier, inc=1, device_id=line_peer(j)[1], device_id_type=mesh_ids)
    pl.semaphore_wait(barrier, planes + lines - 1)

    def remote(src, dst, send, recv, to):
        return pltpu.make_async_remote_copy(src, dst, send, recv, to, mesh_ids)

    def rows_at(start, size):
        return pl.ds(pl.multiple_of(start, 16), size)

    def core_copy(c):
        src = grads[c].at[rows_at((1 - core) * half, half)]
        return [remote(src, core_got.at[c], core_send.at[c], core_recv.at[c], other_core)]

    def plane_copies(c):
        made = []
        for j in range(1, planes):
            at, to = plane_peer(j)
            src = core_sum.at[c, rows_at(at * quarter, quarter)]
            made.append(
                remote(src, plane_got.at[c, j], plane_send.at[c, j], plane_recv.at[c, j], to)
            )
        return made

    def line_copies(c):
        made = []
        for j in range(1, lines):
            at, to = line_peer(j)
            src = plane_sum.at[c, rows_at(at * piece, piece)]
            made.append(remote(src, line_got.at[c, j], line_send.at[c, j], line_recv.at[c, j], to))
        return made

    base = core * half + plane_at * quarter

    def line_back(c):
        at = rows_at(base + high * piece, piece)
        made = []
        for j in range(1, lines):
            to = line_peer(j)[1]
            made.append(
                remote(
                    out_ref.at[c, at],
                    out_ref.at[c, at],
                    line_back_send.at[c, j],
                    line_back_recv.at[c, j],
                    to,
                )
            )
        return made

    def plane_back(c):
        at = rows_at(base, quarter)
        made = []
        for j in range(1, planes):
            to = plane_peer(j)[1]
            made.append(
                remote(
                    out_ref.at[c, at],
                    out_ref.at[c, at],
                    plane_back_send.at[c, j],
                    plane_back_recv.at[c, j],
                    to,
                )
            )
        return made

    def core_back(c):
        at = rows_at(core * half, half)
        return [
            remote(
                out_ref.at[c, at],
                out_ref.at[c, at],
                core_back_send.at[c],
                core_back_recv.at[c],
                other_core,
            )
        ]

    def small_copies(stage):
        made = []
        if stage == 0:
            made.append(
                remote(
                    small_got.at[0, 0],
                    small_got.at[0, 1],
                    small_send.at[0, 1],
                    small_recv.at[0, 1],
                    other_core,
                )
            )
        else:
            for j in range(1, planes if stage == 1 else lines):
                to = plane_peer(j)[1] if stage == 1 else line_peer(j)[1]
                made.append(
                    remote(
                        small_got.at[stage, 0],
                        small_got.at[stage, j],
                        small_send.at[stage, j],
                        small_recv.at[stage, j],
                        to,
                    )
                )
        return made

    def start(copies):
        for copy in copies:
            copy.start()

    def received(copies):
        for copy in copies:
            copy.wait_recv()

    def ordered(got, at, count):
        total = None
        for i in range(count):
            value = got(lax.rem(at + count - i, count))
            total = value if total is None else total + value
        return total

    def stage_run(stage, c):
        if stage == 0:
            start(core_copy(c))
        elif stage == 1:
            received(core_copy(c))
            add_rows(
                half, core_sum.at[c], 0, [(grads[c], core * half), (core_got.at[c], 0)]
            )
            start(plane_copies(c))
        elif stage == 2:
            received(plane_copies(c))
            add_rows(
                quarter,
                plane_sum.at[c],
                0,
                [(core_sum.at[c], plane_at * quarter)]
                + [(plane_got.at[c, j], 0) for j in range(1, planes)],
            )
            start(line_copies(c))
        elif stage == 3:
            received(line_copies(c))
            add_rows(
                piece,
                out_ref.at[c],
                base + high * piece,
                [(plane_sum.at[c], high * piece)]
                + [(line_got.at[c, j], 0) for j in range(1, lines)],
            )
            start(line_back(c))
        elif stage == 4:
            received(line_back(c))
            start(plane_back(c))
        elif stage == 5:
            received(plane_back(c))
            start(core_back(c))
        else:
            received(core_back(c))

    def small_run(stage):
        if stage == 0:
            small_got[0, 0] = small_ref[...]
            start(small_copies(0))
        elif stage == 1:
            received(small_copies(0))
            small_got[1, 0] = small_got[0, 0] + small_got[0, 1]
            start(small_copies(1))
        elif stage == 2:
            received(small_copies(1))
            small_got[2, 0] = ordered(lambda j: small_got[1, j], plane_at, planes)
            start(small_copies(2))
        elif stage == 3:
            received(small_copies(2))
            small_out[...] = ordered(lambda j: small_got[2, j], high, lines)

    for tick in range(n + 6):
        for stage in reversed(range(7)):
            c = tick - stage
            if 0 <= c < n:
                stage_run(stage, c)
        if tick < 4:
            small_run(tick)
    for stage in range(3):
        for copy in small_copies(stage):
            copy.wait_send()
    for c in range(n):
        for made in (core_copy, plane_copies, line_copies, line_back, plane_back, core_back):
            for copy in made(c):
                copy.wait_send()


def reduce_all(grads, small, dp_size, experts):
    n = len(grads)
    tiles, width, _ = grads[0].shape
    rows = tiles * width
    x_axis, lines, planes = dp_size // 2, experts // 2, dp_size
    if rows % (48 * dp_size * experts):
        out, small = lax.psum((jnp.stack(grads).astype(F32), small), ("dp", "expert"))
        return out.astype(BF16), small
    half = rows // 2
    quarter = half // planes
    piece = quarter // lines
    most = max(planes, lines)
    sems = pltpu.SemaphoreType.DMA
    out, small = pl.pallas_call(
        functools.partial(reduce_kernel, x_axis, experts, n),
        in_specs=[pl.BlockSpec(memory_space=pltpu.VMEM)] * (n + 1),
        out_specs=[pl.BlockSpec(memory_space=pltpu.VMEM)] * 2,
        out_shape=[
            jax.ShapeDtypeStruct((n, rows, 128), BF16),
            jax.ShapeDtypeStruct(small.shape, F32),
        ],
        scratch_shapes=[
            pltpu.VMEM((n, half, 128), BF16),
            pltpu.VMEM((n, half, 128), BF16),
            pltpu.VMEM((n, planes, quarter, 128), BF16),
            pltpu.VMEM((n, quarter, 128), BF16),
            pltpu.VMEM((n, lines, piece, 128), BF16),
            pltpu.VMEM((3, most, *small.shape), F32),
        ]
        + [sems((n,))] * 2
        + [sems((n, planes))] * 2
        + [sems((n, lines))] * 4
        + [sems((n, planes))] * 2
        + [sems((n,))] * 2
        + [sems((3, most))] * 2,
        compiler_params=pltpu.CompilerParams(
            vmem_limit_bytes=40 * MIB, collective_id=1, has_side_effects=True
        ),
        cost_estimate=cost(8 * n * rows * 128, 100e6),
        name="reduce_all",
    )(*[g.reshape(rows, 128) for g in grads], small)
    return out.reshape(n, tiles, width, 128), small


def finish_kernel(
    experts, cap, hidden_ref, gate_ref, place_ref, sums_ref, *refs
):
    made_refs = refs[:experts]
    out_ref = refs[experts]
    grad_refs = refs[experts + 1 : experts + 5]
    slot_ref = refs[-1]
    tokens, width = hidden_ref.shape
    rows = 256
    slot_ref[...] = jnp.broadcast_to(slot_col_of(place_ref[...], experts, cap), slot_ref.shape)

    def row_block(i, carry):
        at = pl.ds(pl.multiple_of(i * rows, rows), rows)
        produced = jnp.zeros((rows, width), F32)
        for e in range(experts):
            pick = one_hot(iota((rows, cap), 1) + e * cap == slot_ref[at, 0:1])
            produced = produced + mm(pick, made_refs[e][...])
        out_ref[at, :] = (hidden_ref[at, :] + gate_ref[at, 0:1] * produced).astype(BF16)
        return carry

    lax.fori_loop(0, tokens // rows, row_block, 0)
    for w, ref in enumerate(grad_refs):
        for tile in range(width // 128):
            ref[:, tile * 128 : (tile + 1) * 128] = sums_ref[w, tile].astype(F32)


def finish(made, hidden, gate, place, sums, experts, cap):
    tokens, width = hidden.shape
    return pl.pallas_call(
        functools.partial(finish_kernel, experts, cap),
        out_shape=[jax.ShapeDtypeStruct((tokens, width), BF16)]
        + [jax.ShapeDtypeStruct((width, width), F32)] * 4,
        scratch_shapes=[pltpu.VMEM((tokens, 128), jnp.int32)],
        compiler_params=params(),
        cost_estimate=cost(2 * tokens * width * experts * cap, 10 * tokens * width),
        name="finish",
    )(hidden, gate, place, sums, *made)


def shifted(blocks, axis, size, step=1):
    moved = [blocks[0]]
    for s in range(1, len(blocks)):
        moved.append(
            lax.ppermute(blocks[s], axis, [(i, (i + s * step) % size) for i in range(size)])
        )
    return moved


def on_device(
    tokens,
    segment_ids,
    routes,
    norm1_gain,
    norm1_bias,
    query_weight,
    w_key,
    w_value,
    w_output,
    norm2_gain,
    norm2_bias,
    router_proj,
    expert_embed,
    expert_in,
    expert_out,
    cotangent,
):
    count, width = tokens.shape
    experts = lax.axis_size("expert")
    dp_size = lax.axis_size("dp")
    cap = 2 * count // experts
    longest = segment_ids.shape[1] // 2
    place = lax.rem(routes - lax.axis_index("expert") + experts, experts)
    place_row = place.reshape(1, count)
    seg_col = segment_ids.reshape(count, 1)
    gain1, bias1 = norm1_gain[None], norm1_bias[None]
    gain2, bias2 = norm2_gain[None], norm2_bias[None]
    space = router_proj.shape[1]
    proj = jnp.pad(router_proj, ((0, 0), (0, 128 - space)))
    embed = jnp.pad(expert_embed, ((0, 128 - experts), (0, 128 - space)))

    up = gather_slots(place_row, cotangent, experts, cap)
    tokens, *up = lax.optimization_barrier((tokens, *up))
    up = shifted(up, "expert", experts)
    q, k, v = qkv(tokens, gain1, bias1, query_weight, w_key, w_value)
    mixed, probs = attention(q, k, v, seg_col, longest)
    hidden, gate, slots, gates = middle(
        mixed, tokens, w_output, gain2, bias2, proj, embed, routes, place_row, experts, cap
    )
    back, gate_grads, made, din, dout = expert(
        slots, gates, up, expert_in[0], expert_out[0], dp_size
    )
    din = shifted(din, "dp", dp_size, 2)
    dout = shifted(dout, "dp", dp_size, 2)
    made = [made[0]] + [
        lax.ppermute(made[s], "expert", [(i, (i - s) % experts) for i in range(experts)])
        for s in range(1, experts)
    ]
    grad_hidden, grad_mixed, delta, dwo, small2 = middle_back(
        back, gate_grads, hidden, cotangent, mixed, w_output, gain2, bias2,
        proj, embed, routes, place, space, experts, cap,
    )
    dq, dk, dv = attention_back(q, k, v, grad_mixed, probs, delta, longest)
    grad_input, dwq, dwk, dwv, small1 = qkv_back(
        tokens, gain1, bias1, grad_hidden, dq, dk, dv, query_weight, w_key, w_value
    )
    sums, small = reduce_all(
        [dwo, dwq, dwk, dwv], jnp.concatenate([small1, small2], 0), dp_size, experts
    )
    output, dwo, dwq, dwk, dwv = finish(made, hidden, gate, place, sums, experts, cap)
    grad_in = sum(block.astype(F32) for block in din)
    grad_out = sum(block.astype(F32) for block in dout)
    return (
        output,
        grad_input,
        small[0],
        small[1],
        dwq,
        dwk,
        dwv,
        dwo,
        small[8],
        small[9],
        small[16 : 16 + space].T,
        small[16 + space : 16 + space + experts, :space],
        grad_in[None],
        grad_out[None],
    )


def solution(mesh):
    split = P(("dp", "expert"), None)
    in_specs = (
        (split,) * 3 + (P(),) * 10 + (P("expert", None, None), P("expert", None, None), split)
    )
    out_specs = (
        (split, split) + (P(),) * 10 + (P("expert", None, "dp"), P("expert", "dp", None))
    )
    return jax.shard_map(
        on_device, mesh=mesh, in_specs=in_specs, out_specs=out_specs, check_vma=False
    )
```

```python
import functools

import jax
import jax.numpy as jnp
from jax import lax
from jax.experimental import pallas as pl
from jax.experimental.pallas import tpu as pltpu
from jax.sharding import PartitionSpec as P

HEAD_DIM = 64
PAIR = 2 * HEAD_DIM
SHARPNESS = 0.25
EXACT = lax.Precision.HIGHEST
BF16 = jnp.bfloat16
F32 = jnp.float32
FAR = -1e30
MIB = 1 << 20


def mm(left, right):
    return jnp.dot(left, right, preferred_element_type=F32)


def mm_rows(left, right, precision=None):
    return lax.dot_general(
        left, right, (((0,), (0,)), ((), ())), precision=precision, preferred_element_type=F32
    )


def mm_cols(left, right, precision=None):
    return lax.dot_general(
        left, right, (((1,), (1,)), ((), ())), precision=precision, preferred_element_type=F32
    )


def iota(shape, axis):
    return lax.broadcasted_iota(jnp.int32, shape, axis)


def one_hot(condition):
    return jnp.where(condition, 1.0, 0.0).astype(BF16)


def params(limit=56):
    return pltpu.CompilerParams(vmem_limit_bytes=limit * MIB)


def cost(flops, moved, trans=0):
    return pl.CostEstimate(flops=int(flops), bytes_accessed=int(moved), transcendentals=int(trans))


def spec_all(shape):
    zeros = (0,) * len(shape)
    return pl.BlockSpec(shape, lambda *ids: zeros)


def slot_row_of(route_row, experts, cap):
    tokens = route_row.shape[1]
    padded = max(8, experts)
    hits = one_hot(iota((padded, tokens), 0) == route_row)
    earlier = one_hot(iota((tokens, tokens), 0) < iota((tokens, tokens), 1))
    ranks = mm(hits, earlier)
    rank = jnp.sum(ranks * hits.astype(F32), 0, keepdims=True)
    return route_row * cap + rank.astype(jnp.int32)


def slot_col_of(route_col, experts, cap):
    tokens = route_col.shape[0]
    hits = one_hot(iota((tokens, 128), 1) == route_col)
    earlier = one_hot(iota((tokens, tokens), 1) < iota((tokens, tokens), 0))
    ranks = mm(earlier, hits)
    rank = jnp.sum(ranks * hits.astype(F32), 1, keepdims=True)
    return route_col * cap + rank.astype(jnp.int32)


def as_row(col):
    rows = col.shape[0]
    eye = iota((rows, rows), 0) == iota((rows, rows), 1)
    return jnp.sum(jnp.where(eye, col, 0.0), 0, keepdims=True)


def as_col(row):
    rows = row.shape[1]
    eye = iota((rows, rows), 0) == iota((rows, rows), 1)
    return jnp.sum(jnp.where(eye, row, 0.0), 1, keepdims=True)


def gather_kernel(experts, cap, route_ref, x_ref, *out_refs):
    slot = slot_row_of(route_ref[...], experts, cap)
    tokens = x_ref.shape[0]
    for e, out_ref in enumerate(out_refs):
        pick = one_hot(iota((cap, tokens), 0) + e * cap == slot)
        out_ref[...] = mm(pick, x_ref[...]).astype(BF16)


def gather_slots(route_row, x, experts, cap):
    tokens, width = x.shape
    slots = experts * cap
    return pl.pallas_call(
        functools.partial(gather_kernel, experts, cap),
        out_shape=[jax.ShapeDtypeStruct((cap, width), BF16)] * experts,
        compiler_params=params(32),
        cost_estimate=cost(2 * slots * tokens * width, 2 * width * (tokens + slots)),
        name="gather_slots",
    )(route_row, x)


def norm_parts(values):
    average = jnp.mean(values, -1, keepdims=True)
    centred = values - average
    spread = jnp.mean(centred * centred, -1, keepdims=True)
    scale = lax.rsqrt(spread + 1e-05)
    return centred * scale, scale


def norm_back(grad, gain, unit, scale):
    grad_unit = grad * gain
    inner = jnp.mean(grad_unit * unit, -1, keepdims=True)
    return scale * (grad_unit - jnp.mean(grad_unit, -1, keepdims=True) - unit * inner)


def qkv_kernel(x_ref, gain_ref, bias_ref, wq_ref, wk_ref, wv_ref, q_ref, k_ref, v_ref):
    unit, _ = norm_parts(x_ref[...].astype(F32))
    normed = (unit * gain_ref[...] + bias_ref[...]).astype(BF16)
    for w_ref, o_ref in ((wq_ref, q_ref), (wk_ref, k_ref), (wv_ref, v_ref)):
        o_ref[...] = mm(normed, w_ref[...]).astype(BF16)


def qkv(x, gain, bias, wq, wk, wv):
    tokens, width = x.shape
    rows = 256
    block = pl.BlockSpec((rows, width), lambda i: (i, 0))
    made = jax.ShapeDtypeStruct((tokens, width), BF16)
    return pl.pallas_call(
        qkv_kernel,
        grid=(tokens // rows,),
        in_specs=[block, spec_all((1, width)), spec_all((1, width))]
        + [spec_all((width, width))] * 3,
        out_specs=[block] * 3,
        out_shape=[made] * 3,
        compiler_params=params(32),
        cost_estimate=cost(6 * tokens * width * width, 2 * (4 * tokens * width + 3 * width * width)),
        name="qkv",
    )(x, gain, bias, wq, wk, wv)


def key_window(block, rows, tokens, longest):
    first = max(0, (block * rows - longest + 1) // 128 * 128)
    last = min(tokens, -(-(block * rows + rows - 1 + longest) // 128) * 128)
    return first, last


def attention_kernel(rows, longest, q_ref, k_ref, v_ref, seg_ref, mixed_ref, prob_ref):
    tokens = q_ref.shape[0]
    lane = iota((tokens, PAIR), 1)
    own = (lane < HEAD_DIM, lane >= HEAD_DIM)
    seg = seg_ref[...]
    queries = q_ref[...] * jnp.asarray(HEAD_DIM**-0.5, BF16)
    keys = k_ref[...]
    for h in range(2):
        other = (1 - h) * HEAD_DIM
        q_tag = jnp.where(lane - other == seg, 1.0, 0.0).astype(BF16)
        k_tag = jnp.where(lane - other == seg, 0.0, FAR)
        k_tag = jnp.where((lane >= other) & (lane < other + 8), k_tag, 0.0).astype(BF16)
        q_h = jnp.where(own[h], queries, q_tag)
        k_h = jnp.where(own[h], keys, k_tag)
        for block in range(tokens // rows):
            first, last = key_window(block, rows, tokens, longest)
            mine = slice(block * rows, (block + 1) * rows)
            scores = mm_cols(k_h[first:last], q_h[mine])
            largest = jnp.max(scores, 0, keepdims=True)
            weights = jnp.exp(scores - largest)
            total = jnp.sum(weights, 0, keepdims=True)
            probs = (weights * (1.0 / total)).astype(BF16)
            prob_ref[h, first:last, mine] = probs
            out = mm_rows(probs, v_ref[first:last, :]).astype(BF16)
            if h == 0:
                mixed_ref[mine, :] = out
            else:
                mixed_ref[mine, :] = jnp.where(own[1][mine], out, mixed_ref[mine, :])


def attention(q, k, v, seg_col, longest):
    tokens, width = q.shape
    pairs = width // PAIR
    rows = 256
    block = pl.BlockSpec((tokens, PAIR), lambda p: (0, p))
    return pl.pallas_call(
        functools.partial(attention_kernel, rows, longest),
        grid=(pairs,),
        in_specs=[block, block, block, spec_all((tokens, 1))],
        out_specs=[block, pl.BlockSpec((2, tokens, tokens), lambda p: (p, 0, 0))],
        out_shape=[
            jax.ShapeDtypeStruct((tokens, width), BF16),
            jax.ShapeDtypeStruct((2 * pairs, tokens, tokens), BF16),
        ],
        compiler_params=params(),
        cost_estimate=cost(
            4 * 2 * pairs * tokens * tokens * 256, 4 * pairs * tokens * tokens, tokens * tokens
        ),
        name="attention",
    )(q, k, v, seg_col)


def attention_back_kernel(
    rows, longest, q_ref, k_ref, v_ref, do_ref, prob_ref, delta_ref,
    dq_ref, dk_ref, dv_ref, dk_sum, dv_sum,
):
    tokens = q_ref.shape[0]
    lane = iota((tokens, PAIR), 1)
    own = (lane < HEAD_DIM, lane >= HEAD_DIM)
    zero = jnp.zeros((), BF16)
    scale = HEAD_DIM**-0.5
    dk_sum[...] = jnp.zeros_like(dk_sum)
    dv_sum[...] = jnp.zeros_like(dv_sum)
    for block in range(tokens // rows):
        first, last = key_window(block, rows, tokens, longest)
        mine = slice(block * rows, (block + 1) * rows)
        values = v_ref[first:last, :]
        dq = jnp.zeros((rows, PAIR), F32)
        dk = jnp.zeros((last - first, PAIR), F32)
        dv = jnp.zeros((last - first, PAIR), F32)
        for h in range(2):
            do_h = jnp.where(own[h][mine], do_ref[mine, :], zero)
            q_h = jnp.where(own[h][mine], q_ref[mine, :], zero)
            k_h = jnp.where(own[h][first:last], k_ref[first:last, :], zero)
            probs = prob_ref[h, first:last, mine]
            grad_probs = mm_cols(values, do_h)
            grad_scores = (
                probs.astype(F32) * (grad_probs - delta_ref[0, h : h + 1, mine])
            ).astype(BF16)
            dq = dq + mm_rows(grad_scores, k_h)
            dk = dk + mm(grad_scores, q_h)
            dv = dv + mm(probs, do_h)
        dq_ref[mine, :] = (dq * scale).astype(BF16)
        dk_sum[first:last, :] += dk
        dv_sum[first:last, :] += dv
    dk_ref[...] = (dk_sum[...] * scale).astype(BF16)
    dv_ref[...] = dv_sum[...].astype(BF16)


def attention_back(q, k, v, grad_mixed, probs, delta, longest):
    tokens, width = q.shape
    pairs = width // PAIR
    rows = 256
    block = pl.BlockSpec((tokens, PAIR), lambda p: (0, p))
    made = jax.ShapeDtypeStruct((tokens, width), BF16)
    return pl.pallas_call(
        functools.partial(attention_back_kernel, rows, longest),
        grid=(pairs,),
        in_specs=[block] * 4
        + [
            pl.BlockSpec((2, tokens, tokens), lambda p: (p, 0, 0)),
            pl.BlockSpec((1, 8, tokens), lambda p: (p, 0, 0)),
        ],
        out_specs=[block] * 3,
        out_shape=[made] * 3,
        scratch_shapes=[pltpu.VMEM((tokens, PAIR), F32)] * 2,
        compiler_params=params(),
        cost_estimate=cost(8 * 2 * pairs * tokens * tokens * 256, 4 * pairs * tokens * tokens),
        name="attention_back",
    )(q, k, v, grad_mixed, probs, delta)


def router_parts(normed, proj, embed, route, experts):
    low = jnp.dot(normed, proj, precision=EXACT, preferred_element_type=F32)
    low_squares = jnp.sum(low * low, -1, keepdims=True)
    low_scale = lax.rsqrt(jnp.maximum(low_squares, 1.0))
    low_unit = low * low_scale
    squares = jnp.sum(embed * embed, -1, keepdims=True)
    table_scale = lax.rsqrt(jnp.maximum(squares, 1.0))
    table = embed * table_scale
    logits = mm_cols(low_unit, table, EXACT) / SHARPNESS
    lane = iota(logits.shape, 1)
    logits = jnp.where(lane < experts, logits, FAR)
    weights = jnp.exp(logits - jnp.max(logits, -1, keepdims=True))
    probs = weights / jnp.sum(weights, -1, keepdims=True)
    chosen = jnp.where(lane == route, 1.0, 0.0)
    gate = jnp.sum(probs * chosen, -1, keepdims=True)
    return gate, probs, chosen, low, low_squares, low_scale, low_unit, squares, table_scale, table


def clipped_back(grad_unit, raw, scale, squares):
    share = jnp.where(squares > 1.0, 1.0, jnp.where(squares == 1.0, 0.5, 0.0))
    inner = jnp.sum(grad_unit * raw, -1, keepdims=True)
    return scale * grad_unit - share * scale * scale * scale * inner * raw


def middle_kernel(
    experts, cap, mixed_ref, x_ref, wo_ref, gain_ref, bias_ref, proj_ref, embed_ref,
    route_ref, place_row_ref, hidden_ref, gate_ref, slots_ref, gates_ref, kept,
):
    tokens, width = x_ref.shape
    rows = 256

    def row_block(i, carry):
        at = pl.ds(pl.multiple_of(i * rows, rows), rows)
        hidden = x_ref[at, :].astype(F32) + mm(mixed_ref[at, :], wo_ref[...])
        hidden_ref[at, :] = hidden
        unit, _ = norm_parts(hidden)
        normed = unit * gain_ref[...] + bias_ref[...]
        gate = router_parts(normed, proj_ref[...], embed_ref[...], route_ref[at, :], experts)[0]
        gate_ref[at, :] = jnp.broadcast_to(gate, (rows, 128))
        high = gate.astype(BF16).astype(F32)
        mid = (gate - high).astype(BF16).astype(F32)
        rest = gate - high - mid
        lane = iota((rows, 128), 1)
        split = jnp.where(lane == 0, high, jnp.where(lane == 1, mid, jnp.where(lane == 2, rest, 0.0)))
        kept[at, 0:width] = normed.astype(BF16)
        kept[at, width : width + 128] = split.astype(BF16)
        return carry

    lax.fori_loop(0, tokens // rows, row_block, 0)
    slot = slot_row_of(place_row_ref[...], experts, cap)

    def slot_block(e, carry):
        pick = one_hot(iota((cap, tokens), 0) + e * cap == slot)
        got = mm(pick, kept[...])
        slots_ref[e] = got[:, 0:width].astype(BF16)
        gates = as_row(jnp.sum(got[:, width : width + 128], 1, keepdims=True))
        gates_ref[e] = jnp.broadcast_to(gates, (8, cap))
        return carry

    lax.fori_loop(0, experts, slot_block, 0)


def middle(mixed, x, wo, gain, bias, proj, embed, route, place_row, experts, cap):
    tokens, width = x.shape
    slots = experts * cap
    args = (mixed, x, wo, gain, bias, proj, embed, route, place_row)
    return pl.pallas_call(
        functools.partial(middle_kernel, experts, cap),
        out_shape=[
            jax.ShapeDtypeStruct((tokens, width), F32),
            jax.ShapeDtypeStruct((tokens, 128), F32),
            jax.ShapeDtypeStruct((experts, cap, width), BF16),
            jax.ShapeDtypeStruct((experts, 8, cap), F32),
        ],
        scratch_shapes=[pltpu.VMEM((tokens, width + 128), BF16)],
        compiler_params=params(),
        cost_estimate=cost(2 * tokens * width * (width + slots), 16 * tokens * width),
        name="middle",
    )(*args)


def gelu_parts(pre):
    size = jnp.abs(pre)
    t = pl.reciprocal(1.0 + 0.23164189298 * size, approx=False)
    bell = jnp.exp(-0.5 * pre * pre)
    tail = t * (
        0.127414796
        + t * (-0.142248368 + t * (0.7107068705 + t * (-0.7265760135 + t * 0.5307027145)))
    )
    tail = tail * bell
    phi_sum = jnp.where(pre >= 0, 1.0 - tail, tail)
    return phi_sum, pre * bell * 0.3989422804014327


def expert_kernel(experts, x_axis, *refs):
    x_ref, gates_ref, w_in_ref, w_out_ref = refs[:4]
    up_refs = refs[4 : 4 + experts]
    back_ref, gate_grads_ref = refs[4 + experts : 6 + experts]
    rest = refs[6 + experts :]
    made_ref = rest[0]
    din_refs = rest[1 : 1 + x_axis]
    dout_refs = rest[1 + x_axis : 1 + 2 * x_axis]
    (
        x_here, up_here, gates_here, back_here, gate_grads_here, made_here,
        active, grad_pre, w_in, w_out, din_got, dout_got,
        load_sem, x_send, x_recv, g_send, g_recv, b_send, b_recv, gg_send, gg_recv,
        d_send, d_recv, store_sem,
    ) = rest[1 + 2 * x_axis :]
    cap, width = x_here.shape[1:]
    hidden = w_in.shape[1]
    me = lax.axis_index("expert")
    dp = lax.axis_index("dp")
    core = lax.rem(dp, 2)
    mesh_ids = pl.DeviceIdType.MESH

    barrier = pltpu.get_barrier_semaphore()

    def greet(s, carry):
        pl.semaphore_signal(
            barrier, inc=1, device_id={"expert": lax.rem(me + s, experts)}, device_id_type=mesh_ids
        )
        return carry

    lax.fori_loop(1, experts, greet, 0)
    pl.semaphore_signal(
        barrier, inc=1, device_id={"dp": dp + 1 - 2 * core}, device_id_type=mesh_ids
    )
    pl.semaphore_wait(barrier, experts)

    def out_copy(s):
        to = {"expert": lax.rem(me + s, experts)}
        return (
            pltpu.make_async_remote_copy(
                x_ref.at[s], x_here.at[s], x_send.at[s], x_recv.at[s], to, mesh_ids
            ),
            pltpu.make_async_remote_copy(
                gates_ref.at[s], gates_here.at[s], g_send.at[s], g_recv.at[s], to, mesh_ids
            ),
        )

    def home_copy(s):
        to = {"expert": lax.rem(me + experts - s, experts)}
        return (
            pltpu.make_async_remote_copy(
                back_here.at[s], back_ref.at[s], b_send.at[s], b_recv.at[s], to, mesh_ids
            ),
            pltpu.make_async_remote_copy(
                gate_grads_here.at[s], gate_grads_ref.at[s], gg_send.at[s], gg_recv.at[s], to, mesh_ids
            ),
        )

    def send_out(s, carry):
        for copy in out_copy(s):
            copy.start()
        return carry

    lax.fori_loop(1, experts, send_out, 0)
    loads = [
        pltpu.make_async_copy(x_ref.at[0], x_here.at[0], load_sem.at[0]),
        pltpu.make_async_copy(gates_ref.at[0], gates_here.at[0], load_sem.at[1]),
        pltpu.make_async_copy(w_in_ref, w_in, load_sem.at[2]),
        pltpu.make_async_copy(w_out_ref, w_out, load_sem.at[3]),
    ]
    for s, up_ref in enumerate(up_refs):
        loads.append(pltpu.make_async_copy(up_ref, up_here.at[s], load_sem.at[4 + s]))
    for load in loads:
        load.start()
    for load in loads:
        load.wait()

    step = 512

    def chunk(s, carry):
        @pl.when(s > 0)
        def _():
            for copy in out_copy(s):
                copy.wait_recv()

        at_rows = pl.ds(pl.multiple_of(s * cap, cap), cap)
        gate = as_col(gates_here[s][0:1, :])
        up = up_here[s].astype(F32)
        scaled = (up * gate).astype(BF16)
        x = x_here[s]
        for at in range(0, hidden, step):
            part = slice(at, at + step)
            pre = mm(x, w_in[:, part])
            grad_active = mm_cols(scaled, w_out[part, :])
            phi_sum, slope = gelu_parts(pre)
            active[at_rows, part] = (pre * phi_sum).astype(BF16)
            grad_pre[at_rows, part] = (grad_active * (phi_sum + slope)).astype(BF16)
        made = mm(active[at_rows, :], w_out[...]).astype(BF16)
        made_here[s] = made
        gate_grad = jnp.sum(up * made.astype(F32), 1, keepdims=True)
        gate_grads_here[s] = jnp.broadcast_to(as_row(gate_grad), (8, cap))
        up_here[s] = scaled
        back_here[s] = mm_cols(grad_pre[at_rows, :], w_in[...]).astype(BF16)

        @pl.when(s > 0)
        def _():
            for copy in home_copy(s):
                copy.start()

        return carry

    lax.fori_loop(0, experts, chunk, 0)
    stores = [
        pltpu.make_async_copy(back_here.at[0], back_ref.at[0], store_sem.at[0]),
        pltpu.make_async_copy(gate_grads_here.at[0], gate_grads_ref.at[0], store_sem.at[1]),
    ]
    for s in range(experts):
        home = lax.rem(me + experts - s, experts)
        stores.append(
            pltpu.make_async_copy(made_here.at[s], made_ref.at[home], store_sem.at[2 + s])
        )
    for store in stores:
        store.start()

    block = hidden // (2 * x_axis)
    slots = experts * cap
    other = {"dp": dp + 1 - 2 * core}
    x_all = x_here.reshape(slots, width)
    up_all = up_here.reshape(slots, width)

    def block_start(k, for_core):
        x_at = lax.rem(dp // 2 + k, x_axis)
        return pl.multiple_of((2 * x_at + for_core) * block, 128)

    def din_out(k):
        return w_in.at[:, k * block : (k + 1) * block]

    def dout_out(k):
        return w_out.at[k * block : (k + 1) * block]

    def core_copies(k):
        return (
            pltpu.make_async_remote_copy(
                din_out(k), din_got.at[k], d_send.at[k], d_recv.at[k], other, mesh_ids
            ),
            pltpu.make_async_remote_copy(
                dout_out(k),
                dout_got.at[k],
                d_send.at[x_axis + k],
                d_recv.at[x_axis + k],
                other,
                mesh_ids,
            ),
        )

    tile = 256 if block % 256 == 0 else 128

    def weight_grads(k, for_core, out, got):
        start = block_start(k, for_core)
        columns = slice(out * block, (out + 1) * block)
        for at in range(0, width, tile):
            part = slice(at, at + tile)
            value = mm_rows(x_all[:, part], grad_pre[:, pl.ds(start, block)])
            if got is not None:
                value = value + din_got[got, part, :].astype(F32)
            w_in[part, columns] = value.astype(BF16)
        for at in range(0, block, tile):
            value = mm_rows(active[:, pl.ds(pl.multiple_of(start + at, 128), tile)], up_all[...])
            if got is not None:
                value = value + dout_got[got, at : at + tile, :].astype(F32)
            w_out[out * block + at : out * block + at + tile, :] = value.astype(BF16)

    for k in range(x_axis):
        weight_grads(k, 1 - core, k, None)
        for copy in core_copies(k):
            copy.start()
    for k in range(x_axis):
        for copy in core_copies(k):
            copy.wait_recv()
        weight_grads(k, core, x_axis + k, k)
        for i, (src, ref) in enumerate(
            ((din_out(x_axis + k), din_refs[k]), (dout_out(x_axis + k), dout_refs[k]))
        ):
            store = pltpu.make_async_copy(src, ref, store_sem.at[2 + experts + 2 * k + i])
            store.start()
            stores.append(store)
    for store in stores:
        store.wait()
    for k in range(x_axis):
        for copy in core_copies(k):
            copy.wait_send()

    def finish(s, carry):
        for copy in out_copy(s):
            copy.wait_send()
        for copy in home_copy(s):
            copy.wait()
        return carry

    lax.fori_loop(1, experts, finish, 0)


def expert(x, gates, up, w_in, w_out, dp_size):
    experts, cap, width = x.shape
    hidden = w_in.shape[1]
    slots = experts * cap
    x_axis = dp_size // 2
    block = hidden // dp_size
    anywhere = pl.BlockSpec(memory_space=pl.ANY)
    rows = jax.ShapeDtypeStruct((experts, cap, width), BF16)
    out_shape = (
        [rows, jax.ShapeDtypeStruct((experts, 8, cap), F32), rows]
        + [jax.ShapeDtypeStruct((width, block), BF16)] * x_axis
        + [jax.ShapeDtypeStruct((block, width), BF16)] * x_axis
    )
    chunks = pltpu.VMEM((experts, cap, width), BF16)
    lines = pltpu.VMEM((experts, 8, cap), F32)
    sems = pltpu.SemaphoreType.DMA
    out = pl.pallas_call(
        functools.partial(expert_kernel, experts, x_axis),
        in_specs=[anywhere] * (4 + experts),
        out_specs=[anywhere] * len(out_shape),
        out_shape=out_shape,
        scratch_shapes=[
            chunks,
            chunks,
            lines,
            chunks,
            lines,
            chunks,
            pltpu.VMEM((slots, hidden), BF16),
            pltpu.VMEM((slots, hidden), BF16),
            pltpu.VMEM((width, hidden), BF16),
            pltpu.VMEM((hidden, width), BF16),
            pltpu.VMEM((x_axis, width, block), BF16),
            pltpu.VMEM((x_axis, block, width), BF16),
            sems((4 + experts,)),
        ]
        + [sems((experts,))] * 8
        + [sems((2 * x_axis,))] * 2
        + [sems((2 + experts + 2 * x_axis,))],
        compiler_params=pltpu.CompilerParams(
            vmem_limit_bytes=63 * MIB, collective_id=0, has_side_effects=True
        ),
        cost_estimate=cost(12 * slots * width * hidden, 8 * width * hidden),
        name="expert",
    )(x, gates, w_in, w_out, *up)
    back, gate_grads, made = out[:3]
    din = out[3 : 3 + x_axis]
    dout = out[3 + x_axis :]
    return back, gate_grads, made, din, dout


def store_tiles(out_ref, value):
    for tile in range(out_ref.shape[0]):
        out_ref[tile] = value[:, tile * 128 : (tile + 1) * 128].astype(BF16)


def middle_back_kernel(
    experts, cap, back_ref, gate_grads_ref, hidden_ref, cot_ref, mixed_ref, wo_ref,
    gain_ref, bias_ref, proj_ref, embed_ref, route_ref, place_ref,
    grad_hidden_ref, grad_mixed_ref, delta_ref, dwo_ref, small_ref,
    slot_ref, low_ref, dproj_ref, dembed_ref,
):
    tokens, width = hidden_ref.shape
    slots = back_ref.shape[0]
    rows = 256
    slot_ref[...] = jnp.broadcast_to(slot_col_of(place_ref[...], experts, cap), slot_ref.shape)
    small_ref[...] = jnp.zeros_like(small_ref)
    dproj_ref[...] = jnp.zeros_like(dproj_ref)
    dembed_ref[...] = jnp.zeros_like(dembed_ref)
    heads = width // HEAD_DIM
    pairs = heads // 2
    head_of = iota((8 * pairs, width), 1) // HEAD_DIM
    line = iota((8 * pairs, width), 0)
    head_lines = jnp.where(head_of == line // 8 * 2 + line % 8, 1.0, 0.0)
    head_lines = jnp.where(line % 8 < 2, head_lines, 0.0)

    def row_block(i, carry):
        at = pl.ds(pl.multiple_of(i * rows, rows), rows)
        place = slot_ref[at, 0:1]
        pick = iota((rows, slots), 1) == place
        grad = mm(one_hot(pick), back_ref[...])
        gate_grad = jnp.zeros((rows, 1), F32)
        for e in range(experts):
            gate_grad = gate_grad + jnp.sum(
                jnp.where(pick[:, e * cap : (e + 1) * cap], gate_grads_ref[e, 0:1, :], 0.0),
                1,
                keepdims=True,
            )
        unit, scale = norm_parts(hidden_ref[at, :])
        normed = unit * gain_ref[...] + bias_ref[...]
        proj = proj_ref[...]
        embed = embed_ref[...]
        gate, probs, chosen, low, low_squares, low_scale, low_unit, _, _, table = router_parts(
            normed, proj, embed, route_ref[at, :], experts
        )
        grad_logits = gate_grad * gate * (chosen - probs) / SHARPNESS
        grad_unit = jnp.dot(grad_logits, table, precision=EXACT, preferred_element_type=F32)
        dembed_ref[...] += mm_rows(grad_logits, low_unit, EXACT)
        grad_low = clipped_back(grad_unit, low, low_scale, low_squares)
        dproj_ref[...] += mm_rows(grad_low, normed, EXACT)
        grad = grad + mm_cols(grad_low, proj, EXACT)
        small_ref[0:1, :] += jnp.sum(grad * unit, 0, keepdims=True)
        small_ref[1:2, :] += jnp.sum(grad, 0, keepdims=True)
        grad_hidden = cot_ref[at, :].astype(F32) + norm_back(grad, gain_ref[...], unit, scale)
        grad_hidden_ref[at, :] = grad_hidden
        low_grad = grad_hidden.astype(BF16)
        low_ref[at, :] = low_grad
        grad_mixed = mm_cols(low_grad, wo_ref[...]).astype(BF16)
        grad_mixed_ref[at, :] = grad_mixed
        products = grad_mixed.astype(F32) * mixed_ref[at, :].astype(F32)
        lines = mm_cols(head_lines, products, EXACT)
        for p in range(pairs):
            delta_ref[p, :, at] = lines[8 * p : 8 * p + 8, :]
        return carry

    lax.fori_loop(0, tokens // rows, row_block, 0)
    embed = embed_ref[...]
    squares = jnp.sum(embed * embed, -1, keepdims=True)
    table_scale = lax.rsqrt(jnp.maximum(squares, 1.0))
    dembed = clipped_back(dembed_ref[...], embed, table_scale, squares)
    lines_proj = small_ref.shape[0] - 8 - max(8, experts)
    small_ref[8 : 8 + lines_proj, :] = dproj_ref[0:lines_proj, :]
    small_ref[8 + lines_proj :, 0:128] = dembed[0 : max(8, experts), :]
    store_tiles(dwo_ref, mm_rows(mixed_ref[...], low_ref[...]))


def middle_back(
    back, gate_grads, hidden, cot, mixed, wo, gain, bias, proj, embed, route, place, space,
    experts, cap,
):
    tokens, width = hidden.shape
    slots = experts * cap
    back = back.reshape(slots, width)
    args = (back, gate_grads, hidden, cot, mixed, wo, gain, bias, proj, embed, route, place)
    return pl.pallas_call(
        functools.partial(middle_back_kernel, experts, cap),
        out_shape=[
            jax.ShapeDtypeStruct((tokens, width), F32),
            jax.ShapeDtypeStruct((tokens, width), BF16),
            jax.ShapeDtypeStruct((width // PAIR, 8, tokens), F32),
            jax.ShapeDtypeStruct((width // 128, width, 128), BF16),
            jax.ShapeDtypeStruct((8 + space + max(8, experts), width), F32),
        ],
        scratch_shapes=[
            pltpu.VMEM((tokens, 128), jnp.int32),
            pltpu.VMEM((tokens, width), BF16),
            pltpu.VMEM((128, width), F32),
            pltpu.VMEM((128, 128), F32),
        ],
        compiler_params=params(),
        cost_estimate=cost(2 * tokens * width * (2 * width + slots), 20 * tokens * width),
        name="middle_back",
    )(*args)


def qkv_back_kernel(
    x_ref, gain_ref, bias_ref, grad_hidden_ref, dq_ref, dk_ref, dv_ref, wq_ref, wk_ref, wv_ref,
    grad_ref, dwq_ref, dwk_ref, dwv_ref, small_ref, low_ref,
):
    tokens, width = x_ref.shape
    rows = 256
    small_ref[...] = jnp.zeros_like(small_ref)

    def row_block(i, carry):
        at = pl.ds(pl.multiple_of(i * rows, rows), rows)
        unit, scale = norm_parts(x_ref[at, :].astype(F32))
        low_ref[at, :] = (unit * gain_ref[...] + bias_ref[...]).astype(BF16)
        grad = (
            mm_cols(dq_ref[at, :], wq_ref[...])
            + mm_cols(dk_ref[at, :], wk_ref[...])
            + mm_cols(dv_ref[at, :], wv_ref[...])
        )
        small_ref[0:1, :] += jnp.sum(grad * unit, 0, keepdims=True)
        small_ref[1:2, :] += jnp.sum(grad, 0, keepdims=True)
        grad_ref[at, :] = grad_hidden_ref[at, :] + norm_back(grad, gain_ref[...], unit, scale)
        return carry

    lax.fori_loop(0, tokens // rows, row_block, 0)
    low = low_ref[...]
    store_tiles(dwq_ref, mm_rows(low, dq_ref[...]))
    store_tiles(dwk_ref, mm_rows(low, dk_ref[...]))
    store_tiles(dwv_ref, mm_rows(low, dv_ref[...]))


def qkv_back(x, gain, bias, grad_hidden, dq, dk, dv, wq, wk, wv):
    tokens, width = x.shape
    square = jax.ShapeDtypeStruct((width // 128, width, 128), BF16)
    return pl.pallas_call(
        qkv_back_kernel,
        out_shape=[
            jax.ShapeDtypeStruct((tokens, width), F32),
            square,
            square,
            square,
            jax.ShapeDtypeStruct((8, width), F32),
        ],
        scratch_shapes=[pltpu.VMEM((tokens, width), BF16)],
        compiler_params=params(),
        cost_estimate=cost(12 * tokens * width * width, 20 * tokens * width),
        name="qkv_back",
    )(x, gain, bias, grad_hidden, dq, dk, dv, wq, wk, wv)


def add_rows(rows, out_ref, out_at, terms):
    step = 48

    def body(i, carry):
        at = i * step
        total = None
        for ref, start in terms:
            value = ref[pl.ds(pl.multiple_of(start + at, 16), step), :].astype(F32)
            total = value if total is None else total + value
        out_ref[pl.ds(pl.multiple_of(out_at + at, 16), step), :] = total.astype(out_ref.dtype)
        return carry

    lax.fori_loop(0, rows // step, body, 0)


def can_reduce(width, dp_size, experts):
    return (width // 128) % 2 == 0 and (width // 128) * width % (48 * dp_size * experts) == 0


def tail_kernel(
    x_axis, experts, longest,
    q_ref, k_ref, v_ref, do_ref, delta_ref, x_ref, gain_ref, bias_ref,
    wq_ref, wk_ref, wv_ref, small_ref, probs_ref, grad_hidden_hbm, dwo_ref,
    grad_ref, out_ref, small_out,
    dq_all, dk_all, dv_all, normed_t, prob_buf, dk_sum, dv_sum, grads, grad_hidden, small_in,
    core_got, core_sum, plane_got, plane_sum, line_got, small_got,
    load_sem, prob_sem,
    core_send, core_recv, plane_send, plane_recv, line_send, line_recv,
    line_back_send, line_back_recv, plane_back_send, plane_back_recv,
    core_back_send, core_back_recv, small_send, small_recv,
):
    tokens, width = x_ref.shape
    pairs = width // PAIR
    n = grads.shape[0]
    block_rows = 256
    dp = lax.axis_index("dp")
    me = lax.axis_index("expert")
    core = lax.rem(dp, 2)
    x_at = dp // 2
    low = lax.rem(me, 2)
    high = me // 2
    planes, lines = 2 * x_axis, experts // 2
    mesh_ids = pl.DeviceIdType.MESH
    rows = grads.shape[1]
    half = rows // 2
    quarter = half // planes
    piece = quarter // lines
    plane_at = x_at * 2 + low

    other_core = {"dp": dp + 1 - 2 * core}

    def plane_peer(j):
        at = lax.rem(plane_at + j, planes)
        return at, (2 * (at // 2) + core, 2 * high + lax.rem(at, 2))

    def line_peer(j):
        at = lax.rem(high + j, lines)
        return at, {"expert": 2 * at + low}

    barrier = pltpu.get_barrier_semaphore()
    pl.semaphore_signal(barrier, inc=1, device_id=other_core, device_id_type=mesh_ids)
    for j in range(1, planes):
        pl.semaphore_signal(barrier, inc=1, device_id=plane_peer(j)[1], device_id_type=mesh_ids)
    for j in range(1, lines):
        pl.semaphore_signal(barrier, inc=1, device_id=line_peer(j)[1], device_id_type=mesh_ids)
    pl.semaphore_wait(barrier, planes + lines - 1)

    def remote(src, dst, send, recv, to):
        return pltpu.make_async_remote_copy(src, dst, send, recv, to, mesh_ids)

    def rows_at(start, size):
        return pl.ds(pl.multiple_of(start, 16), size)

    def core_copy(c):
        src = grads.at[c, rows_at((1 - core) * half, half)]
        return [remote(src, core_got.at[c], core_send.at[c], core_recv.at[c], other_core)]

    def plane_copies(c):
        made = []
        for j in range(1, planes):
            at, to = plane_peer(j)
            src = core_sum.at[c, rows_at(at * quarter, quarter)]
            made.append(
                remote(src, plane_got.at[c, j], plane_send.at[c, j], plane_recv.at[c, j], to)
            )
        return made

    def line_copies(c):
        made = []
        for j in range(1, lines):
            at, to = line_peer(j)
            src = plane_sum.at[c, rows_at(at * piece, piece)]
            made.append(remote(src, line_got.at[c, j], line_send.at[c, j], line_recv.at[c, j], to))
        return made

    base = core * half + plane_at * quarter

    def line_back(c):
        at = rows_at(base + high * piece, piece)
        made = []
        for j in range(1, lines):
            to = line_peer(j)[1]
            made.append(
                remote(
                    out_ref.at[c, at],
                    out_ref.at[c, at],
                    line_back_send.at[c, j],
                    line_back_recv.at[c, j],
                    to,
                )
            )
        return made

    def plane_back(c):
        at = rows_at(base, quarter)
        made = []
        for j in range(1, planes):
            to = plane_peer(j)[1]
            made.append(
                remote(
                    out_ref.at[c, at],
                    out_ref.at[c, at],
                    plane_back_send.at[c, j],
                    plane_back_recv.at[c, j],
                    to,
                )
            )
        return made

    def core_back(c):
        at = rows_at(core * half, half)
        return [
            remote(
                out_ref.at[c, at],
                out_ref.at[c, at],
                core_back_send.at[c],
                core_back_recv.at[c],
                other_core,
            )
        ]

    def small_copies(stage):
        made = []
        if stage == 0:
            made.append(
                remote(
                    small_got.at[0, 0],
                    small_got.at[0, 1],
                    small_send.at[0, 1],
                    small_recv.at[0, 1],
                    other_core,
                )
            )
        else:
            for j in range(1, planes if stage == 1 else lines):
                to = plane_peer(j)[1] if stage == 1 else line_peer(j)[1]
                made.append(
                    remote(
                        small_got.at[stage, 0],
                        small_got.at[stage, j],
                        small_send.at[stage, j],
                        small_recv.at[stage, j],
                        to,
                    )
                )
        return made

    def start(copies):
        for copy in copies:
            copy.start()

    def received(copies):
        for copy in copies:
            copy.wait_recv()

    def ordered(got, at, count):
        total = None
        for i in range(count):
            value = got(lax.rem(at + count - i, count))
            total = value if total is None else total + value
        return total

    def stage_run(stage, c):
        if stage == 0:
            start(core_copy(c))
        elif stage == 1:
            received(core_copy(c))
            add_rows(
                half, core_sum.at[c], 0, [(grads.at[c], core * half), (core_got.at[c], 0)]
            )
            start(plane_copies(c))
        elif stage == 2:
            received(plane_copies(c))
            add_rows(
                quarter,
                plane_sum.at[c],
                0,
                [(core_sum.at[c], plane_at * quarter)]
                + [(plane_got.at[c, j], 0) for j in range(1, planes)],
            )
            start(line_copies(c))
        elif stage == 3:
            received(line_copies(c))
            add_rows(
                piece,
                out_ref.at[c],
                base + high * piece,
                [(plane_sum.at[c], high * piece)]
                + [(line_got.at[c, j], 0) for j in range(1, lines)],
            )
            start(line_back(c))
        elif stage == 4:
            received(line_back(c))
            start(plane_back(c))
        elif stage == 5:
            received(plane_back(c))
            start(core_back(c))
        else:
            received(core_back(c))

    def small_run(stage):
        if stage == 0:
            small_got[0, 0] = small_in[...]
            start(small_copies(0))
        elif stage == 1:
            received(small_copies(0))
            small_got[1, 0] = small_got[0, 0] + small_got[0, 1]
            start(small_copies(1))
        elif stage == 2:
            received(small_copies(1))
            small_got[2, 0] = ordered(lambda j: small_got[1, j], plane_at, planes)
            start(small_copies(2))
        elif stage == 3:
            received(small_copies(2))
            small_out[...] = ordered(lambda j: small_got[2, j], high, lines)


    def prob_copy(p, slot):
        return pltpu.make_async_copy(
            probs_ref.at[pl.ds(2 * p, 2)], prob_buf.at[slot], prob_sem.at[slot]
        )

    loads = [
        pltpu.make_async_copy(dwo_ref, grads.at[0], load_sem.at[0]),
        pltpu.make_async_copy(grad_hidden_hbm, grad_hidden, load_sem.at[1]),
    ]
    prob_copy(0, 0).start()
    for load in loads:
        load.start()
    for at in range(0, tokens, block_rows):
        part = slice(at, at + block_rows)
        unit, _ = norm_parts(x_ref[part, :].astype(F32))
        normed = unit * gain_ref[...] + bias_ref[...]
        normed_t[:, part] = normed.T.astype(BF16)
    loads[0].wait()
    stage_run(0, 0)
    scale = HEAD_DIM**-0.5
    lane = iota((tokens, PAIR), 1)
    own = (lane < HEAD_DIM, lane >= HEAD_DIM)
    zero = jnp.zeros((), BF16)

    def pair_step(p, carry):
        slot = lax.rem(p, 2)
        prob_copy(p, slot).wait()

        @pl.when(p < pairs - 1)
        def _():
            prob_copy(p + 1, 1 - slot).start()

        lanes = pl.ds(pl.multiple_of(p * PAIR, PAIR), PAIR)
        dk_sum[...] = jnp.zeros_like(dk_sum)
        dv_sum[...] = jnp.zeros_like(dv_sum)
        for block in range(tokens // block_rows):
            first, last = key_window(block, block_rows, tokens, longest)
            mine = slice(block * block_rows, (block + 1) * block_rows)
            values = v_ref[first:last, lanes]
            keys = k_ref[first:last, lanes]
            queries = q_ref[mine, lanes]
            grad_out = do_ref[mine, lanes]
            dq = jnp.zeros((block_rows, PAIR), F32)
            dk = jnp.zeros((last - first, PAIR), F32)
            dv = jnp.zeros((last - first, PAIR), F32)
            for h in range(2):
                do_h = jnp.where(own[h][mine], grad_out, zero)
                q_h = jnp.where(own[h][mine], queries, zero)
                k_h = jnp.where(own[h][first:last], keys, zero)
                probs = prob_buf[slot, h, first:last, mine]
                grad_probs = mm_cols(values, do_h)
                grad_scores = (
                    probs.astype(F32) * (grad_probs - delta_ref[p, h : h + 1, mine])
                ).astype(BF16)
                dq = dq + mm_rows(grad_scores, k_h)
                dk = dk + mm(grad_scores, q_h)
                dv = dv + mm(probs, do_h)
            dq_all[mine, lanes] = (dq * scale).astype(BF16)
            dk_sum[first:last, :] += dk
            dv_sum[first:last, :] += dv
        dk_all[:, lanes] = (dk_sum[...] * scale).astype(BF16)
        dv_all[:, lanes] = dv_sum[...].astype(BF16)
        j = p // 2

        @pl.when(lax.rem(p, 2) == 0)
        def _():
            @pl.when(j >= 2)
            def _():
                stage_run(5, j - 2)

            @pl.when(j >= 1)
            def _():
                stage_run(3, j - 1)

            stage_run(1, j)

        @pl.when(lax.rem(p, 2) == 1)
        def _():
            both = pl.ds(pl.multiple_of(j * 2 * PAIR, PAIR), 2 * PAIR)
            for w, ref in enumerate((dq_all, dk_all, dv_all)):
                made = mm(normed_t[...], ref[:, both]).astype(BF16)
                for i in range(2):
                    start_at = (2 * w + i) * width
                    grads[j + 1, start_at : start_at + width, :] = made[:, i * 128 : (i + 1) * 128]
            stage_run(0, j + 1)

            @pl.when(j >= 2)
            def _():
                stage_run(6, j - 2)

            @pl.when(j >= 1)
            def _():
                stage_run(4, j - 1)

            stage_run(2, j)

        return carry

    lax.fori_loop(0, pairs, pair_step, 0)
    loads[1].wait()
    small_in[0:8, :] = jnp.zeros((8, width), F32)
    small_in[8:, :] = small_ref[...]

    def row_block(i):
        at = slice(i * block_rows, (i + 1) * block_rows)
        unit, unit_scale = norm_parts(x_ref[at, :].astype(F32))
        grad = (
            mm_cols(dq_all[at, :], wq_ref[...])
            + mm_cols(dk_all[at, :], wk_ref[...])
            + mm_cols(dv_all[at, :], wv_ref[...])
        )
        small_in[0:1, :] += jnp.sum(grad * unit, 0, keepdims=True)
        small_in[1:2, :] += jnp.sum(grad, 0, keepdims=True)
        grad_ref[at, :] = grad_hidden[at, :] + norm_back(grad, gain_ref[...], unit, unit_scale)

    blocks = tokens // block_rows
    done = 0
    small_at = 0
    for tick in range(pairs + 1, pairs + 7):
        if done < blocks:
            row_block(done)
            done += 1
        for stage in reversed(range(7)):
            for c in range(n):
                if tick - 2 * c == stage:
                    stage_run(stage, c)
        if done == blocks and small_at < 4:
            small_run(small_at)
            small_at += 1
    while done < blocks:
        row_block(done)
        done += 1
    while small_at < 4:
        small_run(small_at)
        small_at += 1
    for stage in range(3):
        for copy in small_copies(stage):
            copy.wait_send()

    def sent(c, carry):
        for made in (core_copy, plane_copies, line_copies, line_back, plane_back, core_back):
            for copy in made(c):
                copy.wait_send()
        return carry

    lax.fori_loop(0, n, sent, 0)


def tail(
    q, k, v, grad_mixed, probs, delta, x, gain, bias, grad_hidden, wq, wk, wv, dwo, small2,
    longest, dp_size, experts,
):
    tokens, width = x.shape
    pairs = width // PAIR
    n = 1 + pairs // 2
    rows = width // 128 * width
    x_axis, lines, planes = dp_size // 2, experts // 2, dp_size
    half = rows // 2
    quarter = half // planes
    piece = quarter // lines
    most = max(planes, lines)
    small_shape = (8 + small2.shape[0], width)
    sems = pltpu.SemaphoreType.DMA
    local = pl.BlockSpec(memory_space=pltpu.VMEM)
    anywhere = pl.BlockSpec(memory_space=pl.ANY)
    low = pltpu.VMEM((tokens, width), BF16)
    return pl.pallas_call(
        functools.partial(tail_kernel, x_axis, experts, longest),
        in_specs=[local] * 12 + [anywhere] * 3,
        out_specs=[local] * 3,
        out_shape=[
            jax.ShapeDtypeStruct((tokens, width), F32),
            jax.ShapeDtypeStruct((n, rows, 128), BF16),
            jax.ShapeDtypeStruct(small_shape, F32),
        ],
        scratch_shapes=[
            low,
            low,
            low,
            pltpu.VMEM((width, tokens), BF16),
            pltpu.VMEM((2, 2, tokens, tokens), BF16),
            pltpu.VMEM((tokens, PAIR), F32),
            pltpu.VMEM((tokens, PAIR), F32),
            pltpu.VMEM((n, rows, 128), BF16),
            pltpu.VMEM((tokens, width), F32),
            pltpu.VMEM(small_shape, F32),
            pltpu.VMEM((n, half, 128), BF16),
            pltpu.VMEM((n, half, 128), BF16),
            pltpu.VMEM((n, planes, quarter, 128), BF16),
            pltpu.VMEM((n, quarter, 128), BF16),
            pltpu.VMEM((n, lines, piece, 128), BF16),
            pltpu.VMEM((3, most, *small_shape), F32),
            sems((2,)),
            sems((2,)),
        ]
        + [sems((n,))] * 2
        + [sems((n, planes))] * 2
        + [sems((n, lines))] * 4
        + [sems((n, planes))] * 2
        + [sems((n,))] * 2
        + [sems((3, most))] * 2,
        compiler_params=pltpu.CompilerParams(
            vmem_limit_bytes=60 * MIB, collective_id=1, has_side_effects=True
        ),
        cost_estimate=cost(16 * pairs * tokens * tokens * 256, 4 * pairs * tokens * tokens),
        name="tail",
    )(
        q, k, v, grad_mixed, delta, x, gain, bias, wq, wk, wv, small2,
        probs, grad_hidden, dwo.reshape(rows, 128),
    )


def finish_kernel(experts, cap, x_axis, made_ref, hidden_ref, gate_ref, route_ref, sums_ref, *refs):
    din_refs = refs[:x_axis]
    dout_refs = refs[x_axis : 2 * x_axis]
    out_ref, dwo_ref, dwq_ref, dwk_ref, dwv_ref, din_ref, dout_ref, slot_ref = refs[2 * x_axis :]
    tokens, width = hidden_ref.shape
    rows = 256
    slot_ref[...] = jnp.broadcast_to(slot_col_of(route_ref[...], experts, cap), slot_ref.shape)
    slots = experts * cap

    def row_block(i, carry):
        at = pl.ds(pl.multiple_of(i * rows, rows), rows)
        pick = one_hot(iota((rows, slots), 1) == slot_ref[at, 0:1])
        produced = mm(pick, made_ref[...])
        out_ref[at, :] = (hidden_ref[at, :] + gate_ref[at, 0:1] * produced).astype(BF16)
        return carry

    lax.fori_loop(0, tokens // rows, row_block, 0)
    for tile in range(width // 128):
        lanes = slice(tile * 128, (tile + 1) * 128)
        dwo_ref[:, lanes] = sums_ref[0, tile * width : (tile + 1) * width, :].astype(F32)
        for w, ref in enumerate((dwq_ref, dwk_ref, dwv_ref)):
            start = (2 * w + tile % 2) * width
            ref[:, lanes] = sums_ref[1 + tile // 2, start : start + width, :].astype(F32)
    for out, parts in ((din_ref, din_refs), (dout_ref, dout_refs)):
        total = parts[0][...].astype(F32)
        for part in parts[1:]:
            total = total + part[...].astype(F32)
        out[...] = total


def finish(made, hidden, gate, route, sums, din, dout, experts, cap):
    tokens, width = hidden.shape
    square = jax.ShapeDtypeStruct((width, width), F32)
    return pl.pallas_call(
        functools.partial(finish_kernel, experts, cap, len(din)),
        out_shape=[jax.ShapeDtypeStruct((tokens, width), BF16)]
        + [square] * 4
        + [jax.ShapeDtypeStruct(din[0].shape, F32), jax.ShapeDtypeStruct(dout[0].shape, F32)],
        scratch_shapes=[pltpu.VMEM((tokens, 128), jnp.int32)],
        compiler_params=params(),
        cost_estimate=cost(2 * tokens * width * experts * cap, 10 * tokens * width),
        name="finish",
    )(made.reshape(-1, width), hidden, gate, route, sums, *din, *dout)


def exchange(blocks, axis):
    return lax.all_to_all(blocks, axis, split_axis=0, concat_axis=0, tiled=True)


def shifted(blocks, axis, size, step=1):
    moved = [blocks[0]]
    for s in range(1, len(blocks)):
        moved.append(
            lax.ppermute(blocks[s], axis, [(i, (i + s * step) % size) for i in range(size)])
        )
    return moved


def on_device(
    tokens,
    segment_ids,
    routes,
    norm1_gain,
    norm1_bias,
    query_weight,
    w_key,
    w_value,
    w_output,
    norm2_gain,
    norm2_bias,
    router_proj,
    expert_embed,
    expert_in,
    expert_out,
    cotangent,
):
    count, width = tokens.shape
    experts = lax.axis_size("expert")
    dp_size = lax.axis_size("dp")
    cap = 2 * count // experts
    longest = segment_ids.shape[1] // 2
    place = lax.rem(routes - lax.axis_index("expert") + experts, experts)
    place_row = place.reshape(1, count)
    seg_col = segment_ids.reshape(count, 1)
    gain1, bias1 = norm1_gain[None], norm1_bias[None]
    gain2, bias2 = norm2_gain[None], norm2_bias[None]
    space = router_proj.shape[1]
    proj = jnp.pad(router_proj, ((0, 0), (0, 128 - space)))
    embed = jnp.pad(expert_embed, ((0, 128 - experts), (0, 128 - space)))

    up = gather_slots(place_row, cotangent, experts, cap)
    tokens, *up = lax.optimization_barrier((tokens, *up))
    up = shifted(up, "expert", experts)
    q, k, v = qkv(tokens, gain1, bias1, query_weight, w_key, w_value)
    mixed, probs = attention(q, k, v, seg_col, longest)
    hidden, gate, slots, gates = middle(
        mixed, tokens, w_output, gain2, bias2, proj, embed, routes, place_row, experts, cap
    )
    back, gate_grads, made, din, dout = expert(
        slots, gates, up, expert_in[0], expert_out[0], dp_size
    )
    din = shifted(din, "dp", dp_size, 2)
    dout = shifted(dout, "dp", dp_size, 2)
    made = exchange(made, "expert")
    grad_hidden, grad_mixed, delta, dwo, small2 = middle_back(
        back, gate_grads, hidden, cotangent, mixed, w_output, gain2, bias2,
        proj, embed, routes, place, space, experts, cap,
    )
    if can_reduce(width, dp_size, experts):
        grad_input, sums, small = tail(
            q, k, v, grad_mixed, probs, delta, tokens, gain1, bias1, grad_hidden,
            query_weight, w_key, w_value, dwo, small2, longest, dp_size, experts,
        )
    else:
        dq, dk, dv = attention_back(q, k, v, grad_mixed, probs, delta, longest)
        grad_input, dwq, dwk, dwv, small1 = qkv_back(
            tokens, gain1, bias1, grad_hidden, dq, dk, dv, query_weight, w_key, w_value
        )
        chunks = [dwo]
        for at in range(0, width // 128, 2):
            chunks.append(jnp.concatenate([dw[at : at + 2] for dw in (dwq, dwk, dwv)], 0))
        small = jnp.concatenate([small1, small2], 0)
        sums, small = lax.psum((jnp.stack(chunks).astype(F32), small), ("dp", "expert"))
        sums = sums.astype(BF16).reshape(len(chunks), -1, 128)
    output, dwo, dwq, dwk, dwv, grad_in, grad_out = finish(
        made, hidden, gate, routes, sums, din, dout, experts, cap
    )
    return (
        output,
        grad_input,
        small[0],
        small[1],
        dwq,
        dwk,
        dwv,
        dwo,
        small[8],
        small[9],
        small[16 : 16 + space].T,
        small[16 + space : 16 + space + experts, :space],
        grad_in[None],
        grad_out[None],
    )


def solution(mesh):
    split = P(("dp", "expert"), None)
    in_specs = (
        (split,) * 3 + (P(),) * 10 + (P("expert", None, None), P("expert", None, None), split)
    )
    out_specs = (
        (split, split) + (P(),) * 10 + (P("expert", None, "dp"), P("expert", "dp", None))
    )
    return jax.shard_map(
        on_device, mesh=mesh, in_specs=in_specs, out_specs=out_specs, check_vma=False
    )
```

```python
import functools

import jax
import jax.numpy as jnp
from jax import lax
from jax.experimental import pallas as pl
from jax.experimental.pallas import tpu as pltpu
from jax.sharding import PartitionSpec as P

HEAD_DIM = 64
PAIR = 2 * HEAD_DIM
SHARPNESS = 0.25
EXACT = lax.Precision.HIGHEST
BF16 = jnp.bfloat16
F32 = jnp.float32
FAR = -1e30
MIB = 1 << 20
WINDOW = 4
PARTS = 4
OUTPUT_TICK = 4
PARTS_EARLY = 16
PARTS_LOOP = 2
PARTS_DRAIN = 2


def mm(left, right):
    return jnp.dot(left, right, preferred_element_type=F32)


def mm_rows(left, right, precision=None):
    return lax.dot_general(
        left, right, (((0,), (0,)), ((), ())), precision=precision, preferred_element_type=F32
    )


def mm_cols(left, right, precision=None):
    return lax.dot_general(
        left, right, (((1,), (1,)), ((), ())), precision=precision, preferred_element_type=F32
    )


def iota(shape, axis):
    return lax.broadcasted_iota(jnp.int32, shape, axis)


def one_hot(condition):
    return jnp.where(condition, 1.0, 0.0).astype(BF16)


def params(limit=56):
    return pltpu.CompilerParams(vmem_limit_bytes=limit * MIB)


def cost(flops, moved, trans=0):
    return pl.CostEstimate(flops=int(flops), bytes_accessed=int(moved), transcendentals=int(trans))


def spec_all(shape):
    zeros = (0,) * len(shape)
    return pl.BlockSpec(shape, lambda *ids: zeros)


def slot_row_of(route_row, experts, cap):
    tokens = route_row.shape[1]
    padded = max(8, experts)
    hits = one_hot(iota((padded, tokens), 0) == route_row)
    earlier = one_hot(iota((tokens, tokens), 0) < iota((tokens, tokens), 1))
    ranks = mm(hits, earlier)
    rank = jnp.sum(ranks * hits.astype(F32), 0, keepdims=True)
    return route_row * cap + rank.astype(jnp.int32)


def as_row(col):
    rows = col.shape[0]
    eye = iota((rows, rows), 0) == iota((rows, rows), 1)
    return jnp.sum(jnp.where(eye, col, 0.0), 0, keepdims=True)


def as_col(row):
    rows = row.shape[1]
    eye = iota((rows, rows), 0) == iota((rows, rows), 1)
    return jnp.sum(jnp.where(eye, row, 0.0), 1, keepdims=True)


def norm_parts(values):
    average = jnp.mean(values, -1, keepdims=True)
    centred = values - average
    spread = jnp.mean(centred * centred, -1, keepdims=True)
    scale = lax.rsqrt(spread + 1e-05)
    return centred * scale, scale


def norm_back(grad, gain, unit, scale):
    grad_unit = grad * gain
    inner = jnp.mean(grad_unit * unit, -1, keepdims=True)
    return scale * (grad_unit - jnp.mean(grad_unit, -1, keepdims=True) - unit * inner)


def key_window(block, rows, tokens, longest):
    first = max(0, (block * rows - longest + 1) // 128 * 128)
    last = min(tokens, -(-(block * rows + rows - 1 + longest) // 128) * 128)
    return first, last


def attention_back_kernel(
    rows, longest, q_ref, k_ref, v_ref, do_ref, prob_ref, delta_ref,
    dq_ref, dk_ref, dv_ref, dk_sum, dv_sum,
):
    tokens = q_ref.shape[0]
    lane = iota((tokens, PAIR), 1)
    own = (lane < HEAD_DIM, lane >= HEAD_DIM)
    zero = jnp.zeros((), BF16)
    scale = HEAD_DIM**-0.5
    dk_sum[...] = jnp.zeros_like(dk_sum)
    dv_sum[...] = jnp.zeros_like(dv_sum)
    for block in range(tokens // rows):
        first, last = key_window(block, rows, tokens, longest)
        mine = slice(block * rows, (block + 1) * rows)
        values = v_ref[first:last, :]
        dq = jnp.zeros((rows, PAIR), F32)
        dk = jnp.zeros((last - first, PAIR), F32)
        dv = jnp.zeros((last - first, PAIR), F32)
        for h in range(2):
            do_h = jnp.where(own[h][mine], do_ref[mine, :], zero)
            q_h = jnp.where(own[h][mine], q_ref[mine, :], zero)
            k_h = jnp.where(own[h][first:last], k_ref[first:last, :], zero)
            probs = prob_ref[h, first:last, mine]
            grad_probs = mm_cols(values, do_h)
            grad_scores = (
                probs.astype(F32) * (grad_probs - delta_ref[0, h : h + 1, mine])
            ).astype(BF16)
            dq = dq + mm_rows(grad_scores, k_h)
            dk = dk + mm(grad_scores, q_h)
            dv = dv + mm(probs, do_h)
        dq_ref[mine, :] = (dq * scale).astype(BF16)
        dk_sum[first:last, :] += dk
        dv_sum[first:last, :] += dv
    dk_ref[...] = (dk_sum[...] * scale).astype(BF16)
    dv_ref[...] = dv_sum[...].astype(BF16)


def attention_back(q, k, v, grad_mixed, probs, delta, longest):
    tokens, width = q.shape
    pairs = width // PAIR
    rows = 256
    block = pl.BlockSpec((tokens, PAIR), lambda p: (0, p))
    made = jax.ShapeDtypeStruct((tokens, width), BF16)
    return pl.pallas_call(
        functools.partial(attention_back_kernel, rows, longest),
        grid=(pairs,),
        in_specs=[block] * 4
        + [
            pl.BlockSpec((2, tokens, tokens), lambda p: (p, 0, 0)),
            pl.BlockSpec((1, 8, tokens), lambda p: (p, 0, 0)),
        ],
        out_specs=[block] * 3,
        out_shape=[made] * 3,
        scratch_shapes=[pltpu.VMEM((tokens, PAIR), F32)] * 2,
        compiler_params=params(),
        cost_estimate=cost(8 * 2 * pairs * tokens * tokens * 256, 4 * pairs * tokens * tokens),
        name="attention_back",
    )(q, k, v, grad_mixed, probs, delta)


def router_parts(normed, proj_parts, embed, route, experts):
    high, rest = split_two(normed)
    both = mm(high, proj_parts[...])
    low = both[:, 0:128] + (both[:, 128:256] + mm(rest, proj_parts[:, 0:128]))
    low_squares = jnp.sum(low * low, -1, keepdims=True)
    low_scale = lax.rsqrt(jnp.maximum(low_squares, 1.0))
    low_unit = low * low_scale
    squares = jnp.sum(embed * embed, -1, keepdims=True)
    table_scale = lax.rsqrt(jnp.maximum(squares, 1.0))
    table = embed * table_scale
    logits = mm_cols(low_unit, table, EXACT) / SHARPNESS
    lane = iota(logits.shape, 1)
    logits = jnp.where(lane < experts, logits, FAR)
    weights = jnp.exp(logits - jnp.max(logits, -1, keepdims=True))
    probs = weights / jnp.sum(weights, -1, keepdims=True)
    chosen = jnp.where(lane == route, 1.0, 0.0)
    gate = jnp.sum(probs * chosen, -1, keepdims=True)
    return gate, probs, chosen, low, low_squares, low_scale, low_unit, squares, table_scale, table


def clipped_back(grad_unit, raw, scale, squares):
    share = jnp.where(squares > 1.0, 1.0, jnp.where(squares == 1.0, 0.5, 0.0))
    inner = jnp.sum(grad_unit * raw, -1, keepdims=True)
    return scale * grad_unit - share * scale * scale * scale * inner * raw


def col_of(row):
    return as_col(row.astype(F32)).astype(jnp.int32)


def split_two(value):
    high = value.astype(BF16)
    return high, (value - high.astype(F32)).astype(BF16)


def forward_kernel(
    experts, cap, longest,
    route_ref, seg_ref, cot_ref, x_ref, vecs_ref, tables_ref, wq_ref, wk_ref, wv_ref, wo_ref,
    q_ref, k_ref, v_ref, mixed_ref, probs_ref, hidden_ref, gate_ref, slots_ref, gates_ref,
    lines_ref, up_ref,
    weights, q_all, k_all, v_all, mixed_all, prob_buf, hidden_all, gate_all, slots_all,
    gates_all, lines_all, up_all, kept, tags, proj_parts,
    load_sem, store_sem, prob_sem, up_send, up_recv,
):
    tokens, width = x_ref.shape
    pairs = width // PAIR
    rows = 256
    blocks = tokens // rows
    me = lax.axis_index("expert")
    mesh_ids = pl.DeviceIdType.MESH
    loads = [
        pltpu.make_async_copy(ref, weights.at[i], load_sem.at[i])
        for i, ref in enumerate((wq_ref, wk_ref, wv_ref, wo_ref))
    ]
    for load in loads:
        load.start()
    barrier = pltpu.get_barrier_semaphore()

    def greet(s, carry):
        pl.semaphore_signal(
            barrier, inc=1, device_id={"expert": lax.rem(me + s, experts)}, device_id_type=mesh_ids
        )
        return carry

    lax.fori_loop(1, experts, greet, 0)

    route = route_ref[...]
    place = lax.rem(route - me + experts, experts)
    slot = slot_row_of(place, experts, cap)
    lines_all[...] = jnp.zeros_like(lines_all)
    lines_all[0:1, :] = slot
    lines_all[1:2, :] = slot + (route - place) * cap
    lines_all[2:3, :] = route
    pl.semaphore_wait(barrier, experts - 1)

    def up_copy(s):
        to = {"expert": lax.rem(me + s, experts)}
        return pltpu.make_async_remote_copy(
            up_all.at[s], up_ref.at[s], up_send.at[s], up_recv.at[s], to, mesh_ids
        )

    def up_block(s, carry):
        pick = one_hot(iota((cap, tokens), 0) + s * cap == lines_all[0:1, :])
        up_all[s] = mm(pick, cot_ref[...]).astype(BF16)

        @pl.when(s > 0)
        def _():
            up_copy(s).start()

        return carry

    lax.fori_loop(0, experts, up_block, 0)
    stores = []

    def store(src, dst):
        copy = pltpu.make_async_copy(src, dst, store_sem.at[len(stores)])
        copy.start()
        stores.append(copy)

    store(up_all.at[0], up_ref.at[0])
    store(lines_all, lines_ref)
    for load in loads:
        load.wait()

    def qkv_block(i, carry):
        at = pl.ds(pl.multiple_of(i * rows, rows), rows)
        unit, _ = norm_parts(x_ref[at, :].astype(F32))
        normed = (unit * vecs_ref[0:1, :] + vecs_ref[1:2, :]).astype(BF16)
        for w, ref in enumerate((q_all, k_all, v_all)):
            ref[at, :] = mm(normed, weights[w]).astype(BF16)
        lane = iota((rows, PAIR), 1)
        seg = col_of(seg_ref[0:1, at])
        for h in range(2):
            other = (1 - h) * HEAD_DIM
            tags[h, at, :] = jnp.where(lane - other == seg, 1.0, 0.0).astype(BF16)
            k_tag = jnp.where(lane - other == seg, 0.0, FAR)
            k_tag = jnp.where((lane >= other) & (lane < other + 8), k_tag, 0.0)
            tags[2 + h, at, :] = k_tag.astype(BF16)
        return carry

    lax.fori_loop(0, blocks, qkv_block, 0)
    store(q_all, q_ref)
    store(k_all, k_ref)
    store(v_all, v_ref)

    lane = iota((tokens, PAIR), 1)
    own = (lane < HEAD_DIM, lane >= HEAD_DIM)

    def prob_copy(p, at):
        return pltpu.make_async_copy(prob_buf.at[at], probs_ref.at[pl.ds(2 * p, 2)], prob_sem.at[at])

    def pair_step(p, carry):
        buffer = lax.rem(p, 2)

        @pl.when(p >= 2)
        def _():
            prob_copy(p - 2, buffer).wait()

        lanes = pl.ds(pl.multiple_of(p * PAIR, PAIR), PAIR)
        queries = q_all[:, lanes] * jnp.asarray(HEAD_DIM**-0.5, BF16)
        keys = k_all[:, lanes]
        q_h = [jnp.where(own[h], queries, tags[h]) for h in range(2)]
        k_h = [jnp.where(own[h], keys, tags[2 + h]) for h in range(2)]
        for block in range(blocks):
            first, last = key_window(block, rows, tokens, longest)
            mine = slice(block * rows, (block + 1) * rows)
            out = []
            for h in range(2):
                scores = mm_cols(k_h[h][first:last], q_h[h][mine])
                largest = jnp.max(scores, 0, keepdims=True)
                weighted = jnp.exp(scores - largest)
                total = jnp.sum(weighted, 0, keepdims=True)
                probs = (weighted * (1.0 / total)).astype(BF16)
                prob_buf[buffer, h, first:last, mine] = probs
                out.append(mm_rows(probs, v_all[first:last, lanes]))
            mixed_all[mine, lanes] = jnp.where(own[0][mine], out[0], out[1]).astype(BF16)
        prob_copy(p, buffer).start()
        return carry

    lax.fori_loop(0, pairs, pair_step, 0)
    store(mixed_all, mixed_ref)
    high, rest = split_two(tables_ref[0:width, :])
    proj_parts[:, 0:128] = high
    proj_parts[:, 128:256] = rest

    def row_block(i, carry):
        at = pl.ds(pl.multiple_of(i * rows, rows), rows)
        hidden = x_ref[at, :].astype(F32) + mm(mixed_all[at, :], weights[3])
        hidden_all[at, :] = hidden
        unit, _ = norm_parts(hidden)
        normed = unit * vecs_ref[2:3, :] + vecs_ref[3:4, :]
        route_col = col_of(lines_all[2:3, at])
        gate = router_parts(normed, proj_parts, tables_ref[width:, :], route_col, experts)[0]
        gate_all[at, :] = jnp.broadcast_to(gate, (rows, 128))
        high = gate.astype(BF16).astype(F32)
        mid = (gate - high).astype(BF16).astype(F32)
        rest = gate - high - mid
        lane = iota((rows, 128), 1)
        split = jnp.where(lane == 0, high, jnp.where(lane == 1, mid, jnp.where(lane == 2, rest, 0.0)))
        kept[at, 0:width] = normed.astype(BF16)
        kept[at, width : width + 128] = split.astype(BF16)
        return carry

    lax.fori_loop(0, blocks, row_block, 0)
    store(hidden_all, hidden_ref)
    store(gate_all, gate_ref)

    def slot_block(e, carry):
        pick = one_hot(iota((cap, tokens), 0) + e * cap == lines_all[0:1, :])
        got = mm(pick, kept[...])
        slots_all[e] = got[:, 0:width].astype(BF16)
        gates = as_row(jnp.sum(got[:, width : width + 128], 1, keepdims=True))
        gates_all[e] = jnp.broadcast_to(gates, (8, cap))
        return carry

    lax.fori_loop(0, experts, slot_block, 0)
    store(slots_all, slots_ref)
    store(gates_all, gates_ref)
    for p in (pairs - 2, pairs - 1):
        prob_copy(p, p % 2).wait()
    for copy in stores:
        copy.wait()

    def arrived(s, carry):
        up_copy(s).wait()
        return carry

    lax.fori_loop(1, experts, arrived, 0)


def forward(route_row, seg_row, cot, x, vecs, tables, wq, wk, wv, wo, longest, experts, cap):
    tokens, width = x.shape
    pairs = width // PAIR
    local = pl.BlockSpec(memory_space=pltpu.VMEM)
    anywhere = pl.BlockSpec(memory_space=pl.ANY)
    low = jax.ShapeDtypeStruct((tokens, width), BF16)
    chunks = jax.ShapeDtypeStruct((experts, cap, width), BF16)
    out_shape = [
        low,
        low,
        low,
        low,
        jax.ShapeDtypeStruct((2 * pairs, tokens, tokens), BF16),
        jax.ShapeDtypeStruct((tokens, width), F32),
        jax.ShapeDtypeStruct((tokens, 128), F32),
        chunks,
        jax.ShapeDtypeStruct((experts, 8, cap), F32),
        jax.ShapeDtypeStruct((8, tokens), jnp.int32),
        chunks,
    ]
    low_buf = pltpu.VMEM((tokens, width), BF16)
    sems = pltpu.SemaphoreType.DMA
    return pl.pallas_call(
        functools.partial(forward_kernel, experts, cap, longest),
        in_specs=[local] * 6 + [anywhere] * 4,
        out_specs=[anywhere] * len(out_shape),
        out_shape=out_shape,
        scratch_shapes=[
            pltpu.VMEM((4, width, width), BF16),
            low_buf,
            low_buf,
            low_buf,
            low_buf,
            pltpu.VMEM((2, 2, tokens, tokens), BF16),
            pltpu.VMEM((tokens, width), F32),
            pltpu.VMEM((tokens, 128), F32),
            pltpu.VMEM((experts, cap, width), BF16),
            pltpu.VMEM((experts, 8, cap), F32),
            pltpu.VMEM((8, tokens), jnp.int32),
            pltpu.VMEM((experts, cap, width), BF16),
            pltpu.VMEM((tokens, width + 128), BF16),
            pltpu.VMEM((4, tokens, PAIR), BF16),
            pltpu.VMEM((width, 256), BF16),
            sems((4,)),
            sems((10,)),
            sems((2,)),
            sems((experts,)),
            sems((experts,)),
        ],
        compiler_params=pltpu.CompilerParams(
            vmem_limit_bytes=60 * MIB, collective_id=2, has_side_effects=True
        ),
        cost_estimate=cost(8 * pairs * tokens * tokens * 256, 4 * pairs * tokens * tokens),
        name="forward",
    )(route_row, seg_row, cot, x, vecs, tables, wq, wk, wv, wo)


def distance(experts, i):
    near = (i + 1) // 2
    return lax.rem(i % 2 * near + (1 - i % 2) * (experts - near), experts)


def gelu_parts(pre):
    size = jnp.abs(pre)
    t = pl.reciprocal(1.0 + 0.23164189298 * size, approx=False)
    bell = jnp.exp(-0.5 * pre * pre)
    tail = t * (
        0.127414796
        + t * (-0.142248368 + t * (0.7107068705 + t * (-0.7265760135 + t * 0.5307027145)))
    )
    tail = tail * bell
    phi_sum = jnp.where(pre >= 0, 1.0 - tail, tail)
    return phi_sum, pre * bell * 0.3989422804014327


def expert_kernel(experts, x_axis, *refs):
    x_ref, gates_ref, w_in_ref, w_out_ref, up_ref = refs[:5]
    back_ref, gate_grads_ref = refs[5:7]
    rest = refs[7:]
    made_ref = rest[0]
    din_refs = rest[1 : 1 + x_axis]
    dout_refs = rest[1 + x_axis : 1 + 2 * x_axis]
    (
        x_here, up_here, gates_here, back_here, gate_grads_here, made_here,
        active, grad_pre, w_in, w_out, din_got, dout_got,
        load_sem, x_send, x_recv, g_send, g_recv, b_send, b_recv, gg_send, gg_recv,
        d_send, d_recv, e_send, e_recv, store_sem,
    ) = rest[1 + 2 * x_axis :]
    cap, width = x_here.shape[1:]
    hidden = w_in.shape[1]
    me = lax.axis_index("expert")
    dp = lax.axis_index("dp")
    core = lax.rem(dp, 2)
    mesh_ids = pl.DeviceIdType.MESH

    barrier = pltpu.get_barrier_semaphore()

    def greet(s, carry):
        pl.semaphore_signal(
            barrier, inc=1, device_id={"expert": lax.rem(me + s, experts)}, device_id_type=mesh_ids
        )
        return carry

    lax.fori_loop(1, experts, greet, 0)
    pl.semaphore_signal(
        barrier, inc=1, device_id={"dp": dp + 1 - 2 * core}, device_id_type=mesh_ids
    )

    def x_peer(k):
        return {"dp": 2 * lax.rem(dp // 2 + k, x_axis) + core}

    for k in range(1, x_axis):
        pl.semaphore_signal(barrier, inc=1, device_id=x_peer(k), device_id_type=mesh_ids)
    pl.semaphore_wait(barrier, experts + x_axis - 1)

    def out_copy(s):
        to = {"expert": lax.rem(me + s, experts)}
        return (
            pltpu.make_async_remote_copy(
                x_ref.at[s], x_here.at[s], x_send.at[s], x_recv.at[s], to, mesh_ids
            ),
            pltpu.make_async_remote_copy(
                gates_ref.at[s], gates_here.at[s], g_send.at[s], g_recv.at[s], to, mesh_ids
            ),
        )

    def home_copy(s):
        to = {"expert": lax.rem(me + experts - s, experts)}
        return (
            pltpu.make_async_remote_copy(
                back_here.at[s], back_ref.at[s], b_send.at[s], b_recv.at[s], to, mesh_ids
            ),
            pltpu.make_async_remote_copy(
                gate_grads_here.at[s], gate_grads_ref.at[s], gg_send.at[s], gg_recv.at[s], to, mesh_ids
            ),
        )

    nth = functools.partial(distance, experts)
    window = min(WINDOW, experts - 1)

    def send_out(i, carry):
        for copy in out_copy(nth(i)):
            copy.start()
        return carry

    lax.fori_loop(1, 1 + window, send_out, 0)
    loads = [
        pltpu.make_async_copy(x_ref.at[0], x_here.at[0], load_sem.at[0]),
        pltpu.make_async_copy(gates_ref.at[0], gates_here.at[0], load_sem.at[1]),
        pltpu.make_async_copy(w_in_ref, w_in, load_sem.at[2]),
        pltpu.make_async_copy(w_out_ref, w_out, load_sem.at[3]),
    ]
    loads.append(pltpu.make_async_copy(up_ref, up_here, load_sem.at[4]))
    for load in loads:
        load.start()
    for load in loads:
        load.wait()

    step = 512

    def send_home(i, carry):
        for copy in home_copy(nth(i)):
            copy.start()
        return carry

    def chunk(i, carry):
        s = nth(i)

        @pl.when(i > 0)
        def _():
            for copy in out_copy(s):
                copy.wait_recv()

            @pl.when(i + window < experts)
            def _():
                send_out(i + window, 0)

        @pl.when(i == experts - 1)
        def _():
            lax.fori_loop(1, experts - 1, send_home, 0)

        at_rows = pl.ds(pl.multiple_of(s * cap, cap), cap)
        gate = as_col(gates_here[s][0:1, :])
        up = up_here[s].astype(F32)
        scaled = (up * gate).astype(BF16)
        x = x_here[s]
        for at in range(0, hidden, step):
            part = slice(at, at + step)
            pre = mm(x, w_in[:, part])
            grad_active = mm_cols(scaled, w_out[part, :])
            phi_sum, slope = gelu_parts(pre)
            active[at_rows, part] = (pre * phi_sum).astype(BF16)
            grad_pre[at_rows, part] = (grad_active * (phi_sum + slope)).astype(BF16)
        made = mm(active[at_rows, :], w_out[...]).astype(BF16)
        made_here[s] = made
        gate_grad = jnp.sum(up * made.astype(F32), 1, keepdims=True)
        gate_grads_here[s] = jnp.broadcast_to(as_row(gate_grad), (8, cap))
        up_here[s] = scaled
        back_here[s] = mm_cols(grad_pre[at_rows, :], w_in[...]).astype(BF16)

        return carry

    lax.fori_loop(0, experts, chunk, 0)
    send_home(experts - 1, 0)
    stores = [
        pltpu.make_async_copy(back_here.at[0], back_ref.at[0], store_sem.at[0]),
        pltpu.make_async_copy(gate_grads_here.at[0], gate_grads_ref.at[0], store_sem.at[1]),
    ]
    for s in range(experts):
        home = lax.rem(me + experts - s, experts)
        stores.append(
            pltpu.make_async_copy(made_here.at[s], made_ref.at[home], store_sem.at[2 + s])
        )
    for store in stores:
        store.start()

    block = hidden // (2 * x_axis)
    slots = experts * cap
    other = {"dp": dp + 1 - 2 * core}
    x_all = x_here.reshape(slots, width)
    up_all = up_here.reshape(slots, width)

    def block_start(k, for_core):
        x_at = lax.rem(dp // 2 + k, x_axis)
        return pl.multiple_of((2 * x_at + for_core) * block, 128)

    def din_out(k):
        return w_in.at[:, k * block : (k + 1) * block]

    def dout_out(k):
        return w_out.at[k * block : (k + 1) * block]

    def core_copies(k):
        return (
            pltpu.make_async_remote_copy(
                din_out(k), din_got.at[k], d_send.at[k], d_recv.at[k], other, mesh_ids
            ),
            pltpu.make_async_remote_copy(
                dout_out(k),
                dout_got.at[k],
                d_send.at[x_axis + k],
                d_recv.at[x_axis + k],
                other,
                mesh_ids,
            ),
        )

    tile = 256 if block % 256 == 0 else 128

    def in_grads(k, for_core, out, got):
        start = block_start(k, for_core)
        columns = slice(out * block, (out + 1) * block)
        for at in range(0, width, tile):
            part = slice(at, at + tile)
            value = mm_rows(x_all[:, part], grad_pre[:, pl.ds(start, block)])
            if got is not None:
                value = value + din_got[got, part, :].astype(F32)
            w_in[part, columns] = value.astype(BF16)

    def out_grads(k, for_core, out, got):
        start = block_start(k, for_core)
        for at in range(0, block, tile):
            value = mm_rows(active[:, pl.ds(pl.multiple_of(start + at, 128), tile)], up_all[...])
            if got is not None:
                value = value + dout_got[got, at : at + tile, :].astype(F32)
            w_out[out * block + at : out * block + at + tile, :] = value.astype(BF16)

    def x_copies(k):
        return (
            pltpu.make_async_remote_copy(
                din_out(x_axis + k), din_refs[k], e_send.at[k], e_recv.at[k], x_peer(k), mesh_ids
            ),
            pltpu.make_async_remote_copy(
                dout_out(x_axis + k),
                dout_refs[k],
                e_send.at[x_axis + k],
                e_recv.at[x_axis + k],
                x_peer(k),
                mesh_ids,
            ),
        )

    for k in [*range(1, x_axis), 0]:
        in_copy, out_copy_k = core_copies(k)
        in_grads(k, 1 - core, k, None)
        in_copy.start()
        out_grads(k, 1 - core, k, None)
        out_copy_k.start()
        in_copy.wait_recv()
        in_grads(k, core, x_axis + k, k)
        if k:
            x_copies(k)[0].start()
        out_copy_k.wait_recv()
        out_grads(k, core, x_axis + k, k)
        if k:
            x_copies(k)[1].start()
    for i, (src, ref) in enumerate(
        ((din_out(x_axis), din_refs[0]), (dout_out(x_axis), dout_refs[0]))
    ):
        store = pltpu.make_async_copy(src, ref, store_sem.at[2 + experts + i])
        store.start()
        stores.append(store)
    for k in range(1, x_axis):
        for copy in x_copies(k):
            copy.wait()
    for store in stores:
        store.wait()
    for k in range(x_axis):
        for copy in core_copies(k):
            copy.wait_send()

    def finish(s, carry):
        for copy in out_copy(s):
            copy.wait_send()
        for copy in home_copy(s):
            copy.wait()
        return carry

    lax.fori_loop(1, experts, finish, 0)


def expert(x, gates, up, w_in, w_out, dp_size):
    experts, cap, width = x.shape
    hidden = w_in.shape[1]
    slots = experts * cap
    x_axis = dp_size // 2
    block = hidden // dp_size
    anywhere = pl.BlockSpec(memory_space=pl.ANY)
    rows = jax.ShapeDtypeStruct((experts, cap, width), BF16)
    out_shape = (
        [rows, jax.ShapeDtypeStruct((experts, 8, cap), F32), rows]
        + [jax.ShapeDtypeStruct((width, block), BF16)] * x_axis
        + [jax.ShapeDtypeStruct((block, width), BF16)] * x_axis
    )
    chunks = pltpu.VMEM((experts, cap, width), BF16)
    lines = pltpu.VMEM((experts, 8, cap), F32)
    sems = pltpu.SemaphoreType.DMA
    out = pl.pallas_call(
        functools.partial(expert_kernel, experts, x_axis),
        in_specs=[anywhere] * 5,
        out_specs=[anywhere] * len(out_shape),
        out_shape=out_shape,
        scratch_shapes=[
            chunks,
            chunks,
            lines,
            chunks,
            lines,
            chunks,
            pltpu.VMEM((slots, hidden), BF16),
            pltpu.VMEM((slots, hidden), BF16),
            pltpu.VMEM((width, hidden), BF16),
            pltpu.VMEM((hidden, width), BF16),
            pltpu.VMEM((x_axis, width, block), BF16),
            pltpu.VMEM((x_axis, block, width), BF16),
            sems((5,)),
        ]
        + [sems((experts,))] * 8
        + [sems((2 * x_axis,))] * 4
        + [sems((4 + experts,))],
        compiler_params=pltpu.CompilerParams(
            vmem_limit_bytes=63 * MIB, collective_id=0, has_side_effects=True
        ),
        cost_estimate=cost(12 * slots * width * hidden, 8 * width * hidden),
        name="expert",
    )(x, gates, w_in, w_out, up)
    back, gate_grads, made = out[:3]
    din = out[3 : 3 + x_axis]
    dout = out[3 + x_axis :]
    return back, gate_grads, made, din, dout


def store_tiles(out_ref, value):
    for tile in range(out_ref.shape[0]):
        out_ref[tile] = value[:, tile * 128 : (tile + 1) * 128].astype(BF16)


def middle_back_kernel(
    experts, cap, back_ref, gate_grads_ref, lines_ref, hidden_ref, cot_ref, mixed_ref, wo_ref,
    gain_ref, bias_ref, proj_ref, embed_ref,
    grad_hidden_ref, grad_mixed_ref, delta_ref, dwo_ref, small_ref,
    dwo_sum, dproj_sum, dembed_sum, gate_parts, proj_parts,
):
    step = pl.program_id(0)
    rows, width = hidden_ref.shape
    slots = back_ref.shape[0]

    @pl.when(step == 0)
    def _():
        small_ref[...] = jnp.zeros_like(small_ref)
        dwo_sum[...] = jnp.zeros_like(dwo_sum)
        dproj_sum[...] = jnp.zeros_like(dproj_sum)
        dembed_sum[...] = jnp.zeros_like(dembed_sum)
        high, rest = split_two(proj_ref[...])
        proj_parts[:, 0:128] = high
        proj_parts[:, 128:256] = rest
        line = iota((16, cap), 0)
        for e in range(experts):
            grads = gate_grads_ref[e, 0:1, :]
            high = grads.astype(BF16).astype(F32)
            mid = (grads - high).astype(BF16).astype(F32)
            rest = grads - high - mid
            split = jnp.where(line == 0, high, jnp.where(line == 1, mid, rest))
            gate_parts[:, e * cap : (e + 1) * cap] = jnp.where(line < 3, split, 0.0).astype(BF16)

    heads = width // HEAD_DIM
    pairs = heads // 2
    head_of = iota((8 * pairs, width), 1) // HEAD_DIM
    line = iota((8 * pairs, width), 0)
    head_lines = one_hot((head_of == line // 8 * 2 + line % 8) & (line % 8 < 2))
    pick = one_hot(iota((rows, slots), 1) == col_of(lines_ref[0:1, :]))
    grad = mm(pick, back_ref[...])
    gate_grad = jnp.sum(mm_cols(pick, gate_parts[...]), 1, keepdims=True)
    unit, scale = norm_parts(hidden_ref[...])
    normed = unit * gain_ref[...] + bias_ref[...]
    gate, probs, chosen, low, low_squares, low_scale, low_unit, _, _, table = router_parts(
        normed, proj_parts, embed_ref[...], col_of(lines_ref[2:3, :]), experts
    )
    grad_logits = (gate_grad * gate * (chosen - probs) / SHARPNESS).astype(BF16)
    grad_unit = mm(grad_logits, table.astype(BF16))
    dembed_sum[...] += mm_rows(grad_logits, low_unit.astype(BF16))
    grad_low = clipped_back(grad_unit, low, low_scale, low_squares).astype(BF16)
    dproj_sum[...] += mm_rows(grad_low, normed.astype(BF16))
    grad = grad + mm_cols(grad_low, proj_parts[:, 0:128])
    small_ref[0:1, :] += jnp.sum(grad * unit, 0, keepdims=True)
    small_ref[1:2, :] += jnp.sum(grad, 0, keepdims=True)
    grad_hidden = cot_ref[...].astype(F32) + norm_back(grad, gain_ref[...], unit, scale)
    grad_hidden_ref[...] = grad_hidden
    low_grad = grad_hidden.astype(BF16)
    grad_mixed = mm_cols(low_grad, wo_ref[...]).astype(BF16)
    grad_mixed_ref[...] = grad_mixed
    dwo_sum[...] += mm_rows(mixed_ref[...], low_grad)
    high, rest = split_two(grad_mixed.astype(F32) * mixed_ref[...].astype(F32))
    sums = mm_cols(head_lines, high) + mm_cols(head_lines, rest)
    for p in range(pairs):
        delta_ref[p] = sums[8 * p : 8 * p + 8, :]

    @pl.when(step == pl.num_programs(0) - 1)
    def _():
        embed = embed_ref[...]
        squares = jnp.sum(embed * embed, -1, keepdims=True)
        table_scale = lax.rsqrt(jnp.maximum(squares, 1.0))
        dembed = clipped_back(dembed_sum[...], embed, table_scale, squares)
        lines_proj = small_ref.shape[0] - 8 - max(8, experts)
        small_ref[8 : 8 + lines_proj, :] = dproj_sum[0:lines_proj, :]
        small_ref[8 + lines_proj :, 0:128] = dembed[0 : max(8, experts), :]
        store_tiles(dwo_ref, dwo_sum[...])


def middle_back(
    back, gate_grads, lines, hidden, cot, mixed, wo, gain, bias, proj, embed, space, experts, cap
):
    tokens, width = hidden.shape
    slots = experts * cap
    rows = 256
    back = back.reshape(slots, width)
    block = pl.BlockSpec((rows, width), lambda i: (i, 0))
    tiles = width // 128
    small_shape = (8 + space + max(8, experts), width)
    args = (back, gate_grads, lines, hidden, cot, mixed, wo, gain, bias, proj, embed)
    return pl.pallas_call(
        functools.partial(middle_back_kernel, experts, cap),
        grid=(tokens // rows,),
        in_specs=[
            spec_all(back.shape),
            spec_all(gate_grads.shape),
            pl.BlockSpec((8, rows), lambda i: (0, i)),
            block,
            block,
            block,
        ]
        + [spec_all(a.shape) for a in args[6:]],
        out_specs=[
            block,
            block,
            pl.BlockSpec((tiles, 8, rows), lambda i: (0, 0, i)),
            spec_all((tiles, width, 128)),
            spec_all(small_shape),
        ],
        out_shape=[
            jax.ShapeDtypeStruct((tokens, width), F32),
            jax.ShapeDtypeStruct((tokens, width), BF16),
            jax.ShapeDtypeStruct((tiles, 8, tokens), F32),
            jax.ShapeDtypeStruct((tiles, width, 128), BF16),
            jax.ShapeDtypeStruct(small_shape, F32),
        ],
        scratch_shapes=[
            pltpu.VMEM((width, width), F32),
            pltpu.VMEM((128, width), F32),
            pltpu.VMEM((128, 128), F32),
            pltpu.VMEM((16, slots), BF16),
            pltpu.VMEM((width, 256), BF16),
        ],
        compiler_params=params(),
        cost_estimate=cost(2 * tokens * width * (2 * width + slots), 20 * tokens * width),
        name="middle_back",
    )(*args)


def qkv_back_kernel(
    x_ref, gain_ref, bias_ref, grad_hidden_ref, dq_ref, dk_ref, dv_ref, wq_ref, wk_ref, wv_ref,
    grad_ref, dwq_ref, dwk_ref, dwv_ref, small_ref, low_ref,
):
    tokens, width = x_ref.shape
    rows = 256
    small_ref[...] = jnp.zeros_like(small_ref)

    def row_block(i, carry):
        at = pl.ds(pl.multiple_of(i * rows, rows), rows)
        unit, scale = norm_parts(x_ref[at, :].astype(F32))
        low_ref[at, :] = (unit * gain_ref[...] + bias_ref[...]).astype(BF16)
        grad = (
            mm_cols(dq_ref[at, :], wq_ref[...])
            + mm_cols(dk_ref[at, :], wk_ref[...])
            + mm_cols(dv_ref[at, :], wv_ref[...])
        )
        small_ref[0:1, :] += jnp.sum(grad * unit, 0, keepdims=True)
        small_ref[1:2, :] += jnp.sum(grad, 0, keepdims=True)
        grad_ref[at, :] = grad_hidden_ref[at, :] + norm_back(grad, gain_ref[...], unit, scale)
        return carry

    lax.fori_loop(0, tokens // rows, row_block, 0)
    low = low_ref[...]
    store_tiles(dwq_ref, mm_rows(low, dq_ref[...]))
    store_tiles(dwk_ref, mm_rows(low, dk_ref[...]))
    store_tiles(dwv_ref, mm_rows(low, dv_ref[...]))


def qkv_back(x, gain, bias, grad_hidden, dq, dk, dv, wq, wk, wv):
    tokens, width = x.shape
    square = jax.ShapeDtypeStruct((width // 128, width, 128), BF16)
    return pl.pallas_call(
        qkv_back_kernel,
        out_shape=[
            jax.ShapeDtypeStruct((tokens, width), F32),
            square,
            square,
            square,
            jax.ShapeDtypeStruct((8, width), F32),
        ],
        scratch_shapes=[pltpu.VMEM((tokens, width), BF16)],
        compiler_params=params(),
        cost_estimate=cost(12 * tokens * width * width, 20 * tokens * width),
        name="qkv_back",
    )(x, gain, bias, grad_hidden, dq, dk, dv, wq, wk, wv)


def add_rows(rows, out_ref, out_at, terms):
    step = next(step for step in (320, 160, 80, 48, 16) if rows % step == 0)

    def body(i, carry):
        at = i * step
        total = None
        for ref, start in terms:
            value = ref[pl.ds(pl.multiple_of(start + at, 16), step), :].astype(F32)
            total = value if total is None else total + value
        out_ref[pl.ds(pl.multiple_of(out_at + at, 16), step), :] = total.astype(out_ref.dtype)
        return carry

    lax.fori_loop(0, rows // step, body, 0)


def can_reduce(width, space, dp_size, experts):
    spare = chunk_rows(width, dp_size, experts) - 3 * width
    lines2 = 8 + space + max(8, experts)
    return (
        width // 128 % 2 == 0
        and 64 * dp_size * experts <= 3 * width
        and spare >= width // 128 * lines2
    )


def chunk_rows(width, dp_size, experts):
    unit = 16 * dp_size * experts
    return -(-3 * width // unit) * unit


def tail_kernel(
    x_axis, experts, longest,
    x_ref, vecs_ref, tables_ref, lines_ref, gate_grads_ref, gate_ref,
    q_hbm, k_hbm, v_hbm, wq_hbm, wk_hbm, wv_hbm, wo_hbm, probs_ref, back_hbm, hidden_hbm,
    cot_hbm, mixed_hbm, made_hbm,
    grad_hbm, sums_hbm, output_hbm, small_out, small_out2,
    q_ref, k_ref, v_ref, do_ref, weights, out_ref, made_home, hidden_part, delta_ref, small_ref,
    dproj_sum, dembed_sum, gate_parts, proj_parts,
    dq_all, dk_all, dv_all, normed_t, prob_buf, dk_sum, dv_sum, grads, grad_hidden, small_in,
    core_got, core_sum, plane_got, plane_sum, line_got, small_got,
    load_sem, prob_sem, sums_sem, grad_sem, hidden_sem, made_send, made_recv,
    core_send, core_recv, plane_send, plane_recv, line_send, line_recv,
    line_back_send, line_back_recv, plane_back_send, plane_back_recv,
    core_back_send, core_back_recv, small_send, small_recv,
):
    tokens, width = x_ref.shape
    pairs = width // PAIR
    n = grads.shape[0]
    block_rows = 256
    dp = lax.axis_index("dp")
    me = lax.axis_index("expert")
    core = lax.rem(dp, 2)
    x_at = dp // 2
    low = lax.rem(me, 2)
    high = me // 2
    planes, lines = 2 * x_axis, experts // 2
    mesh_ids = pl.DeviceIdType.MESH
    rows = grads.shape[1]
    half = rows // 2
    quarter = half // planes
    piece = quarter // lines
    plane_at = x_at * 2 + low

    other_core = {"dp": dp + 1 - 2 * core}

    def plane_peer(j):
        at = lax.rem(plane_at + j, planes)
        return at, (2 * (at // 2) + core, 2 * high + lax.rem(at, 2))

    def line_peer(j):
        at = lax.rem(high + j, lines)
        return at, {"expert": 2 * at + low}

    barrier = pltpu.get_barrier_semaphore()
    pl.semaphore_signal(barrier, inc=1, device_id=other_core, device_id_type=mesh_ids)
    for j in range(1, planes):
        pl.semaphore_signal(barrier, inc=1, device_id=plane_peer(j)[1], device_id_type=mesh_ids)
    for j in range(1, lines):
        pl.semaphore_signal(barrier, inc=1, device_id=line_peer(j)[1], device_id_type=mesh_ids)

    def expert_peer(j):
        return lax.rem(me + j, experts)

    for j in range(1, experts):
        pl.semaphore_signal(
            barrier, inc=1, device_id={"expert": expert_peer(j)}, device_id_type=mesh_ids
        )

    def remote(src, dst, send, recv, to):
        return pltpu.make_async_remote_copy(src, dst, send, recv, to, mesh_ids)

    def rows_at(start, size):
        return pl.ds(pl.multiple_of(start, 16), size)

    def core_copy(c):
        src = grads.at[c, rows_at((1 - core) * half, half)]
        return [remote(src, core_got.at[c], core_send.at[c], core_recv.at[c], other_core)]

    def plane_copies(c):
        made = []
        for j in range(1, planes):
            at, to = plane_peer(j)
            src = core_sum.at[c, rows_at(at * quarter, quarter)]
            made.append(
                remote(src, plane_got.at[c, j - 1], plane_send.at[c, j], plane_recv.at[c, j], to)
            )
        return made

    def line_copies(c):
        made = []
        for j in range(1, lines):
            at, to = line_peer(j)
            src = plane_sum.at[c, rows_at(at * piece, piece)]
            made.append(remote(src, line_got.at[c, j - 1], line_send.at[c, j], line_recv.at[c, j], to))
        return made

    base = core * half + plane_at * quarter

    def line_back(c):
        at = rows_at(base + high * piece, piece)
        made = []
        for j in range(1, lines):
            to = line_peer(j)[1]
            made.append(
                remote(
                    out_ref.at[c, at],
                    out_ref.at[c, at],
                    line_back_send.at[c, j],
                    line_back_recv.at[c, j],
                    to,
                )
            )
        return made

    def plane_back(c):
        at = rows_at(base, quarter)
        made = []
        for j in range(1, planes):
            to = plane_peer(j)[1]
            made.append(
                remote(
                    out_ref.at[c, at],
                    out_ref.at[c, at],
                    plane_back_send.at[c, j],
                    plane_back_recv.at[c, j],
                    to,
                )
            )
        return made

    def core_back(c):
        at = rows_at(core * half, half)
        return [
            remote(
                out_ref.at[c, at],
                out_ref.at[c, at],
                core_back_send.at[c],
                core_back_recv.at[c],
                other_core,
            )
        ]

    def small_copies(stage):
        made = []
        if stage == 0:
            made.append(
                remote(
                    small_got.at[0, 0],
                    small_got.at[0, 1],
                    small_send.at[0, 1],
                    small_recv.at[0, 1],
                    other_core,
                )
            )
        else:
            for j in range(1, planes if stage == 1 else lines):
                to = plane_peer(j)[1] if stage == 1 else line_peer(j)[1]
                made.append(
                    remote(
                        small_got.at[stage, 0],
                        small_got.at[stage, j],
                        small_send.at[stage, j],
                        small_recv.at[stage, j],
                        to,
                    )
                )
        return made

    def start(copies):
        for copy in copies:
            copy.start()

    def received(copies):
        for copy in copies:
            copy.wait_recv()

    def ordered(got, at, count):
        total = None
        for i in range(count):
            value = got(lax.rem(at + count - i, count))
            total = value if total is None else total + value
        return total

    def stage_run(stage, c):
        if stage == 0:
            start(core_copy(c))
        elif stage == 1:
            received(core_copy(c))
            add_rows(
                half, core_sum.at[c], 0, [(grads.at[c], core * half), (core_got.at[c], 0)]
            )
            start(plane_copies(c))
        elif stage == 2:
            received(plane_copies(c))
            add_rows(
                quarter,
                plane_sum.at[c],
                0,
                [(core_sum.at[c], plane_at * quarter)]
                + [(plane_got.at[c, j - 1], 0) for j in range(1, planes)],
            )
            start(line_copies(c))
        elif stage == 3:
            received(line_copies(c))
            add_rows(
                piece,
                out_ref.at[c],
                base + high * piece,
                [(plane_sum.at[c], high * piece)]
                + [(line_got.at[c, j - 1], 0) for j in range(1, lines)],
            )
            start(line_back(c))
        elif stage == 4:
            received(line_back(c))
            start(plane_back(c))
        elif stage == 5:
            received(plane_back(c))
            start(core_back(c))
        else:
            received(core_back(c))
            sums_copy(c).start()

    def sums_copy(c):
        return pltpu.make_async_copy(out_ref.at[c], sums_hbm.at[c], sums_sem.at[c])

    def small_run(stage):
        if stage == 0:
            small_got[0, 0] = small_in[...]
            start(small_copies(0))
        elif stage == 1:
            received(small_copies(0))
            small_got[1, 0] = small_got[0, 0] + small_got[0, 1]
            start(small_copies(1))
        elif stage == 2:
            received(small_copies(1))
            small_got[2, 0] = ordered(lambda j: small_got[1, j], plane_at, planes)
            start(small_copies(2))
        elif stage == 3:
            received(small_copies(2))
            small_out[...] = ordered(lambda j: small_got[2, j], high, lines)


    def prob_copy(p, slot):
        return pltpu.make_async_copy(
            probs_ref.at[pl.ds(2 * p, 2)], prob_buf.at[slot], prob_sem.at[slot]
        )

    full = 3 * width
    experts_cap = made_home.shape[1]
    slots = experts * experts_cap
    gain1, bias1 = vecs_ref[0:1, :], vecs_ref[1:2, :]
    gain2, bias2 = vecs_ref[2:3, :], vecs_ref[3:4, :]
    back_buf = prob_buf.at[1, :, :, 0:width]
    sources = [
        (back_hbm, back_buf),
        (hidden_hbm, grad_hidden),
        (cot_hbm, dq_all),
        (mixed_hbm, dv_all),
        (wo_hbm, weights.at[3]),
        (q_hbm, q_ref),
        (k_hbm, k_ref),
        (v_hbm, v_ref),
        (wq_hbm, weights.at[0]),
        (wk_hbm, weights.at[1]),
        (wv_hbm, weights.at[2]),
        (made_hbm.at[me], made_home.at[me]),
    ]
    loads = [
        pltpu.make_async_copy(src, dst, load_sem.at[i]) for i, (src, dst) in enumerate(sources)
    ]
    for load in loads:
        load.start()
    prob_copy(0, 0).start()
    pl.semaphore_wait(barrier, planes + lines - 1 + experts - 1)

    parts = PARTS * (experts - 1)
    early = min(PARTS_EARLY, parts)

    def made_copy(m):
        to = expert_peer(distance(experts, m // PARTS + 1))
        at = rows_at(m % PARTS * (experts_cap // PARTS), experts_cap // PARTS)
        return remote(
            made_hbm.at[to, at],
            made_home.at[me, at],
            made_send.at[m],
            made_recv.at[m],
            {"expert": to},
        )

    def made_start(m, carry):
        made_copy(m).start()
        return carry

    def made_received(m, carry):
        made_copy(m).wait_recv()
        return carry

    def made_sent(m, carry):
        made_copy(m).wait_send()
        return carry

    lax.fori_loop(0, early, made_start, 0)

    for c in range(n):
        grads[c, full:rows, :] = jnp.zeros((rows - full, 128), BF16)
    small_ref[...] = jnp.zeros_like(small_ref)
    dproj_sum[...] = jnp.zeros_like(dproj_sum)
    dembed_sum[...] = jnp.zeros_like(dembed_sum)
    upper, rest = split_two(tables_ref[0:width, :])
    proj_parts[:, 0:128] = upper
    proj_parts[:, 128:256] = rest
    split_line = iota((16, experts_cap), 0)
    for e in range(experts):
        line_grads = gate_grads_ref[e, 0:1, :]
        upper = line_grads.astype(BF16).astype(F32)
        mid = (line_grads - upper).astype(BF16).astype(F32)
        rest = line_grads - upper - mid
        split = jnp.where(split_line == 0, upper, jnp.where(split_line == 1, mid, rest))
        gate_parts[:, e * experts_cap : (e + 1) * experts_cap] = jnp.where(
            split_line < 3, split, 0.0
        ).astype(BF16)
    head_of = iota((8 * pairs, width), 1) // HEAD_DIM
    line = iota((8 * pairs, width), 0)
    head_lines = one_hot((head_of == line // 8 * 2 + line % 8) & (line % 8 < 2))
    embed = tables_ref[width:, :]
    for load in loads[0:5]:
        load.wait()

    def middle_block(i, carry):
        at = pl.ds(pl.multiple_of(i * block_rows, block_rows), block_rows)
        pick = one_hot(iota((block_rows, slots), 1) == col_of(lines_ref[0:1, at]))
        grad = mm(pick[:, 0:tokens], prob_buf[1, 0, :, 0:width])
        grad = grad + mm(pick[:, tokens:], prob_buf[1, 1, :, 0:width])
        gate_grad = jnp.sum(mm_cols(pick, gate_parts[...]), 1, keepdims=True)
        unit, unit_scale = norm_parts(grad_hidden[at, :])
        normed = unit * gain2 + bias2
        gate, probs, chosen, low, low_squares, low_scale, low_unit, _, _, table = router_parts(
            normed, proj_parts, embed, col_of(lines_ref[2:3, at]), experts
        )
        grad_logits = (gate_grad * gate * (chosen - probs) / SHARPNESS).astype(BF16)
        grad_unit = mm(grad_logits, table.astype(BF16))
        dembed_sum[...] += mm_rows(grad_logits, low_unit.astype(BF16))
        grad_low = clipped_back(grad_unit, low, low_scale, low_squares).astype(BF16)
        dproj_sum[...] += mm_rows(grad_low, normed.astype(BF16))
        grad = grad + mm_cols(grad_low, proj_parts[:, 0:128])
        small_ref[0:1, :] += jnp.sum(grad * unit, 0, keepdims=True)
        small_ref[1:2, :] += jnp.sum(grad, 0, keepdims=True)
        total_grad = dq_all[at, :].astype(F32) + norm_back(grad, gain2, unit, unit_scale)
        grad_hidden[at, :] = total_grad
        low_grad = total_grad.astype(BF16)
        dk_all[at, :] = low_grad
        grad_mixed = mm_cols(low_grad, weights[3]).astype(BF16)
        do_ref[at, :] = grad_mixed
        high, rest = split_two(grad_mixed.astype(F32) * dv_all[at, :].astype(F32))
        lines_sum = mm_cols(head_lines, high) + mm_cols(head_lines, rest)
        for p in range(pairs):
            delta_ref[p, :, at] = lines_sum[8 * p : 8 * p + 8, :]
        return carry

    lax.fori_loop(0, tokens // block_rows, middle_block, 0)
    squares = jnp.sum(embed * embed, -1, keepdims=True)
    table_scale = lax.rsqrt(jnp.maximum(squares, 1.0))
    dembed = clipped_back(dembed_sum[...], embed, table_scale, squares)
    lines2 = small_ref.shape[0]
    lines_proj = lines2 - 8 - max(8, experts)
    small_ref[8 : 8 + lines_proj, :] = dproj_sum[0:lines_proj, :]
    small_ref[8 + lines_proj :, 0:128] = dembed[0 : max(8, experts), :]
    for tile in range(width // 128):
        at = full + tile * lines2
        grads[0, at : at + lines2, :] = small_ref[:, tile * 128 : (tile + 1) * 128].astype(BF16)
    half_tiles = width // 256
    for wide in range(half_tiles):
        made = mm_rows(dv_all[...], dk_all[:, wide * 256 : (wide + 1) * 256]).astype(BF16)
        for i in range(2):
            tile = 2 * wide + i
            start_at = tile % half_tiles * width
            grads[tile // half_tiles, start_at : start_at + width, :] = made[
                :, i * 128 : (i + 1) * 128
            ]
        if wide == (half_tiles - 1) // 2:
            stage_run(0, 0)
    for at in range(0, tokens, block_rows):
        part = slice(at, at + block_rows)
        unit, _ = norm_parts(x_ref[part, :].astype(F32))
        normed = unit * gain1 + bias1
        normed_t[:, part] = normed.T.astype(BF16)
    stage_run(1, 0)
    stage_run(0, 1)
    for load in loads[5:8]:
        load.wait()
    scale = HEAD_DIM**-0.5
    lane = iota((tokens, PAIR), 1)
    own = (lane < HEAD_DIM, lane >= HEAD_DIM)
    zero = jnp.zeros((), BF16)

    def pair_step(p, carry):
        slot = lax.rem(p, 2)
        prob_copy(p, slot).wait()

        @pl.when(p < pairs - 1)
        def _():
            prob_copy(p + 1, 1 - slot).start()

        lanes = pl.ds(pl.multiple_of(p * PAIR, PAIR), PAIR)
        dk_sum[...] = jnp.zeros_like(dk_sum)
        dv_sum[...] = jnp.zeros_like(dv_sum)
        for block in range(tokens // block_rows):
            first, last = key_window(block, block_rows, tokens, longest)
            mine = slice(block * block_rows, (block + 1) * block_rows)
            values = v_ref[first:last, lanes]
            keys = k_ref[first:last, lanes]
            queries = q_ref[mine, lanes]
            grad_out = do_ref[mine, lanes]
            dq = jnp.zeros((block_rows, PAIR), F32)
            dk = jnp.zeros((last - first, PAIR), F32)
            dv = jnp.zeros((last - first, PAIR), F32)
            for h in range(2):
                do_h = jnp.where(own[h][mine], grad_out, zero)
                q_h = jnp.where(own[h][mine], queries, zero)
                k_h = jnp.where(own[h][first:last], keys, zero)
                probs = prob_buf[slot, h, first:last, mine]
                grad_probs = mm_cols(values, do_h)
                grad_scores = (
                    probs.astype(F32) * (grad_probs - delta_ref[p, h : h + 1, mine])
                ).astype(BF16)
                dq = dq + mm_rows(grad_scores, k_h)
                dk = dk + mm(grad_scores, q_h)
                dv = dv + mm(probs, do_h)
            dq_all[mine, lanes] = (dq * scale).astype(BF16)
            dk_sum[first:last, :] += dk
            dv_sum[first:last, :] += dv
        dk_all[:, lanes] = (dk_sum[...] * scale).astype(BF16)
        dv_all[:, lanes] = dv_sum[...].astype(BF16)
        first_part = jnp.minimum(early + p * PARTS_LOOP, parts)
        last_part = jnp.minimum(early + (p + 1) * PARTS_LOOP, parts)
        lax.fori_loop(first_part, last_part, made_start, 0)
        for w, ref in enumerate((dq_all, dk_all, dv_all)):
            made = mm(normed_t[...], ref[:, lanes]).astype(BF16)
            grads[p + 2, w * width : (w + 1) * width, :] = made
        for stage in reversed(range(7)):
            if stage <= 2:
                stage_run(stage, p + 2 - stage)
            else:

                @pl.when(p + 2 >= stage)
                def _(stage=stage):
                    stage_run(stage, p + 2 - stage)

        return carry

    lax.fori_loop(0, pairs, pair_step, 0)
    for load in loads[8:]:
        load.wait()
    small_in[...] = jnp.zeros_like(small_in)

    def row_block(i):
        at = slice(i * block_rows, (i + 1) * block_rows)
        unit, unit_scale = norm_parts(x_ref[at, :].astype(F32))
        grad = (
            mm_cols(dq_all[at, :], weights[0])
            + mm_cols(dk_all[at, :], weights[1])
            + mm_cols(dv_all[at, :], weights[2])
        )
        small_in[0:1, :] += jnp.sum(grad * unit, 0, keepdims=True)
        small_in[1:2, :] += jnp.sum(grad, 0, keepdims=True)
        grad_hidden[at, :] += norm_back(grad, gain1, unit, unit_scale)

    grad_copy = pltpu.make_async_copy(grad_hidden, grad_hbm, grad_sem.at[0])

    def hidden_copy(i):
        at = slice(i * block_rows, (i + 1) * block_rows)
        return pltpu.make_async_copy(hidden_hbm.at[at], hidden_part.at[i % 2], hidden_sem.at[i % 2])

    output_copy = pltpu.make_async_copy(do_ref, output_hbm, grad_sem.at[1])

    def output_block(i):
        at = slice(i * block_rows, (i + 1) * block_rows)
        if i == 0:
            lax.fori_loop(0, parts, made_received, 0)
        hidden_copy(i).wait()
        if i + 1 < tokens // block_rows:
            hidden_copy(i + 1).start()
        slot = col_of(lines_ref[1:2, at])
        pick = one_hot(iota((block_rows, slots), 1) == slot)
        produced = jnp.zeros((block_rows, width), F32)
        for e in range(experts):
            produced = produced + mm(
                pick[:, e * experts_cap : (e + 1) * experts_cap], made_home[e]
            )
        total = hidden_part[i % 2] + gate_ref[at, 0:1] * produced
        do_ref[at, :] = total.astype(BF16)

    hidden_copy(0).start()

    blocks = tokens // block_rows
    done = 0
    out_done = 0
    small_at = 0
    next_part = min(early + pairs * PARTS_LOOP, parts)
    for tick in range(pairs + 1, pairs + 8):
        if next_part < parts:
            some = min(parts, next_part + PARTS_DRAIN)
            lax.fori_loop(next_part, some, made_start, 0)
            next_part = some
        for _ in range(2):
            if done < blocks:
                row_block(done)
                done += 1
                if done == blocks:
                    grad_copy.start()
            elif out_done < blocks and tick > pairs + OUTPUT_TICK and next_part == parts:
                output_block(out_done)
                out_done += 1
                if out_done == blocks:
                    output_copy.start()
        for stage in reversed(range(7)):
            c = tick + 1 - stage
            if 0 <= c < n:
                stage_run(stage, c)
        if done == blocks and small_at < 4:
            small_run(small_at)
            small_at += 1
    while done < blocks:
        row_block(done)
        done += 1
        if done == blocks:
            grad_copy.start()
    lax.fori_loop(next_part, parts, made_start, 0)
    while out_done < blocks:
        output_block(out_done)
        out_done += 1
        if out_done == blocks:
            output_copy.start()
    while small_at < 4:
        small_run(small_at)
        small_at += 1
    for tile in range(width // 128):
        at = full + tile * lines2
        small_out2[:, tile * 128 : (tile + 1) * 128] = out_ref[0, at : at + lines2, :].astype(F32)
    grad_copy.wait()
    output_copy.wait()
    for c in range(n):
        sums_copy(c).wait()
    lax.fori_loop(0, parts, made_sent, 0)
    for stage in range(3):
        for copy in small_copies(stage):
            copy.wait_send()

    def sent(c, carry):
        for made in (core_copy, plane_copies, line_copies, line_back, plane_back, core_back):
            for copy in made(c):
                copy.wait_send()
        return carry

    lax.fori_loop(0, n, sent, 0)


def tail(
    x, vecs, tables, lines, gate_grads, gate, q, k, v, wq, wk, wv, wo, probs, back, hidden, cot,
    mixed, made, space, longest, dp_size, experts,
):
    tokens, width = x.shape
    pairs = width // PAIR
    n = 2 + pairs
    rows = chunk_rows(width, dp_size, experts)
    x_axis, members, planes = dp_size // 2, experts // 2, dp_size
    half = rows // 2
    quarter = half // planes
    piece = quarter // members
    most = max(planes, members)
    small_shape = (8, width)
    cap = made.shape[1]
    small2_shape = (8 + space + max(8, experts), width)
    block_rows = 256
    sems = pltpu.SemaphoreType.DMA
    local = pl.BlockSpec(memory_space=pltpu.VMEM)
    anywhere = pl.BlockSpec(memory_space=pl.ANY)
    low = pltpu.VMEM((tokens, width), BF16)
    return pl.pallas_call(
        functools.partial(tail_kernel, x_axis, experts, longest),
        in_specs=[local] * 6 + [anywhere] * 13,
        out_specs=[anywhere] * 3 + [local] * 2,
        out_shape=[
            jax.ShapeDtypeStruct((tokens, width), F32),
            jax.ShapeDtypeStruct((n, rows, 128), BF16),
            jax.ShapeDtypeStruct((tokens, width), BF16),
            jax.ShapeDtypeStruct(small_shape, F32),
            jax.ShapeDtypeStruct(small2_shape, F32),
        ],
        scratch_shapes=[
            low,
            low,
            low,
            low,
            pltpu.VMEM((4, width, width), BF16),
            pltpu.VMEM((n, rows, 128), BF16),
            pltpu.VMEM((experts, cap, width), BF16),
            pltpu.VMEM((2, block_rows, width), F32),
            pltpu.VMEM((pairs, 8, tokens), F32),
            pltpu.VMEM(small2_shape, F32),
            pltpu.VMEM((128, width), F32),
            pltpu.VMEM((128, 128), F32),
            pltpu.VMEM((16, experts * cap), BF16),
            pltpu.VMEM((width, 256), BF16),
            low,
            low,
            low,
            pltpu.VMEM((width, tokens), BF16),
            pltpu.VMEM((2, 2, tokens, tokens), BF16),
            pltpu.VMEM((tokens, PAIR), F32),
            pltpu.VMEM((tokens, PAIR), F32),
            pltpu.VMEM((n, rows, 128), BF16),
            pltpu.VMEM((tokens, width), F32),
            pltpu.VMEM(small_shape, F32),
            pltpu.VMEM((n, half, 128), BF16),
            pltpu.VMEM((n, half, 128), BF16),
            pltpu.VMEM((n, planes - 1, quarter, 128), BF16),
            pltpu.VMEM((n, quarter, 128), BF16),
            pltpu.VMEM((n, members - 1, piece, 128), BF16),
            pltpu.VMEM((3, most, *small_shape), F32),
            sems((12,)),
            sems((2,)),
            sems((n,)),
            sems((2,)),
            sems((2,)),
            sems((PARTS * (experts - 1),)),
            sems((PARTS * (experts - 1),)),
        ]
        + [sems((n,))] * 2
        + [sems((n, planes))] * 2
        + [sems((n, members))] * 4
        + [sems((n, planes))] * 2
        + [sems((n,))] * 2
        + [sems((3, most))] * 2,
        compiler_params=pltpu.CompilerParams(
            vmem_limit_bytes=63 * MIB, collective_id=1, has_side_effects=True
        ),
        cost_estimate=cost(16 * pairs * tokens * tokens * 256, 4 * pairs * tokens * tokens),
        name="tail",
    )(
        x, vecs, tables, lines, gate_grads, gate, q, k, v, wq, wk, wv, wo, probs,
        back.reshape(2, tokens, width), hidden, cot, mixed, made,
    )


def finish_kernel(x_axis, *refs):
    sums_refs = refs[:3]
    din_refs = refs[3 : 3 + x_axis]
    dout_refs = refs[3 + x_axis : 3 + 2 * x_axis]
    dwo_ref, dwq_ref, dwk_ref, dwv_ref, din_ref, dout_ref = refs[3 + 2 * x_axis :]
    width = dwo_ref.shape[1]
    half = width // 256
    for tile in range(width // 128):
        lanes = slice(tile * 128, (tile + 1) * 128)
        dwo_ref[:, lanes] = sums_refs[tile % half][tile // half].astype(F32)
        for w, ref in enumerate((dwq_ref, dwk_ref, dwv_ref)):
            ref[:, lanes] = sums_refs[w][2 + tile].astype(F32)
    for out, parts in ((din_ref, din_refs), (dout_ref, dout_refs)):
        total = parts[0][...].astype(F32)
        for part in parts[1:]:
            total = total + part[...].astype(F32)
        out[...] = total


def finish(width, sums, din, dout):
    n = sums.shape[0]
    steps = 4

    def row_spec(array):
        return pl.BlockSpec((array.shape[0] // steps, array.shape[1]), lambda i: (i, 0))

    square = jax.ShapeDtypeStruct((width, width), F32)
    out_shape = [square] * 4 + [
        jax.ShapeDtypeStruct(din[0].shape, F32),
        jax.ShapeDtypeStruct(dout[0].shape, F32),
    ]
    return pl.pallas_call(
        functools.partial(finish_kernel, len(din)),
        grid=(steps,),
        in_specs=[
            pl.BlockSpec((n, width // steps, 128), lambda i, w=w: (0, w * steps + i, 0))
            for w in range(3)
        ]
        + [row_spec(part) for part in (*din, *dout)],
        out_specs=[row_spec(out) for out in out_shape],
        out_shape=out_shape,
        compiler_params=params(),
        cost_estimate=cost(0, 24 * width * width),
        name="finish",
    )(sums, sums, sums, *din, *dout)


def output_kernel(experts, cap, made_ref, hidden_ref, gate_ref, lines_ref, out_ref):
    rows, width = hidden_ref.shape
    pick = one_hot(iota((rows, experts * cap), 1) == col_of(lines_ref[1:2, :]))
    produced = mm(pick, made_ref[...])
    out_ref[...] = (hidden_ref[...] + gate_ref[:, 0:1] * produced).astype(BF16)


def layer_output(made, hidden, gate, lines, experts, cap):
    tokens, width = hidden.shape
    rows = 256
    made = made.reshape(-1, width)
    block = pl.BlockSpec((rows, width), lambda i: (i, 0))
    return pl.pallas_call(
        functools.partial(output_kernel, experts, cap),
        grid=(tokens // rows,),
        in_specs=[
            spec_all(made.shape),
            block,
            pl.BlockSpec((rows, 128), lambda i: (i, 0)),
            pl.BlockSpec((8, rows), lambda i: (0, i)),
        ],
        out_specs=block,
        out_shape=jax.ShapeDtypeStruct((tokens, width), BF16),
        compiler_params=params(),
        cost_estimate=cost(2 * tokens * width * experts * cap, 10 * tokens * width),
        name="layer_output",
    )(made, hidden, gate, lines)


def exchange(blocks, axis):
    return lax.all_to_all(blocks, axis, split_axis=0, concat_axis=0, tiled=True)


def on_device(
    tokens,
    segment_ids,
    routes,
    norm1_gain,
    norm1_bias,
    query_weight,
    w_key,
    w_value,
    w_output,
    norm2_gain,
    norm2_bias,
    router_proj,
    expert_embed,
    expert_in,
    expert_out,
    cotangent,
):
    count, width = tokens.shape
    experts = lax.axis_size("expert")
    dp_size = lax.axis_size("dp")
    cap = 2 * count // experts
    longest = segment_ids.shape[1] // 2
    space = router_proj.shape[1]
    vecs = jnp.stack([norm1_gain, norm1_bias, norm2_gain, norm2_bias])
    tables = jnp.concatenate(
        [
            jnp.pad(router_proj, ((0, 0), (0, 128 - space))),
            jnp.pad(expert_embed, ((0, 128 - experts), (0, 128 - space))),
        ]
    )
    q, k, v, mixed, probs, hidden, gate, slots, gates, lines, up = forward(
        routes.reshape(1, count), segment_ids.reshape(1, count), cotangent, tokens, vecs, tables,
        query_weight, w_key, w_value, w_output, longest, experts, cap,
    )
    back, gate_grads, made, din, dout = expert(
        slots, gates, up, expert_in[0], expert_out[0], dp_size
    )
    if can_reduce(width, space, dp_size, experts):
        grad_input, sums, output, small1, small2 = tail(
            tokens, vecs, tables, lines, gate_grads, gate, q, k, v, query_weight, w_key, w_value,
            w_output, probs, back, hidden, cotangent, mixed, made, space, longest, dp_size,
            experts,
        )
    else:
        made = exchange(made, "expert")
        grad_hidden, grad_mixed, delta, dwo, small2 = middle_back(
            back, gate_grads, lines, hidden, cotangent, mixed, w_output, vecs[2:3], vecs[3:4],
            tables[:width], tables[width:], space, experts, cap,
        )
        dq, dk, dv = attention_back(q, k, v, grad_mixed, probs, delta, longest)
        grad_input, dwq, dwk, dwv, small1 = qkv_back(
            tokens, vecs[0:1], vecs[1:2], grad_hidden, dq, dk, dv, query_weight, w_key, w_value
        )
        half = width // 256
        chunks = [dwo[:half], dwo[half:]]
        for at in range(width // 128):
            chunks.append(jnp.stack([dwq[at], dwk[at], dwv[at]]))
        sums, small1, small2 = lax.psum(
            (jnp.stack(chunks).astype(F32), small1, small2), ("dp", "expert")
        )
        sums = sums.astype(BF16).reshape(len(chunks), -1, 128)
        output = layer_output(made, hidden, gate, lines, experts, cap)
    dwo, dwq, dwk, dwv, grad_in, grad_out = finish(width, sums, din, dout)
    return (
        output,
        grad_input,
        small1[0],
        small1[1],
        dwq,
        dwk,
        dwv,
        dwo,
        small2[0],
        small2[1],
        small2[8 : 8 + space].T,
        small2[8 + space : 8 + space + experts, :space],
        grad_in[None],
        grad_out[None],
    )


def solution(mesh):
    split = P(("dp", "expert"), None)
    in_specs = (
        (split,) * 3 + (P(),) * 10 + (P("expert", None, None), P("expert", None, None), split)
    )
    out_specs = (
        (split, split) + (P(),) * 10 + (P("expert", None, "dp"), P("expert", "dp", None))
    )
    return jax.shard_map(
        on_device, mesh=mesh, in_specs=in_specs, out_specs=out_specs, check_vma=False
    )
```

```python
import functools

import jax
import jax.numpy as jnp
from jax import lax
from jax.experimental import pallas as pl
from jax.experimental.pallas import tpu as pltpu
from jax.sharding import PartitionSpec as P

HEAD_DIM = 64
PAIR = 2 * HEAD_DIM
SHARPNESS = 0.25
EXACT = lax.Precision.HIGHEST
BF16 = jnp.bfloat16
F32 = jnp.float32
FAR = -1e30
MIB = 1 << 20
WINDOW = 4
PARTS = 4
OUTPUT_TICK = 4
PARTS_EARLY = 18
PARTS_LOOP = 1
PARTS_DRAIN = 1


def mm(left, right):
    return jnp.dot(left, right, preferred_element_type=F32)


def mm_rows(left, right, precision=None):
    return lax.dot_general(
        left, right, (((0,), (0,)), ((), ())), precision=precision, preferred_element_type=F32
    )


def mm_cols(left, right, precision=None):
    return lax.dot_general(
        left, right, (((1,), (1,)), ((), ())), precision=precision, preferred_element_type=F32
    )


def iota(shape, axis):
    return lax.broadcasted_iota(jnp.int32, shape, axis)


def one_hot(condition):
    return jnp.where(condition, 1.0, 0.0).astype(BF16)


def params(limit=56):
    return pltpu.CompilerParams(vmem_limit_bytes=limit * MIB)


def cost(flops, moved, trans=0):
    return pl.CostEstimate(flops=int(flops), bytes_accessed=int(moved), transcendentals=int(trans))


def spec_all(shape):
    zeros = (0,) * len(shape)
    return pl.BlockSpec(shape, lambda *ids: zeros)


def slot_row_of(route_row, experts, cap):
    tokens = route_row.shape[1]
    padded = max(8, experts)
    hits = one_hot(iota((padded, tokens), 0) == route_row)
    earlier = one_hot(iota((tokens, tokens), 0) < iota((tokens, tokens), 1))
    ranks = mm(hits, earlier)
    rank = jnp.sum(ranks * hits.astype(F32), 0, keepdims=True)
    return route_row * cap + rank.astype(jnp.int32)


def as_row(col):
    rows = col.shape[0]
    eye = iota((rows, rows), 0) == iota((rows, rows), 1)
    return jnp.sum(jnp.where(eye, col, 0.0), 0, keepdims=True)


def as_col(row):
    rows = row.shape[1]
    eye = iota((rows, rows), 0) == iota((rows, rows), 1)
    return jnp.sum(jnp.where(eye, row, 0.0), 1, keepdims=True)


def norm_parts(values):
    average = jnp.mean(values, -1, keepdims=True)
    centred = values - average
    spread = jnp.mean(centred * centred, -1, keepdims=True)
    scale = lax.rsqrt(spread + 1e-05)
    return centred * scale, scale


def norm_back(grad, gain, unit, scale):
    grad_unit = grad * gain
    inner = jnp.mean(grad_unit * unit, -1, keepdims=True)
    return scale * (grad_unit - jnp.mean(grad_unit, -1, keepdims=True) - unit * inner)


def key_window(block, rows, tokens, longest):
    first = max(0, (block * rows - longest + 1) // 128 * 128)
    last = min(tokens, -(-(block * rows + rows - 1 + longest) // 128) * 128)
    return first, last


def attention_back_kernel(
    rows, longest, q_ref, k_ref, v_ref, do_ref, prob_ref, delta_ref,
    dq_ref, dk_ref, dv_ref, dk_sum, dv_sum,
):
    tokens = q_ref.shape[0]
    lane = iota((tokens, PAIR), 1)
    own = (lane < HEAD_DIM, lane >= HEAD_DIM)
    zero = jnp.zeros((), BF16)
    scale = HEAD_DIM**-0.5
    dk_sum[...] = jnp.zeros_like(dk_sum)
    dv_sum[...] = jnp.zeros_like(dv_sum)
    for block in range(tokens // rows):
        first, last = key_window(block, rows, tokens, longest)
        mine = slice(block * rows, (block + 1) * rows)
        values = v_ref[first:last, :]
        dq = jnp.zeros((rows, PAIR), F32)
        dk = jnp.zeros((last - first, PAIR), F32)
        dv = jnp.zeros((last - first, PAIR), F32)
        for h in range(2):
            do_h = jnp.where(own[h][mine], do_ref[mine, :], zero)
            q_h = jnp.where(own[h][mine], q_ref[mine, :], zero)
            k_h = jnp.where(own[h][first:last], k_ref[first:last, :], zero)
            probs = prob_ref[h, first:last, mine]
            grad_probs = mm_cols(values, do_h)
            grad_scores = (
                probs.astype(F32) * (grad_probs - delta_ref[0, h : h + 1, mine])
            ).astype(BF16)
            dq = dq + mm_rows(grad_scores, k_h)
            dk = dk + mm(grad_scores, q_h)
            dv = dv + mm(probs, do_h)
        dq_ref[mine, :] = (dq * scale).astype(BF16)
        dk_sum[first:last, :] += dk
        dv_sum[first:last, :] += dv
    dk_ref[...] = (dk_sum[...] * scale).astype(BF16)
    dv_ref[...] = dv_sum[...].astype(BF16)


def attention_back(q, k, v, grad_mixed, probs, delta, longest):
    tokens, width = q.shape
    pairs = width // PAIR
    rows = 256
    block = pl.BlockSpec((tokens, PAIR), lambda p: (0, p))
    made = jax.ShapeDtypeStruct((tokens, width), BF16)
    return pl.pallas_call(
        functools.partial(attention_back_kernel, rows, longest),
        grid=(pairs,),
        in_specs=[block] * 4
        + [
            pl.BlockSpec((2, tokens, tokens), lambda p: (p, 0, 0)),
            pl.BlockSpec((1, 8, tokens), lambda p: (p, 0, 0)),
        ],
        out_specs=[block] * 3,
        out_shape=[made] * 3,
        scratch_shapes=[pltpu.VMEM((tokens, PAIR), F32)] * 2,
        compiler_params=params(),
        cost_estimate=cost(8 * 2 * pairs * tokens * tokens * 256, 4 * pairs * tokens * tokens),
        name="attention_back",
    )(q, k, v, grad_mixed, probs, delta)


def router_parts(normed, proj_parts, embed, route, experts):
    high, rest = split_two(normed)
    both = mm(high, proj_parts[...])
    low = both[:, 0:128] + (both[:, 128:256] + mm(rest, proj_parts[:, 0:128]))
    low_squares = jnp.sum(low * low, -1, keepdims=True)
    low_scale = lax.rsqrt(jnp.maximum(low_squares, 1.0))
    low_unit = low * low_scale
    squares = jnp.sum(embed * embed, -1, keepdims=True)
    table_scale = lax.rsqrt(jnp.maximum(squares, 1.0))
    table = embed * table_scale
    logits = mm_cols(low_unit, table, EXACT) / SHARPNESS
    lane = iota(logits.shape, 1)
    logits = jnp.where(lane < experts, logits, FAR)
    weights = jnp.exp(logits - jnp.max(logits, -1, keepdims=True))
    probs = weights / jnp.sum(weights, -1, keepdims=True)
    chosen = jnp.where(lane == route, 1.0, 0.0)
    gate = jnp.sum(probs * chosen, -1, keepdims=True)
    return gate, probs, chosen, low, low_squares, low_scale, low_unit, squares, table_scale, table


def clipped_back(grad_unit, raw, scale, squares):
    share = jnp.where(squares > 1.0, 1.0, jnp.where(squares == 1.0, 0.5, 0.0))
    inner = jnp.sum(grad_unit * raw, -1, keepdims=True)
    return scale * grad_unit - share * scale * scale * scale * inner * raw


def col_of(row):
    return as_col(row.astype(F32)).astype(jnp.int32)


def split_two(value):
    high = value.astype(BF16)
    return high, (value - high.astype(F32)).astype(BF16)


def forward_kernel(
    experts, cap, longest,
    route_ref, seg_ref, cot_ref, x_ref, vecs_ref, tables_ref, wq_ref, wk_ref, wv_ref, wo_ref,
    q_ref, k_ref, v_ref, mixed_ref, probs_ref, hidden_ref, gate_ref, slots_ref, gates_ref,
    lines_ref, up_ref,
    weights, q_all, k_all, v_all, mixed_all, prob_buf, hidden_all, gate_all, slots_all,
    gates_all, lines_all, up_all, kept, tags, proj_parts,
    load_sem, store_sem, prob_sem, up_send, up_recv,
):
    tokens, width = x_ref.shape
    pairs = width // PAIR
    rows = 256
    blocks = tokens // rows
    me = lax.axis_index("expert")
    mesh_ids = pl.DeviceIdType.MESH
    loads = [
        pltpu.make_async_copy(ref, weights.at[i], load_sem.at[i])
        for i, ref in enumerate((wq_ref, wk_ref, wv_ref, wo_ref))
    ]
    for load in loads:
        load.start()
    barrier = pltpu.get_barrier_semaphore()

    def greet(s, carry):
        pl.semaphore_signal(
            barrier, inc=1, device_id={"expert": lax.rem(me + s, experts)}, device_id_type=mesh_ids
        )
        return carry

    lax.fori_loop(1, experts, greet, 0)

    route = route_ref[...]
    place = lax.rem(route - me + experts, experts)
    slot = slot_row_of(place, experts, cap)
    lines_all[...] = jnp.zeros_like(lines_all)
    lines_all[0:1, :] = slot
    lines_all[1:2, :] = slot + (route - place) * cap
    lines_all[2:3, :] = route
    pl.semaphore_wait(barrier, experts - 1)

    def up_copy(s):
        to = {"expert": lax.rem(me + s, experts)}
        return pltpu.make_async_remote_copy(
            up_all.at[s], up_ref.at[s], up_send.at[s], up_recv.at[s], to, mesh_ids
        )

    def up_block(s, carry):
        pick = one_hot(iota((cap, tokens), 0) + s * cap == lines_all[0:1, :])
        up_all[s] = mm(pick, cot_ref[...]).astype(BF16)

        @pl.when(s > 0)
        def _():
            up_copy(s).start()

        return carry

    lax.fori_loop(0, experts, up_block, 0)
    stores = []

    def store(src, dst):
        copy = pltpu.make_async_copy(src, dst, store_sem.at[len(stores)])
        copy.start()
        stores.append(copy)

    store(up_all.at[0], up_ref.at[0])
    store(lines_all, lines_ref)
    for load in loads:
        load.wait()

    def qkv_block(i, carry):
        at = pl.ds(pl.multiple_of(i * rows, rows), rows)
        unit, _ = norm_parts(x_ref[at, :].astype(F32))
        normed = (unit * vecs_ref[0:1, :] + vecs_ref[1:2, :]).astype(BF16)
        for w, ref in enumerate((q_all, k_all, v_all)):
            ref[at, :] = mm(normed, weights[w]).astype(BF16)
        lane = iota((rows, PAIR), 1)
        seg = col_of(seg_ref[0:1, at])
        for h in range(2):
            other = (1 - h) * HEAD_DIM
            tags[h, at, :] = jnp.where(lane - other == seg, 1.0, 0.0).astype(BF16)
            k_tag = jnp.where(lane - other == seg, 0.0, FAR)
            k_tag = jnp.where((lane >= other) & (lane < other + 8), k_tag, 0.0)
            tags[2 + h, at, :] = k_tag.astype(BF16)
        return carry

    lax.fori_loop(0, blocks, qkv_block, 0)
    store(q_all, q_ref)
    store(k_all, k_ref)
    store(v_all, v_ref)

    lane = iota((tokens, PAIR), 1)
    own = (lane < HEAD_DIM, lane >= HEAD_DIM)

    def prob_copy(p, at):
        return pltpu.make_async_copy(prob_buf.at[at], probs_ref.at[pl.ds(2 * p, 2)], prob_sem.at[at])

    def pair_step(p, carry):
        buffer = lax.rem(p, 2)

        @pl.when(p >= 2)
        def _():
            prob_copy(p - 2, buffer).wait()

        lanes = pl.ds(pl.multiple_of(p * PAIR, PAIR), PAIR)
        queries = q_all[:, lanes] * jnp.asarray(HEAD_DIM**-0.5, BF16)
        keys = k_all[:, lanes]
        q_h = [jnp.where(own[h], queries, tags[h]) for h in range(2)]
        k_h = [jnp.where(own[h], keys, tags[2 + h]) for h in range(2)]
        for block in range(blocks):
            first, last = key_window(block, rows, tokens, longest)
            mine = slice(block * rows, (block + 1) * rows)
            out = []
            for h in range(2):
                scores = mm_cols(k_h[h][first:last], q_h[h][mine])
                largest = jnp.max(scores, 0, keepdims=True)
                weighted = jnp.exp(scores - largest)
                total = jnp.sum(weighted, 0, keepdims=True)
                probs = (weighted * (1.0 / total)).astype(BF16)
                prob_buf[buffer, h, first:last, mine] = probs
                out.append(mm_rows(probs, v_all[first:last, lanes]))
            mixed_all[mine, lanes] = jnp.where(own[0][mine], out[0], out[1]).astype(BF16)
        prob_copy(p, buffer).start()
        return carry

    lax.fori_loop(0, pairs, pair_step, 0)
    store(mixed_all, mixed_ref)
    high, rest = split_two(tables_ref[0:width, :])
    proj_parts[:, 0:128] = high
    proj_parts[:, 128:256] = rest

    def row_block(i, carry):
        at = pl.ds(pl.multiple_of(i * rows, rows), rows)
        hidden = x_ref[at, :].astype(F32) + mm(mixed_all[at, :], weights[3])
        hidden_all[at, :] = hidden
        unit, _ = norm_parts(hidden)
        normed = unit * vecs_ref[2:3, :] + vecs_ref[3:4, :]
        route_col = col_of(lines_all[2:3, at])
        gate = router_parts(normed, proj_parts, tables_ref[width:, :], route_col, experts)[0]
        gate_all[at, :] = jnp.broadcast_to(gate, (rows, 128))
        high = gate.astype(BF16).astype(F32)
        mid = (gate - high).astype(BF16).astype(F32)
        rest = gate - high - mid
        lane = iota((rows, 128), 1)
        split = jnp.where(lane == 0, high, jnp.where(lane == 1, mid, jnp.where(lane == 2, rest, 0.0)))
        kept[at, 0:width] = normed.astype(BF16)
        kept[at, width : width + 128] = split.astype(BF16)
        return carry

    lax.fori_loop(0, blocks, row_block, 0)
    store(hidden_all, hidden_ref)
    store(gate_all, gate_ref)

    def slot_block(e, carry):
        pick = one_hot(iota((cap, tokens), 0) + e * cap == lines_all[0:1, :])
        got = mm(pick, kept[...])
        slots_all[e] = got[:, 0:width].astype(BF16)
        gates = as_row(jnp.sum(got[:, width : width + 128], 1, keepdims=True))
        gates_all[e] = jnp.broadcast_to(gates, (8, cap))
        return carry

    lax.fori_loop(0, experts, slot_block, 0)
    store(slots_all, slots_ref)
    store(gates_all, gates_ref)
    for p in (pairs - 2, pairs - 1):
        prob_copy(p, p % 2).wait()
    for copy in stores:
        copy.wait()

    def arrived(s, carry):
        up_copy(s).wait()
        return carry

    lax.fori_loop(1, experts, arrived, 0)


def forward(route_row, seg_row, cot, x, vecs, tables, wq, wk, wv, wo, longest, experts, cap):
    tokens, width = x.shape
    pairs = width // PAIR
    local = pl.BlockSpec(memory_space=pltpu.VMEM)
    anywhere = pl.BlockSpec(memory_space=pl.ANY)
    low = jax.ShapeDtypeStruct((tokens, width), BF16)
    chunks = jax.ShapeDtypeStruct((experts, cap, width), BF16)
    out_shape = [
        low,
        low,
        low,
        low,
        jax.ShapeDtypeStruct((2 * pairs, tokens, tokens), BF16),
        jax.ShapeDtypeStruct((tokens, width), F32),
        jax.ShapeDtypeStruct((tokens, 128), F32),
        chunks,
        jax.ShapeDtypeStruct((experts, 8, cap), F32),
        jax.ShapeDtypeStruct((8, tokens), jnp.int32),
        chunks,
    ]
    low_buf = pltpu.VMEM((tokens, width), BF16)
    sems = pltpu.SemaphoreType.DMA
    return pl.pallas_call(
        functools.partial(forward_kernel, experts, cap, longest),
        in_specs=[local] * 6 + [anywhere] * 4,
        out_specs=[anywhere] * len(out_shape),
        out_shape=out_shape,
        scratch_shapes=[
            pltpu.VMEM((4, width, width), BF16),
            low_buf,
            low_buf,
            low_buf,
            low_buf,
            pltpu.VMEM((2, 2, tokens, tokens), BF16),
            pltpu.VMEM((tokens, width), F32),
            pltpu.VMEM((tokens, 128), F32),
            pltpu.VMEM((experts, cap, width), BF16),
            pltpu.VMEM((experts, 8, cap), F32),
            pltpu.VMEM((8, tokens), jnp.int32),
            pltpu.VMEM((experts, cap, width), BF16),
            pltpu.VMEM((tokens, width + 128), BF16),
            pltpu.VMEM((4, tokens, PAIR), BF16),
            pltpu.VMEM((width, 256), BF16),
            sems((4,)),
            sems((10,)),
            sems((2,)),
            sems((experts,)),
            sems((experts,)),
        ],
        compiler_params=pltpu.CompilerParams(
            vmem_limit_bytes=60 * MIB, collective_id=2, has_side_effects=True
        ),
        cost_estimate=cost(8 * pairs * tokens * tokens * 256, 4 * pairs * tokens * tokens),
        name="forward",
    )(route_row, seg_row, cot, x, vecs, tables, wq, wk, wv, wo)


def distance(experts, i):
    near = (i + 1) // 2
    return lax.rem(i % 2 * near + (1 - i % 2) * (experts - near), experts)


def gelu_parts(pre):
    size = jnp.abs(pre)
    t = pl.reciprocal(1.0 + 0.23164189298 * size, approx=False)
    bell = jnp.exp(-0.5 * pre * pre)
    tail = t * (
        0.127414796
        + t * (-0.142248368 + t * (0.7107068705 + t * (-0.7265760135 + t * 0.5307027145)))
    )
    tail = tail * bell
    phi_sum = jnp.where(pre >= 0, 1.0 - tail, tail)
    return phi_sum, pre * bell * 0.3989422804014327


def expert_kernel(experts, x_axis, *refs):
    x_ref, gates_ref, w_in_ref, w_out_ref, up_ref = refs[:5]
    back_ref, gate_grads_ref = refs[5:7]
    rest = refs[7:]
    made_ref = rest[0]
    din_refs = rest[1 : 1 + x_axis]
    dout_refs = rest[1 + x_axis : 1 + 2 * x_axis]
    (
        x_here, up_here, gates_here, back_here, gate_grads_here, made_here,
        active, grad_pre, w_in, w_out, din_got, dout_got,
        load_sem, x_send, x_recv, g_send, g_recv, b_send, b_recv, gg_send, gg_recv,
        d_send, d_recv, e_send, e_recv, store_sem,
    ) = rest[1 + 2 * x_axis :]
    cap, width = x_here.shape[1:]
    hidden = w_in.shape[1]
    me = lax.axis_index("expert")
    dp = lax.axis_index("dp")
    core = lax.rem(dp, 2)
    mesh_ids = pl.DeviceIdType.MESH

    barrier = pltpu.get_barrier_semaphore()

    def greet(s, carry):
        pl.semaphore_signal(
            barrier, inc=1, device_id={"expert": lax.rem(me + s, experts)}, device_id_type=mesh_ids
        )
        return carry

    lax.fori_loop(1, experts, greet, 0)
    pl.semaphore_signal(
        barrier, inc=1, device_id={"dp": dp + 1 - 2 * core}, device_id_type=mesh_ids
    )

    def x_peer(k):
        return {"dp": 2 * lax.rem(dp // 2 + k, x_axis) + core}

    for k in range(1, x_axis):
        pl.semaphore_signal(barrier, inc=1, device_id=x_peer(k), device_id_type=mesh_ids)
    pl.semaphore_wait(barrier, experts + x_axis - 1)

    def out_copy(s):
        to = {"expert": lax.rem(me + s, experts)}
        return (
            pltpu.make_async_remote_copy(
                x_ref.at[s], x_here.at[s], x_send.at[s], x_recv.at[s], to, mesh_ids
            ),
            pltpu.make_async_remote_copy(
                gates_ref.at[s], gates_here.at[s], g_send.at[s], g_recv.at[s], to, mesh_ids
            ),
        )

    def home_copy(s):
        to = {"expert": lax.rem(me + experts - s, experts)}
        return (
            pltpu.make_async_remote_copy(
                back_here.at[s], back_ref.at[s], b_send.at[s], b_recv.at[s], to, mesh_ids
            ),
            pltpu.make_async_remote_copy(
                gate_grads_here.at[s], gate_grads_ref.at[s], gg_send.at[s], gg_recv.at[s], to, mesh_ids
            ),
        )

    nth = functools.partial(distance, experts)
    window = min(WINDOW, experts - 1)

    def send_out(i, carry):
        for copy in out_copy(nth(i)):
            copy.start()
        return carry

    lax.fori_loop(1, 1 + window, send_out, 0)
    loads = [
        pltpu.make_async_copy(x_ref.at[0], x_here.at[0], load_sem.at[0]),
        pltpu.make_async_copy(gates_ref.at[0], gates_here.at[0], load_sem.at[1]),
        pltpu.make_async_copy(w_in_ref, w_in, load_sem.at[2]),
        pltpu.make_async_copy(w_out_ref, w_out, load_sem.at[3]),
    ]
    loads.append(pltpu.make_async_copy(up_ref, up_here, load_sem.at[4]))
    for load in loads:
        load.start()
    for load in loads:
        load.wait()

    step = 512

    def send_home(i, carry):
        for copy in home_copy(nth(i)):
            copy.start()
        return carry

    def chunk(i, carry):
        s = nth(i)

        @pl.when(i > 0)
        def _():
            for copy in out_copy(s):
                copy.wait_recv()

            @pl.when(i + window < experts)
            def _():
                send_out(i + window, 0)

        @pl.when(i == experts - 1)
        def _():
            lax.fori_loop(1, experts - 1, send_home, 0)

        at_rows = pl.ds(pl.multiple_of(s * cap, cap), cap)
        gate = as_col(gates_here[s][0:1, :])
        up = up_here[s].astype(F32)
        scaled = (up * gate).astype(BF16)
        x = x_here[s]
        for at in range(0, hidden, step):
            part = slice(at, at + step)
            pre = mm(x, w_in[:, part])
            grad_active = mm_cols(scaled, w_out[part, :])
            phi_sum, slope = gelu_parts(pre)
            active[at_rows, part] = (pre * phi_sum).astype(BF16)
            grad_pre[at_rows, part] = (grad_active * (phi_sum + slope)).astype(BF16)
        made = mm(active[at_rows, :], w_out[...]).astype(BF16)
        made_here[s] = made
        gate_grad = jnp.sum(up * made.astype(F32), 1, keepdims=True)
        gate_grads_here[s] = jnp.broadcast_to(as_row(gate_grad), (8, cap))
        up_here[s] = scaled
        back_here[s] = mm_cols(grad_pre[at_rows, :], w_in[...]).astype(BF16)

        return carry

    lax.fori_loop(0, experts, chunk, 0)
    send_home(experts - 1, 0)
    stores = [
        pltpu.make_async_copy(back_here.at[0], back_ref.at[0], store_sem.at[0]),
        pltpu.make_async_copy(gate_grads_here.at[0], gate_grads_ref.at[0], store_sem.at[1]),
    ]
    for s in range(experts):
        home = lax.rem(me + experts - s, experts)
        stores.append(
            pltpu.make_async_copy(made_here.at[s], made_ref.at[home], store_sem.at[2 + s])
        )
    for store in stores:
        store.start()

    block = hidden // (2 * x_axis)
    slots = experts * cap
    other = {"dp": dp + 1 - 2 * core}
    x_all = x_here.reshape(slots, width)
    up_all = up_here.reshape(slots, width)

    def block_start(k, for_core):
        x_at = lax.rem(dp // 2 + k, x_axis)
        return pl.multiple_of((2 * x_at + for_core) * block, 128)

    def din_out(k):
        return w_in.at[:, k * block : (k + 1) * block]

    def dout_out(k):
        return w_out.at[k * block : (k + 1) * block]

    def core_copies(k):
        return (
            pltpu.make_async_remote_copy(
                din_out(k), din_got.at[k], d_send.at[k], d_recv.at[k], other, mesh_ids
            ),
            pltpu.make_async_remote_copy(
                dout_out(k),
                dout_got.at[k],
                d_send.at[x_axis + k],
                d_recv.at[x_axis + k],
                other,
                mesh_ids,
            ),
        )

    tile = 256 if block % 256 == 0 else 128

    def in_grads(k, for_core, out, got):
        start = block_start(k, for_core)
        columns = slice(out * block, (out + 1) * block)
        for at in range(0, width, tile):
            part = slice(at, at + tile)
            value = mm_rows(x_all[:, part], grad_pre[:, pl.ds(start, block)])
            if got is not None:
                value = value + din_got[got, part, :].astype(F32)
            w_in[part, columns] = value.astype(BF16)

    def out_grads(k, for_core, out, got):
        start = block_start(k, for_core)
        for at in range(0, block, tile):
            value = mm_rows(active[:, pl.ds(pl.multiple_of(start + at, 128), tile)], up_all[...])
            if got is not None:
                value = value + dout_got[got, at : at + tile, :].astype(F32)
            w_out[out * block + at : out * block + at + tile, :] = value.astype(BF16)

    def x_copies(k):
        return (
            pltpu.make_async_remote_copy(
                din_out(x_axis + k), din_refs[k], e_send.at[k], e_recv.at[k], x_peer(k), mesh_ids
            ),
            pltpu.make_async_remote_copy(
                dout_out(x_axis + k),
                dout_refs[k],
                e_send.at[x_axis + k],
                e_recv.at[x_axis + k],
                x_peer(k),
                mesh_ids,
            ),
        )

    for k in [*range(1, x_axis), 0]:
        in_copy, out_copy_k = core_copies(k)
        in_grads(k, 1 - core, k, None)
        in_copy.start()
        out_grads(k, 1 - core, k, None)
        out_copy_k.start()
        in_copy.wait_recv()
        in_grads(k, core, x_axis + k, k)
        if k:
            x_copies(k)[0].start()
        out_copy_k.wait_recv()
        out_grads(k, core, x_axis + k, k)
        if k:
            x_copies(k)[1].start()
    for i, (src, ref) in enumerate(
        ((din_out(x_axis), din_refs[0]), (dout_out(x_axis), dout_refs[0]))
    ):
        store = pltpu.make_async_copy(src, ref, store_sem.at[2 + experts + i])
        store.start()
        stores.append(store)
    for k in range(1, x_axis):
        for copy in x_copies(k):
            copy.wait()
    for store in stores:
        store.wait()
    for k in range(x_axis):
        for copy in core_copies(k):
            copy.wait_send()

    def finish(s, carry):
        for copy in out_copy(s):
            copy.wait_send()
        for copy in home_copy(s):
            copy.wait()
        return carry

    lax.fori_loop(1, experts, finish, 0)


def expert(x, gates, up, w_in, w_out, dp_size):
    experts, cap, width = x.shape
    hidden = w_in.shape[1]
    slots = experts * cap
    x_axis = dp_size // 2
    block = hidden // dp_size
    anywhere = pl.BlockSpec(memory_space=pl.ANY)
    rows = jax.ShapeDtypeStruct((experts, cap, width), BF16)
    out_shape = (
        [rows, jax.ShapeDtypeStruct((experts, 8, cap), F32), rows]
        + [jax.ShapeDtypeStruct((width, block), BF16)] * x_axis
        + [jax.ShapeDtypeStruct((block, width), BF16)] * x_axis
    )
    chunks = pltpu.VMEM((experts, cap, width), BF16)
    lines = pltpu.VMEM((experts, 8, cap), F32)
    sems = pltpu.SemaphoreType.DMA
    out = pl.pallas_call(
        functools.partial(expert_kernel, experts, x_axis),
        in_specs=[anywhere] * 5,
        out_specs=[anywhere] * len(out_shape),
        out_shape=out_shape,
        scratch_shapes=[
            chunks,
            chunks,
            lines,
            chunks,
            lines,
            chunks,
            pltpu.VMEM((slots, hidden), BF16),
            pltpu.VMEM((slots, hidden), BF16),
            pltpu.VMEM((width, hidden), BF16),
            pltpu.VMEM((hidden, width), BF16),
            pltpu.VMEM((x_axis, width, block), BF16),
            pltpu.VMEM((x_axis, block, width), BF16),
            sems((5,)),
        ]
        + [sems((experts,))] * 8
        + [sems((2 * x_axis,))] * 4
        + [sems((4 + experts,))],
        compiler_params=pltpu.CompilerParams(
            vmem_limit_bytes=63 * MIB, collective_id=0, has_side_effects=True
        ),
        cost_estimate=cost(12 * slots * width * hidden, 8 * width * hidden),
        name="expert",
    )(x, gates, w_in, w_out, up)
    back, gate_grads, made = out[:3]
    din = out[3 : 3 + x_axis]
    dout = out[3 + x_axis :]
    return back, gate_grads, made, din, dout


def store_tiles(out_ref, value):
    for tile in range(out_ref.shape[0]):
        out_ref[tile] = value[:, tile * 128 : (tile + 1) * 128].astype(BF16)


def middle_back_kernel(
    experts, cap, back_ref, gate_grads_ref, lines_ref, hidden_ref, cot_ref, mixed_ref, wo_ref,
    gain_ref, bias_ref, proj_ref, embed_ref,
    grad_hidden_ref, grad_mixed_ref, delta_ref, dwo_ref, small_ref,
    dwo_sum, dproj_sum, dembed_sum, gate_parts, proj_parts,
):
    step = pl.program_id(0)
    rows, width = hidden_ref.shape
    slots = back_ref.shape[0]

    @pl.when(step == 0)
    def _():
        small_ref[...] = jnp.zeros_like(small_ref)
        dwo_sum[...] = jnp.zeros_like(dwo_sum)
        dproj_sum[...] = jnp.zeros_like(dproj_sum)
        dembed_sum[...] = jnp.zeros_like(dembed_sum)
        high, rest = split_two(proj_ref[...])
        proj_parts[:, 0:128] = high
        proj_parts[:, 128:256] = rest
        line = iota((16, cap), 0)
        for e in range(experts):
            grads = gate_grads_ref[e, 0:1, :]
            high = grads.astype(BF16).astype(F32)
            mid = (grads - high).astype(BF16).astype(F32)
            rest = grads - high - mid
            split = jnp.where(line == 0, high, jnp.where(line == 1, mid, rest))
            gate_parts[:, e * cap : (e + 1) * cap] = jnp.where(line < 3, split, 0.0).astype(BF16)

    heads = width // HEAD_DIM
    pairs = heads // 2
    head_of = iota((8 * pairs, width), 1) // HEAD_DIM
    line = iota((8 * pairs, width), 0)
    head_lines = one_hot((head_of == line // 8 * 2 + line % 8) & (line % 8 < 2))
    pick = one_hot(iota((rows, slots), 1) == col_of(lines_ref[0:1, :]))
    grad = mm(pick, back_ref[...])
    gate_grad = jnp.sum(mm_cols(pick, gate_parts[...]), 1, keepdims=True)
    unit, scale = norm_parts(hidden_ref[...])
    normed = unit * gain_ref[...] + bias_ref[...]
    gate, probs, chosen, low, low_squares, low_scale, low_unit, _, _, table = router_parts(
        normed, proj_parts, embed_ref[...], col_of(lines_ref[2:3, :]), experts
    )
    grad_logits = (gate_grad * gate * (chosen - probs) / SHARPNESS).astype(BF16)
    grad_unit = mm(grad_logits, table.astype(BF16))
    dembed_sum[...] += mm_rows(grad_logits, low_unit.astype(BF16))
    grad_low = clipped_back(grad_unit, low, low_scale, low_squares).astype(BF16)
    dproj_sum[...] += mm_rows(grad_low, normed.astype(BF16))
    grad = grad + mm_cols(grad_low, proj_parts[:, 0:128])
    small_ref[0:1, :] += jnp.sum(grad * unit, 0, keepdims=True)
    small_ref[1:2, :] += jnp.sum(grad, 0, keepdims=True)
    grad_hidden = cot_ref[...].astype(F32) + norm_back(grad, gain_ref[...], unit, scale)
    grad_hidden_ref[...] = grad_hidden
    low_grad = grad_hidden.astype(BF16)
    grad_mixed = mm_cols(low_grad, wo_ref[...]).astype(BF16)
    grad_mixed_ref[...] = grad_mixed
    dwo_sum[...] += mm_rows(mixed_ref[...], low_grad)
    high, rest = split_two(grad_mixed.astype(F32) * mixed_ref[...].astype(F32))
    sums = mm_cols(head_lines, high) + mm_cols(head_lines, rest)
    for p in range(pairs):
        delta_ref[p] = sums[8 * p : 8 * p + 8, :]

    @pl.when(step == pl.num_programs(0) - 1)
    def _():
        embed = embed_ref[...]
        squares = jnp.sum(embed * embed, -1, keepdims=True)
        table_scale = lax.rsqrt(jnp.maximum(squares, 1.0))
        dembed = clipped_back(dembed_sum[...], embed, table_scale, squares)
        lines_proj = small_ref.shape[0] - 8 - max(8, experts)
        small_ref[8 : 8 + lines_proj, :] = dproj_sum[0:lines_proj, :]
        small_ref[8 + lines_proj :, 0:128] = dembed[0 : max(8, experts), :]
        store_tiles(dwo_ref, dwo_sum[...])


def middle_back(
    back, gate_grads, lines, hidden, cot, mixed, wo, gain, bias, proj, embed, space, experts, cap
):
    tokens, width = hidden.shape
    slots = experts * cap
    rows = 256
    back = back.reshape(slots, width)
    block = pl.BlockSpec((rows, width), lambda i: (i, 0))
    tiles = width // 128
    small_shape = (8 + space + max(8, experts), width)
    args = (back, gate_grads, lines, hidden, cot, mixed, wo, gain, bias, proj, embed)
    return pl.pallas_call(
        functools.partial(middle_back_kernel, experts, cap),
        grid=(tokens // rows,),
        in_specs=[
            spec_all(back.shape),
            spec_all(gate_grads.shape),
            pl.BlockSpec((8, rows), lambda i: (0, i)),
            block,
            block,
            block,
        ]
        + [spec_all(a.shape) for a in args[6:]],
        out_specs=[
            block,
            block,
            pl.BlockSpec((tiles, 8, rows), lambda i: (0, 0, i)),
            spec_all((tiles, width, 128)),
            spec_all(small_shape),
        ],
        out_shape=[
            jax.ShapeDtypeStruct((tokens, width), F32),
            jax.ShapeDtypeStruct((tokens, width), BF16),
            jax.ShapeDtypeStruct((tiles, 8, tokens), F32),
            jax.ShapeDtypeStruct((tiles, width, 128), BF16),
            jax.ShapeDtypeStruct(small_shape, F32),
        ],
        scratch_shapes=[
            pltpu.VMEM((width, width), F32),
            pltpu.VMEM((128, width), F32),
            pltpu.VMEM((128, 128), F32),
            pltpu.VMEM((16, slots), BF16),
            pltpu.VMEM((width, 256), BF16),
        ],
        compiler_params=params(),
        cost_estimate=cost(2 * tokens * width * (2 * width + slots), 20 * tokens * width),
        name="middle_back",
    )(*args)


def qkv_back_kernel(
    x_ref, gain_ref, bias_ref, grad_hidden_ref, dq_ref, dk_ref, dv_ref, wq_ref, wk_ref, wv_ref,
    grad_ref, dwq_ref, dwk_ref, dwv_ref, small_ref, low_ref,
):
    tokens, width = x_ref.shape
    rows = 256
    small_ref[...] = jnp.zeros_like(small_ref)

    def row_block(i, carry):
        at = pl.ds(pl.multiple_of(i * rows, rows), rows)
        unit, scale = norm_parts(x_ref[at, :].astype(F32))
        low_ref[at, :] = (unit * gain_ref[...] + bias_ref[...]).astype(BF16)
        grad = (
            mm_cols(dq_ref[at, :], wq_ref[...])
            + mm_cols(dk_ref[at, :], wk_ref[...])
            + mm_cols(dv_ref[at, :], wv_ref[...])
        )
        small_ref[0:1, :] += jnp.sum(grad * unit, 0, keepdims=True)
        small_ref[1:2, :] += jnp.sum(grad, 0, keepdims=True)
        grad_ref[at, :] = grad_hidden_ref[at, :] + norm_back(grad, gain_ref[...], unit, scale)
        return carry

    lax.fori_loop(0, tokens // rows, row_block, 0)
    low = low_ref[...]
    store_tiles(dwq_ref, mm_rows(low, dq_ref[...]))
    store_tiles(dwk_ref, mm_rows(low, dk_ref[...]))
    store_tiles(dwv_ref, mm_rows(low, dv_ref[...]))


def qkv_back(x, gain, bias, grad_hidden, dq, dk, dv, wq, wk, wv):
    tokens, width = x.shape
    square = jax.ShapeDtypeStruct((width // 128, width, 128), BF16)
    return pl.pallas_call(
        qkv_back_kernel,
        out_shape=[
            jax.ShapeDtypeStruct((tokens, width), F32),
            square,
            square,
            square,
            jax.ShapeDtypeStruct((8, width), F32),
        ],
        scratch_shapes=[pltpu.VMEM((tokens, width), BF16)],
        compiler_params=params(),
        cost_estimate=cost(12 * tokens * width * width, 20 * tokens * width),
        name="qkv_back",
    )(x, gain, bias, grad_hidden, dq, dk, dv, wq, wk, wv)


def add_rows(rows, out_ref, out_at, terms):
    step = next(step for step in (320, 160, 80, 48, 16) if rows % step == 0)

    def body(i, carry):
        at = i * step
        total = None
        for ref, start in terms:
            value = ref[pl.ds(pl.multiple_of(start + at, 16), step), :].astype(F32)
            total = value if total is None else total + value
        out_ref[pl.ds(pl.multiple_of(out_at + at, 16), step), :] = total.astype(out_ref.dtype)
        return carry

    lax.fori_loop(0, rows // step, body, 0)


def can_reduce(width, space, dp_size, experts):
    spare = chunk_rows(width, dp_size, experts) - 3 * width
    lines2 = 8 + space + max(8, experts)
    return (
        width // 128 % 2 == 0
        and 64 * dp_size * experts <= 3 * width
        and spare >= width // 128 * lines2
    )


def chunk_rows(width, dp_size, experts):
    unit = 16 * dp_size * experts
    return -(-3 * width // unit) * unit


def tail_kernel(
    x_axis, experts, longest,
    x_ref, vecs_ref, tables_ref, lines_ref, gate_grads_ref, gate_ref,
    q_hbm, k_hbm, v_hbm, wq_hbm, wk_hbm, wv_hbm, wo_hbm, probs_ref, back_hbm, hidden_hbm,
    cot_hbm, mixed_hbm, made_hbm,
    grad_hbm, sums_hbm, output_hbm, small_out, small_out2,
    q_ref, k_ref, v_ref, do_ref, weights, out_ref, made_home, hidden_part, delta_ref, small_ref,
    dproj_sum, dembed_sum, gate_parts, proj_parts,
    dq_all, dk_all, dv_all, normed_t, prob_buf, dk_sum, dv_sum, grads, grad_hidden, small_in,
    core_got, core_sum, plane_got, plane_sum, line_got, small_got,
    load_sem, prob_sem, sums_sem, grad_sem, hidden_sem, made_send, made_recv,
    core_send, core_recv, plane_send, plane_recv, line_send, line_recv,
    line_back_send, line_back_recv, plane_back_send, plane_back_recv,
    core_back_send, core_back_recv, small_send, small_recv,
):
    tokens, width = x_ref.shape
    pairs = width // PAIR
    n = grads.shape[0]
    block_rows = 256
    dp = lax.axis_index("dp")
    me = lax.axis_index("expert")
    core = lax.rem(dp, 2)
    x_at = dp // 2
    low = lax.rem(me, 2)
    high = me // 2
    planes, lines = 2 * x_axis, experts // 2
    mesh_ids = pl.DeviceIdType.MESH
    rows = grads.shape[1]
    half = rows // 2
    quarter = half // planes
    piece = quarter // lines
    plane_at = x_at * 2 + low

    other_core = {"dp": dp + 1 - 2 * core}

    def plane_peer(j):
        at = lax.rem(plane_at + j, planes)
        return at, (2 * (at // 2) + core, 2 * high + lax.rem(at, 2))

    def line_peer(j):
        at = lax.rem(high + j, lines)
        return at, {"expert": 2 * at + low}

    barrier = pltpu.get_barrier_semaphore()
    pl.semaphore_signal(barrier, inc=1, device_id=other_core, device_id_type=mesh_ids)
    for j in range(1, planes):
        pl.semaphore_signal(barrier, inc=1, device_id=plane_peer(j)[1], device_id_type=mesh_ids)
    for j in range(1, lines):
        pl.semaphore_signal(barrier, inc=1, device_id=line_peer(j)[1], device_id_type=mesh_ids)

    def expert_peer(j):
        return lax.rem(me + j, experts)

    for j in range(1, experts):
        pl.semaphore_signal(
            barrier, inc=1, device_id={"expert": expert_peer(j)}, device_id_type=mesh_ids
        )

    def remote(src, dst, send, recv, to):
        return pltpu.make_async_remote_copy(src, dst, send, recv, to, mesh_ids)

    def rows_at(start, size):
        return pl.ds(pl.multiple_of(start, 16), size)

    def core_copy(c):
        src = grads.at[c, rows_at((1 - core) * half, half)]
        return [remote(src, core_got.at[c], core_send.at[c], core_recv.at[c], other_core)]

    def plane_copies(c):
        made = []
        for j in range(1, planes):
            at, to = plane_peer(j)
            src = core_sum.at[c, rows_at(at * quarter, quarter)]
            made.append(
                remote(src, plane_got.at[c, j - 1], plane_send.at[c, j], plane_recv.at[c, j], to)
            )
        return made

    def line_copies(c):
        made = []
        for j in range(1, lines):
            at, to = line_peer(j)
            src = plane_sum.at[c, rows_at(at * piece, piece)]
            made.append(remote(src, line_got.at[c, j - 1], line_send.at[c, j], line_recv.at[c, j], to))
        return made

    base = core * half + plane_at * quarter

    def line_back(c):
        at = rows_at(base + high * piece, piece)
        made = []
        for j in range(1, lines):
            to = line_peer(j)[1]
            made.append(
                remote(
                    out_ref.at[c, at],
                    out_ref.at[c, at],
                    line_back_send.at[c, j],
                    line_back_recv.at[c, j],
                    to,
                )
            )
        return made

    def plane_back(c):
        at = rows_at(base, quarter)
        made = []
        for j in range(1, planes):
            to = plane_peer(j)[1]
            made.append(
                remote(
                    out_ref.at[c, at],
                    out_ref.at[c, at],
                    plane_back_send.at[c, j],
                    plane_back_recv.at[c, j],
                    to,
                )
            )
        return made

    def core_back(c):
        at = rows_at(core * half, half)
        return [
            remote(
                out_ref.at[c, at],
                out_ref.at[c, at],
                core_back_send.at[c],
                core_back_recv.at[c],
                other_core,
            )
        ]

    def small_copies(stage):
        made = []
        if stage == 0:
            made.append(
                remote(
                    small_got.at[0, 0],
                    small_got.at[0, 1],
                    small_send.at[0, 1],
                    small_recv.at[0, 1],
                    other_core,
                )
            )
        else:
            for j in range(1, planes if stage == 1 else lines):
                to = plane_peer(j)[1] if stage == 1 else line_peer(j)[1]
                made.append(
                    remote(
                        small_got.at[stage, 0],
                        small_got.at[stage, j],
                        small_send.at[stage, j],
                        small_recv.at[stage, j],
                        to,
                    )
                )
        return made

    def start(copies):
        for copy in copies:
            copy.start()

    def received(copies):
        for copy in copies:
            copy.wait_recv()

    def ordered(got, at, count):
        total = None
        for i in range(count):
            value = got(lax.rem(at + count - i, count))
            total = value if total is None else total + value
        return total

    def stage_run(stage, c):
        if stage == 0:
            start(core_copy(c))
        elif stage == 1:
            received(core_copy(c))
            add_rows(
                half, core_sum.at[c], 0, [(grads.at[c], core * half), (core_got.at[c], 0)]
            )
            start(plane_copies(c))
        elif stage == 2:
            received(plane_copies(c))
            add_rows(
                quarter,
                plane_sum.at[c],
                0,
                [(core_sum.at[c], plane_at * quarter)]
                + [(plane_got.at[c, j - 1], 0) for j in range(1, planes)],
            )
            start(line_copies(c))
        elif stage == 3:
            received(line_copies(c))
            add_rows(
                piece,
                out_ref.at[c],
                base + high * piece,
                [(plane_sum.at[c], high * piece)]
                + [(line_got.at[c, j - 1], 0) for j in range(1, lines)],
            )
            start(line_back(c))
        elif stage == 4:
            received(line_back(c))
            start(plane_back(c))
        elif stage == 5:
            received(plane_back(c))
            start(core_back(c))
        else:
            received(core_back(c))
            sums_copy(c).start()

    def sums_copy(c):
        return pltpu.make_async_copy(out_ref.at[c], sums_hbm.at[c], sums_sem.at[c])

    def small_run(stage):
        if stage == 0:
            small_got[0, 0] = small_in[...]
            start(small_copies(0))
        elif stage == 1:
            received(small_copies(0))
            small_got[1, 0] = small_got[0, 0] + small_got[0, 1]
            start(small_copies(1))
        elif stage == 2:
            received(small_copies(1))
            small_got[2, 0] = ordered(lambda j: small_got[1, j], plane_at, planes)
            start(small_copies(2))
        elif stage == 3:
            received(small_copies(2))
            small_out[...] = ordered(lambda j: small_got[2, j], high, lines)


    def prob_copy(p, slot):
        return pltpu.make_async_copy(
            probs_ref.at[pl.ds(2 * p, 2)], prob_buf.at[slot], prob_sem.at[slot]
        )

    full = 3 * width
    experts_cap = made_home.shape[1]
    slots = experts * experts_cap
    gain1, bias1 = vecs_ref[0:1, :], vecs_ref[1:2, :]
    gain2, bias2 = vecs_ref[2:3, :], vecs_ref[3:4, :]
    back_buf = prob_buf.at[1, :, :, 0:width]
    sources = [
        (back_hbm, back_buf),
        (hidden_hbm, grad_hidden),
        (cot_hbm, dq_all),
        (mixed_hbm, dv_all),
        (wo_hbm, weights.at[3]),
        (q_hbm, q_ref),
        (k_hbm, k_ref),
        (v_hbm, v_ref),
        (wq_hbm, weights.at[0]),
        (wk_hbm, weights.at[1]),
        (wv_hbm, weights.at[2]),
        (made_hbm.at[me], made_home.at[me]),
    ]
    loads = [
        pltpu.make_async_copy(src, dst, load_sem.at[i]) for i, (src, dst) in enumerate(sources)
    ]
    for load in loads:
        load.start()
    prob_copy(0, 0).start()
    pl.semaphore_wait(barrier, planes + lines - 1 + experts - 1)

    parts = PARTS * (experts - 1)
    early = min(PARTS_EARLY, parts)

    def half_peer(i):
        half = experts // 2
        far = (i + 1) // half
        return lax.rem(me + i + 1, half) + half * lax.rem(me // half + far, 2)

    def made_copy(m):
        to = half_peer(m // PARTS)
        at = rows_at(m % PARTS * (experts_cap // PARTS), experts_cap // PARTS)
        return remote(
            made_hbm.at[to, at],
            made_home.at[me, at],
            made_send.at[m],
            made_recv.at[m],
            {"expert": to},
        )

    def made_start(m, carry):
        made_copy(m).start()
        return carry

    def made_received(m, carry):
        made_copy(m).wait_recv()
        return carry

    def made_sent(m, carry):
        made_copy(m).wait_send()
        return carry

    lax.fori_loop(0, early, made_start, 0)

    for c in range(n):
        grads[c, full:rows, :] = jnp.zeros((rows - full, 128), BF16)
    small_ref[...] = jnp.zeros_like(small_ref)
    dproj_sum[...] = jnp.zeros_like(dproj_sum)
    dembed_sum[...] = jnp.zeros_like(dembed_sum)
    upper, rest = split_two(tables_ref[0:width, :])
    proj_parts[:, 0:128] = upper
    proj_parts[:, 128:256] = rest
    split_line = iota((16, experts_cap), 0)
    for e in range(experts):
        line_grads = gate_grads_ref[e, 0:1, :]
        upper = line_grads.astype(BF16).astype(F32)
        mid = (line_grads - upper).astype(BF16).astype(F32)
        rest = line_grads - upper - mid
        split = jnp.where(split_line == 0, upper, jnp.where(split_line == 1, mid, rest))
        gate_parts[:, e * experts_cap : (e + 1) * experts_cap] = jnp.where(
            split_line < 3, split, 0.0
        ).astype(BF16)
    head_of = iota((8 * pairs, width), 1) // HEAD_DIM
    line = iota((8 * pairs, width), 0)
    head_lines = one_hot((head_of == line // 8 * 2 + line % 8) & (line % 8 < 2))
    embed = tables_ref[width:, :]
    for load in loads[0:5]:
        load.wait()

    def middle_block(i, carry):
        at = pl.ds(pl.multiple_of(i * block_rows, block_rows), block_rows)
        pick = one_hot(iota((block_rows, slots), 1) == col_of(lines_ref[0:1, at]))
        grad = mm(pick[:, 0:tokens], prob_buf[1, 0, :, 0:width])
        grad = grad + mm(pick[:, tokens:], prob_buf[1, 1, :, 0:width])
        gate_grad = jnp.sum(mm_cols(pick, gate_parts[...]), 1, keepdims=True)
        unit, unit_scale = norm_parts(grad_hidden[at, :])
        normed = unit * gain2 + bias2
        gate, probs, chosen, low, low_squares, low_scale, low_unit, _, _, table = router_parts(
            normed, proj_parts, embed, col_of(lines_ref[2:3, at]), experts
        )
        grad_logits = (gate_grad * gate * (chosen - probs) / SHARPNESS).astype(BF16)
        grad_unit = mm(grad_logits, table.astype(BF16))
        dembed_sum[...] += mm_rows(grad_logits, low_unit.astype(BF16))
        grad_low = clipped_back(grad_unit, low, low_scale, low_squares).astype(BF16)
        dproj_sum[...] += mm_rows(grad_low, normed.astype(BF16))
        grad = grad + mm_cols(grad_low, proj_parts[:, 0:128])
        small_ref[0:1, :] += jnp.sum(grad * unit, 0, keepdims=True)
        small_ref[1:2, :] += jnp.sum(grad, 0, keepdims=True)
        total_grad = dq_all[at, :].astype(F32) + norm_back(grad, gain2, unit, unit_scale)
        grad_hidden[at, :] = total_grad
        low_grad = total_grad.astype(BF16)
        dk_all[at, :] = low_grad
        grad_mixed = mm_cols(low_grad, weights[3]).astype(BF16)
        do_ref[at, :] = grad_mixed
        high, rest = split_two(grad_mixed.astype(F32) * dv_all[at, :].astype(F32))
        lines_sum = mm_cols(head_lines, high) + mm_cols(head_lines, rest)
        for p in range(pairs):
            delta_ref[p, :, at] = lines_sum[8 * p : 8 * p + 8, :]
        return carry

    lax.fori_loop(0, tokens // block_rows, middle_block, 0)
    squares = jnp.sum(embed * embed, -1, keepdims=True)
    table_scale = lax.rsqrt(jnp.maximum(squares, 1.0))
    dembed = clipped_back(dembed_sum[...], embed, table_scale, squares)
    lines2 = small_ref.shape[0]
    lines_proj = lines2 - 8 - max(8, experts)
    small_ref[8 : 8 + lines_proj, :] = dproj_sum[0:lines_proj, :]
    small_ref[8 + lines_proj :, 0:128] = dembed[0 : max(8, experts), :]
    for tile in range(width // 128):
        at = full + tile * lines2
        grads[0, at : at + lines2, :] = small_ref[:, tile * 128 : (tile + 1) * 128].astype(BF16)
    half_tiles = width // 256
    for wide in range(half_tiles):
        made = mm_rows(dv_all[...], dk_all[:, wide * 256 : (wide + 1) * 256]).astype(BF16)
        for i in range(2):
            tile = 2 * wide + i
            start_at = tile % half_tiles * width
            grads[tile // half_tiles, start_at : start_at + width, :] = made[
                :, i * 128 : (i + 1) * 128
            ]
        if wide == (half_tiles - 1) // 2:
            stage_run(0, 0)
    for at in range(0, tokens, block_rows):
        part = slice(at, at + block_rows)
        unit, _ = norm_parts(x_ref[part, :].astype(F32))
        normed = unit * gain1 + bias1
        normed_t[:, part] = normed.T.astype(BF16)
    stage_run(1, 0)
    stage_run(0, 1)
    for load in loads[5:8]:
        load.wait()
    scale = HEAD_DIM**-0.5
    lane = iota((tokens, PAIR), 1)
    own = (lane < HEAD_DIM, lane >= HEAD_DIM)
    zero = jnp.zeros((), BF16)

    def pair_step(p, carry):
        slot = lax.rem(p, 2)
        prob_copy(p, slot).wait()

        @pl.when(p < pairs - 1)
        def _():
            prob_copy(p + 1, 1 - slot).start()

        lanes = pl.ds(pl.multiple_of(p * PAIR, PAIR), PAIR)
        dk_sum[...] = jnp.zeros_like(dk_sum)
        dv_sum[...] = jnp.zeros_like(dv_sum)
        for block in range(tokens // block_rows):
            first, last = key_window(block, block_rows, tokens, longest)
            mine = slice(block * block_rows, (block + 1) * block_rows)
            values = v_ref[first:last, lanes]
            keys = k_ref[first:last, lanes]
            queries = q_ref[mine, lanes]
            grad_out = do_ref[mine, lanes]
            dq = jnp.zeros((block_rows, PAIR), F32)
            dk = jnp.zeros((last - first, PAIR), F32)
            dv = jnp.zeros((last - first, PAIR), F32)
            for h in range(2):
                do_h = jnp.where(own[h][mine], grad_out, zero)
                q_h = jnp.where(own[h][mine], queries, zero)
                k_h = jnp.where(own[h][first:last], keys, zero)
                probs = prob_buf[slot, h, first:last, mine]
                grad_probs = mm_cols(values, do_h)
                grad_scores = (
                    probs.astype(F32) * (grad_probs - delta_ref[p, h : h + 1, mine])
                ).astype(BF16)
                dq = dq + mm_rows(grad_scores, k_h)
                dk = dk + mm(grad_scores, q_h)
                dv = dv + mm(probs, do_h)
            dq_all[mine, lanes] = (dq * scale).astype(BF16)
            dk_sum[first:last, :] += dk
            dv_sum[first:last, :] += dv
        dk_all[:, lanes] = (dk_sum[...] * scale).astype(BF16)
        dv_all[:, lanes] = dv_sum[...].astype(BF16)
        first_part = jnp.minimum(early + p * PARTS_LOOP, parts)
        last_part = jnp.minimum(early + (p + 1) * PARTS_LOOP, parts)
        lax.fori_loop(first_part, last_part, made_start, 0)
        for w, ref in enumerate((dq_all, dk_all, dv_all)):
            made = mm(normed_t[...], ref[:, lanes]).astype(BF16)
            grads[p + 2, w * width : (w + 1) * width, :] = made
        for stage in reversed(range(7)):
            if stage <= 2:
                stage_run(stage, p + 2 - stage)
            else:

                @pl.when(p + 2 >= stage)
                def _(stage=stage):
                    stage_run(stage, p + 2 - stage)

        return carry

    lax.fori_loop(0, pairs, pair_step, 0)
    for load in loads[8:]:
        load.wait()
    small_in[...] = jnp.zeros_like(small_in)

    def row_block(i):
        at = slice(i * block_rows, (i + 1) * block_rows)
        unit, unit_scale = norm_parts(x_ref[at, :].astype(F32))
        grad = (
            mm_cols(dq_all[at, :], weights[0])
            + mm_cols(dk_all[at, :], weights[1])
            + mm_cols(dv_all[at, :], weights[2])
        )
        small_in[0:1, :] += jnp.sum(grad * unit, 0, keepdims=True)
        small_in[1:2, :] += jnp.sum(grad, 0, keepdims=True)
        grad_hidden[at, :] += norm_back(grad, gain1, unit, unit_scale)

    grad_copy = pltpu.make_async_copy(grad_hidden, grad_hbm, grad_sem.at[0])

    def hidden_copy(i):
        at = slice(i * block_rows, (i + 1) * block_rows)
        return pltpu.make_async_copy(hidden_hbm.at[at], hidden_part.at[i % 2], hidden_sem.at[i % 2])

    output_copy = pltpu.make_async_copy(do_ref, output_hbm, grad_sem.at[1])

    def output_block(i):
        at = slice(i * block_rows, (i + 1) * block_rows)
        if i == 0:
            lax.fori_loop(0, parts, made_received, 0)
        hidden_copy(i).wait()
        if i + 1 < tokens // block_rows:
            hidden_copy(i + 1).start()
        slot = col_of(lines_ref[1:2, at])
        pick = one_hot(iota((block_rows, slots), 1) == slot)
        produced = jnp.zeros((block_rows, width), F32)
        for e in range(experts):
            produced = produced + mm(
                pick[:, e * experts_cap : (e + 1) * experts_cap], made_home[e]
            )
        total = hidden_part[i % 2] + gate_ref[at, 0:1] * produced
        do_ref[at, :] = total.astype(BF16)

    hidden_copy(0).start()

    blocks = tokens // block_rows
    done = 0
    out_done = 0
    small_at = 0
    next_part = min(early + pairs * PARTS_LOOP, parts)
    for tick in range(pairs + 1, pairs + 8):
        if next_part < parts:
            some = min(parts, next_part + PARTS_DRAIN)
            lax.fori_loop(next_part, some, made_start, 0)
            next_part = some
        for _ in range(2):
            if done < blocks:
                row_block(done)
                done += 1
                if done == blocks:
                    grad_copy.start()
            elif out_done < blocks and tick > pairs + OUTPUT_TICK and next_part == parts:
                output_block(out_done)
                out_done += 1
                if out_done == blocks:
                    output_copy.start()
        for stage in reversed(range(7)):
            c = tick + 1 - stage
            if 0 <= c < n:
                stage_run(stage, c)
        if done == blocks and small_at < 4:
            small_run(small_at)
            small_at += 1
    while done < blocks:
        row_block(done)
        done += 1
        if done == blocks:
            grad_copy.start()
    lax.fori_loop(next_part, parts, made_start, 0)
    while out_done < blocks:
        output_block(out_done)
        out_done += 1
        if out_done == blocks:
            output_copy.start()
    while small_at < 4:
        small_run(small_at)
        small_at += 1
    for tile in range(width // 128):
        at = full + tile * lines2
        small_out2[:, tile * 128 : (tile + 1) * 128] = out_ref[0, at : at + lines2, :].astype(F32)
    grad_copy.wait()
    output_copy.wait()
    for c in range(n):
        sums_copy(c).wait()
    lax.fori_loop(0, parts, made_sent, 0)
    for stage in range(3):
        for copy in small_copies(stage):
            copy.wait_send()

    def sent(c, carry):
        for made in (core_copy, plane_copies, line_copies, line_back, plane_back, core_back):
            for copy in made(c):
                copy.wait_send()
        return carry

    lax.fori_loop(0, n, sent, 0)


def tail(
    x, vecs, tables, lines, gate_grads, gate, q, k, v, wq, wk, wv, wo, probs, back, hidden, cot,
    mixed, made, space, longest, dp_size, experts,
):
    tokens, width = x.shape
    pairs = width // PAIR
    n = 2 + pairs
    rows = chunk_rows(width, dp_size, experts)
    x_axis, members, planes = dp_size // 2, experts // 2, dp_size
    half = rows // 2
    quarter = half // planes
    piece = quarter // members
    most = max(planes, members)
    small_shape = (8, width)
    cap = made.shape[1]
    small2_shape = (8 + space + max(8, experts), width)
    block_rows = 256
    sems = pltpu.SemaphoreType.DMA
    local = pl.BlockSpec(memory_space=pltpu.VMEM)
    anywhere = pl.BlockSpec(memory_space=pl.ANY)
    low = pltpu.VMEM((tokens, width), BF16)
    return pl.pallas_call(
        functools.partial(tail_kernel, x_axis, experts, longest),
        in_specs=[local] * 6 + [anywhere] * 13,
        out_specs=[anywhere] * 3 + [local] * 2,
        out_shape=[
            jax.ShapeDtypeStruct((tokens, width), F32),
            jax.ShapeDtypeStruct((n, rows, 128), BF16),
            jax.ShapeDtypeStruct((tokens, width), BF16),
            jax.ShapeDtypeStruct(small_shape, F32),
            jax.ShapeDtypeStruct(small2_shape, F32),
        ],
        scratch_shapes=[
            low,
            low,
            low,
            low,
            pltpu.VMEM((4, width, width), BF16),
            pltpu.VMEM((n, rows, 128), BF16),
            pltpu.VMEM((experts, cap, width), BF16),
            pltpu.VMEM((2, block_rows, width), F32),
            pltpu.VMEM((pairs, 8, tokens), F32),
            pltpu.VMEM(small2_shape, F32),
            pltpu.VMEM((128, width), F32),
            pltpu.VMEM((128, 128), F32),
            pltpu.VMEM((16, experts * cap), BF16),
            pltpu.VMEM((width, 256), BF16),
            low,
            low,
            low,
            pltpu.VMEM((width, tokens), BF16),
            pltpu.VMEM((2, 2, tokens, tokens), BF16),
            pltpu.VMEM((tokens, PAIR), F32),
            pltpu.VMEM((tokens, PAIR), F32),
            pltpu.VMEM((n, rows, 128), BF16),
            pltpu.VMEM((tokens, width), F32),
            pltpu.VMEM(small_shape, F32),
            pltpu.VMEM((n, half, 128), BF16),
            pltpu.VMEM((n, half, 128), BF16),
            pltpu.VMEM((n, planes - 1, quarter, 128), BF16),
            pltpu.VMEM((n, quarter, 128), BF16),
            pltpu.VMEM((n, members - 1, piece, 128), BF16),
            pltpu.VMEM((3, most, *small_shape), F32),
            sems((12,)),
            sems((2,)),
            sems((n,)),
            sems((2,)),
            sems((2,)),
            sems((PARTS * (experts - 1),)),
            sems((PARTS * (experts - 1),)),
        ]
        + [sems((n,))] * 2
        + [sems((n, planes))] * 2
        + [sems((n, members))] * 4
        + [sems((n, planes))] * 2
        + [sems((n,))] * 2
        + [sems((3, most))] * 2,
        compiler_params=pltpu.CompilerParams(
            vmem_limit_bytes=63 * MIB, collective_id=1, has_side_effects=True
        ),
        cost_estimate=cost(16 * pairs * tokens * tokens * 256, 4 * pairs * tokens * tokens),
        name="tail",
    )(
        x, vecs, tables, lines, gate_grads, gate, q, k, v, wq, wk, wv, wo, probs,
        back.reshape(2, tokens, width), hidden, cot, mixed, made,
    )


def finish_kernel(x_axis, *refs):
    sums_refs = refs[:3]
    din_refs = refs[3 : 3 + x_axis]
    dout_refs = refs[3 + x_axis : 3 + 2 * x_axis]
    dwo_ref, dwq_ref, dwk_ref, dwv_ref, din_ref, dout_ref = refs[3 + 2 * x_axis :]
    width = dwo_ref.shape[1]
    half = width // 256
    for tile in range(width // 128):
        lanes = slice(tile * 128, (tile + 1) * 128)
        dwo_ref[:, lanes] = sums_refs[tile % half][tile // half].astype(F32)
        for w, ref in enumerate((dwq_ref, dwk_ref, dwv_ref)):
            ref[:, lanes] = sums_refs[w][2 + tile].astype(F32)
    for out, parts in ((din_ref, din_refs), (dout_ref, dout_refs)):
        total = parts[0][...].astype(F32)
        for part in parts[1:]:
            total = total + part[...].astype(F32)
        out[...] = total


def finish(width, sums, din, dout):
    n = sums.shape[0]
    steps = 4

    def row_spec(array):
        return pl.BlockSpec((array.shape[0] // steps, array.shape[1]), lambda i: (i, 0))

    square = jax.ShapeDtypeStruct((width, width), F32)
    out_shape = [square] * 4 + [
        jax.ShapeDtypeStruct(din[0].shape, F32),
        jax.ShapeDtypeStruct(dout[0].shape, F32),
    ]
    return pl.pallas_call(
        functools.partial(finish_kernel, len(din)),
        grid=(steps,),
        in_specs=[
            pl.BlockSpec((n, width // steps, 128), lambda i, w=w: (0, w * steps + i, 0))
            for w in range(3)
        ]
        + [row_spec(part) for part in (*din, *dout)],
        out_specs=[row_spec(out) for out in out_shape],
        out_shape=out_shape,
        compiler_params=params(),
        cost_estimate=cost(0, 24 * width * width),
        name="finish",
    )(sums, sums, sums, *din, *dout)


def output_kernel(experts, cap, made_ref, hidden_ref, gate_ref, lines_ref, out_ref):
    rows, width = hidden_ref.shape
    pick = one_hot(iota((rows, experts * cap), 1) == col_of(lines_ref[1:2, :]))
    produced = mm(pick, made_ref[...])
    out_ref[...] = (hidden_ref[...] + gate_ref[:, 0:1] * produced).astype(BF16)


def layer_output(made, hidden, gate, lines, experts, cap):
    tokens, width = hidden.shape
    rows = 256
    made = made.reshape(-1, width)
    block = pl.BlockSpec((rows, width), lambda i: (i, 0))
    return pl.pallas_call(
        functools.partial(output_kernel, experts, cap),
        grid=(tokens // rows,),
        in_specs=[
            spec_all(made.shape),
            block,
            pl.BlockSpec((rows, 128), lambda i: (i, 0)),
            pl.BlockSpec((8, rows), lambda i: (0, i)),
        ],
        out_specs=block,
        out_shape=jax.ShapeDtypeStruct((tokens, width), BF16),
        compiler_params=params(),
        cost_estimate=cost(2 * tokens * width * experts * cap, 10 * tokens * width),
        name="layer_output",
    )(made, hidden, gate, lines)


def exchange(blocks, axis):
    return lax.all_to_all(blocks, axis, split_axis=0, concat_axis=0, tiled=True)


def on_device(
    tokens,
    segment_ids,
    routes,
    norm1_gain,
    norm1_bias,
    query_weight,
    w_key,
    w_value,
    w_output,
    norm2_gain,
    norm2_bias,
    router_proj,
    expert_embed,
    expert_in,
    expert_out,
    cotangent,
):
    count, width = tokens.shape
    experts = lax.axis_size("expert")
    dp_size = lax.axis_size("dp")
    cap = 2 * count // experts
    longest = segment_ids.shape[1] // 2
    space = router_proj.shape[1]
    vecs = jnp.concatenate([norm1_gain, norm1_bias, norm2_gain, norm2_bias]).reshape(4, width)
    tables = jnp.concatenate(
        [
            jnp.pad(router_proj, ((0, 0), (0, 128 - space))),
            jnp.pad(expert_embed, ((0, 128 - experts), (0, 128 - space))),
        ]
    )
    q, k, v, mixed, probs, hidden, gate, slots, gates, lines, up = forward(
        routes.reshape(1, count), segment_ids.reshape(1, count), cotangent, tokens, vecs, tables,
        query_weight, w_key, w_value, w_output, longest, experts, cap,
    )
    back, gate_grads, made, din, dout = expert(
        slots, gates, up, expert_in[0], expert_out[0], dp_size
    )
    if can_reduce(width, space, dp_size, experts):
        grad_input, sums, output, small1, small2 = tail(
            tokens, vecs, tables, lines, gate_grads, gate, q, k, v, query_weight, w_key, w_value,
            w_output, probs, back, hidden, cotangent, mixed, made, space, longest, dp_size,
            experts,
        )
    else:
        made = exchange(made, "expert")
        grad_hidden, grad_mixed, delta, dwo, small2 = middle_back(
            back, gate_grads, lines, hidden, cotangent, mixed, w_output, vecs[2:3], vecs[3:4],
            tables[:width], tables[width:], space, experts, cap,
        )
        dq, dk, dv = attention_back(q, k, v, grad_mixed, probs, delta, longest)
        grad_input, dwq, dwk, dwv, small1 = qkv_back(
            tokens, vecs[0:1], vecs[1:2], grad_hidden, dq, dk, dv, query_weight, w_key, w_value
        )
        half = width // 256
        chunks = [dwo[:half], dwo[half:]]
        for at in range(width // 128):
            chunks.append(jnp.stack([dwq[at], dwk[at], dwv[at]]))
        sums, small1, small2 = lax.psum(
            (jnp.stack(chunks).astype(F32), small1, small2), ("dp", "expert")
        )
        sums = sums.astype(BF16).reshape(len(chunks), -1, 128)
        output = layer_output(made, hidden, gate, lines, experts, cap)
    dwo, dwq, dwk, dwv, grad_in, grad_out = finish(width, sums, din, dout)
    return (
        output,
        grad_input,
        small1[0],
        small1[1],
        dwq,
        dwk,
        dwv,
        dwo,
        small2[0],
        small2[1],
        small2[8 : 8 + space].T,
        small2[8 + space : 8 + space + experts, :space],
        grad_in[None],
        grad_out[None],
    )


def solution(mesh):
    split = P(("dp", "expert"), None)
    in_specs = (
        (split,) * 3 + (P(),) * 10 + (P("expert", None, None), P("expert", None, None), split)
    )
    out_specs = (
        (split, split) + (P(),) * 10 + (P("expert", None, "dp"), P("expert", "dp", None))
    )
    return jax.shard_map(
        on_device, mesh=mesh, in_specs=in_specs, out_specs=out_specs, check_vma=False
    )
```
